32 devices in a mesh: seq: 4 (over x, core), rows: 8 (over z, y).
Axes of the slice: x: 2, y: 2, z: 4, core: 2. Of those that a mesh axis runs over, the one named last changes fastest.
Arguments:
- patches: bfloat16 [16, 1024, 768], P('rows', 'seq'), may hold values from -6 to 6
- segments: int32 [16, 1024], P('rows', 'seq'), may hold values from 0 to 8, as said below
- masked: int32 [16, 1024], P('rows', 'seq'), may hold values 0 or 1
- mask_embedding: bfloat16 [768], P(('seq', 'rows')), may hold values from -5 to 5
- norm1_gain: bfloat16 [768], P(('seq', 'rows')), may hold values from 0.5 to 1.5
- norm1_bias: bfloat16 [768], P(('seq', 'rows')), may hold values from -4 to 4
- qkv_weight: bfloat16 [768, 2304], P(('seq', 'rows')), may hold values from -0.21875 to 0.21875
- query_bias: bfloat16 [768], P(('seq', 'rows')), may hold values from -4 to 4
- value_bias: bfloat16 [768], P(('seq', 'rows')), may hold values from -0.75 to 0.75
- out_weight: bfloat16 [768, 768], P(('seq', 'rows')), may hold values from -3.5 to 3.5
- out_bias: bfloat16 [768], P(('seq', 'rows')), may hold values from -4 to 4
- norm2_gain: bfloat16 [768], P(('seq', 'rows')), may hold values from 0.5 to 1.5
- norm2_bias: bfloat16 [768], P(('seq', 'rows')), may hold values from -4 to 4
- up_weight: bfloat16 [768, 3072], P(('seq', 'rows')), may hold values from -0.21875 to 0.21875
- up_bias: bfloat16 [3072], P(('seq', 'rows')), may hold values from -4 to 4
- down_weight: bfloat16 [3072, 768], P(('seq', 'rows')), may hold values from -0.109375 to 0.109375
- down_bias: bfloat16 [768], P(('seq', 'rows')), may hold values from -4 to 4
- cotangent: bfloat16 [16, 1024, 768], P('rows', 'seq'), may hold values from -6 to 6
Outputs:
- output: bfloat16 [16, 1024, 768], P('rows', 'seq')
- input_grad: float32 [16, 1024, 768], P('rows', 'seq')
- mask_embedding_grad: float32 [768], P(('seq', 'rows'))
- norm1_gain_grad: float32 [768], P(('seq', 'rows'))
- norm1_bias_grad: float32 [768], P(('seq', 'rows'))
- qkv_weight_grad: float32 [768, 2304], P(('seq', 'rows'))
- query_bias_grad: float32 [768], P(('seq', 'rows'))
- value_bias_grad: float32 [768], P(('seq', 'rows'))
- out_weight_grad: float32 [768, 768], P(('seq', 'rows'))
- out_bias_grad: float32 [768], P(('seq', 'rows'))
- norm2_gain_grad: float32 [768], P(('seq', 'rows'))
- norm2_bias_grad: float32 [768], P(('seq', 'rows'))
- up_weight_grad: float32 [768, 3072], P(('seq', 'rows'))
- up_bias_grad: float32 [3072], P(('seq', 'rows'))
- down_weight_grad: float32 [3072, 768], P(('seq', 'rows'))
- down_bias_grad: float32 [768], P(('seq', 'rows'))
The draws below stay inside these ranges and needn't reach their ends.
Inputs may be any that keep to these rules, and one draw needn't show every extreme that they name: `segments`: along each row the ids never fall except to 0; 0 (padding) stands only in the last fewer than 64 positions of a row; in the first of every 2 rows one clip covers patches of every index of seq.
All inputs are finite; a program needn't handle non-finite values. No bound on the sum of `masked` on one device may be relied on, other than what follows from the above.
Results may differ from the reference program's by a relative error of at most 0.017.
Values may be sent and summed in bfloat16 or wider, within the bound.
No kernel may reach another device: no remote copies, remote signals or barrier semaphores. Data moves between devices by JAX's collectives and lax.ppermute only.
A program may use at most 192 MiB of HBM per device.

```python
import math
import jax
import jax.numpy as jnp
from jax import lax

D = 768
HEADS = 12
HEAD_SIZE = 64
FF = 3072
ROWS_DEV = 2
PATCH_DEV = 256
ROWS = 16
ROW_LEN = 1024


def draw_segments(key, part):
    key = jax.random.fold_in(key, 11)
    key_short, key_first, key_second, key_mode, key_pad = jax.random.split(key, 5)
    half = PATCH_DEV // 2
    count = 2 * ROW_LEN // PATCH_DEV - 1
    base = (jnp.arange(count, dtype=jnp.int32) + 1) * half
    short_cuts = base[None, :] + jax.random.randint(key_short, (ROWS, count), 0, half)
    first = jax.random.randint(key_first, (ROWS, 1), 1, half)
    second = jax.random.randint(key_second, (ROWS, 1), ROW_LEN - half, ROW_LEN - 1)
    long_cuts = jnp.concatenate([first, second, jnp.full((ROWS, count - 2), ROW_LEN, jnp.int32)], axis=1)
    mode = jax.random.randint(key_mode, (ROWS, 1), 0, 2)
    forced = (jnp.arange(ROWS) % ROWS_DEV == 0)[:, None]
    use_long = forced | (mode == 0)
    cuts = jnp.where(use_long, long_cuts, short_cuts)
    position = jnp.arange(ROW_LEN, dtype=jnp.int32)
    ids = 1 + jnp.sum((cuts[:, None, :] <= position[None, :, None]).astype(jnp.int32), axis=-1)
    ids = jnp.where(use_long, ids + (count - 2), ids)
    padding = jax.random.randint(key_pad, (ROWS, 1), 0, max(PATCH_DEV // 4, 1))
    row_index = jnp.arange(ROWS, dtype=jnp.int32)[:, None]
    padding = jnp.where(row_index == 0, 0, padding)
    padding = jnp.where(row_index == ROWS - 1, jnp.maximum(padding, 1), padding)
    ids = jnp.where(position[None, :] >= ROW_LEN - padding, 0, ids)
    return ids.astype(jnp.int32)


def with_ends(values, stream_key, low, largest):
    extent = values.shape
    index_at = [jax.random.randint(jax.random.fold_in(stream_key, axis), (), 0, extent[axis]) for axis in range(len(extent))]
    values = values.at[tuple(index_at)].set(low)
    longest = extent.index(max(extent))
    index_at[longest] = (index_at[longest] + 1) % extent[longest]
    return values.at[tuple(index_at)].set(largest)


def level_of(own_key, shape, cuts, low, top_value):
    loudness, own = 1.0, jax.random.fold_in(own_key, 6)
    for dim, shards_of in cuts:
        steps = jnp.exp(jax.random.uniform(jax.random.fold_in(own, dim), (shards_of,), jnp.float32, low / len(cuts), top_value / len(cuts)))
        loudness = loudness * jnp.repeat(steps, shape[dim] // shards_of).reshape([-1 if axis == dim else 1 for axis in range(len(shape))])
    return loudness


def scatter_about(rng, shape, width, limit, shards=(), kind=jnp.bfloat16):
    level = level_of(rng, shape, shards, -0.22, 0.18) if shards else 1.0
    values = jax.random.normal(rng, shape, jnp.float32) * width * level
    return jnp.minimum(jnp.maximum(values, -limit), limit).astype(kind)


def setup_inputs(seed: int = 0) -> dict:
    seeds = jax.random.split(jax.random.key(seed), 19)
    return {
        "patches": scatter_about(seeds[0], (ROWS, ROW_LEN, D), 1.0, 6.0, ((0, 8), (1, 4))),
        "segments": draw_segments(jax.random.fold_in(seeds[18], 71), 0),
        "masked": with_ends((jax.random.randint(seeds[2], (ROWS, ROW_LEN), 0, 10) < 3).astype(jnp.int32), jax.random.fold_in(seeds[2], 1), 0, 1),
        "mask_embedding": scatter_about(seeds[3], (D,), 1.0, 5.0, ((0, 32),)),
        "norm1_gain": jnp.clip(1.0 + 0.1 * jax.random.normal(seeds[4], (D,), jnp.float32), 0.5, 1.5).astype(jnp.bfloat16),
        "norm1_bias": scatter_about(seeds[5], (D,), 0.3, 4.0, ((0, 32),)),
        "qkv_weight": scatter_about(seeds[6], (D, 3 * D), D ** -0.5, 0.21875, ((0, 32),)),
        "query_bias": scatter_about(seeds[7], (D,), 0.5, 4.0, ((0, 32),)),
        "value_bias": scatter_about(seeds[8], (D,), 0.05, 0.75, ((0, 32),)),
        "out_weight": scatter_about(seeds[9], (D, D), (D // 256) ** -0.5, 3.5, ((0, 32),)),
        "out_bias": scatter_about(seeds[10], (D,), 0.3, 4.0, ((0, 32),)),
        "norm2_gain": jnp.clip(1.0 + 0.1 * jax.random.normal(seeds[11], (D,), jnp.float32), 0.5, 1.5).astype(jnp.bfloat16),
        "norm2_bias": scatter_about(seeds[12], (D,), 0.3, 4.0, ((0, 32),)),
        "up_weight": scatter_about(seeds[13], (D, FF), D ** -0.5, 0.21875, ((0, 32),)),
        "up_bias": scatter_about(seeds[14], (FF,), 0.5, 4.0, ((0, 32),)),
        "down_weight": scatter_about(seeds[15], (FF, D), FF ** -0.5, 0.109375, ((0, 32),)),
        "down_bias": scatter_about(seeds[16], (D,), 0.3, 4.0, ((0, 32),)),
        "cotangent": scatter_about(seeds[17], (ROWS, ROW_LEN, D), 1.0, 6.0, ((0, 8), (1, 4))),
    }


@jax.custom_vjp
def low(v):
    return lax.optimization_barrier(v.astype(jnp.bfloat16)).astype(jnp.float32)

@jax.custom_vjp
def low_back(v):
    return v

def low_keep(v):
    return (low(v), None)

def low_pass(kept, grad):
    return (grad,)

def back_keep(v):
    return (v, None)

def back_low(kept, grad):
    return (low(grad),)
low.defvjp(low_keep, low_pass)
low_back.defvjp(back_keep, back_low)
EPSILON = 1e-06
FLOOR_SCORE = -1e+30
HALF_ROOT = 0.7071067811865476
HIGH = lax.Precision.HIGHEST

def layer_norm(inputs, gain, shift):
    mean = lax.optimization_barrier(jnp.mean(inputs, axis=-1, keepdims=True))
    centered = inputs - mean
    spread = lax.optimization_barrier(jnp.mean(centered * centered, axis=-1, keepdims=True))
    return centered * lax.rsqrt(spread + EPSILON) * gain + shift

def gelu_exact(inputs):
    return 0.5 * inputs * (1.0 + lax.erf(inputs * HALF_ROOT))

def attend(block):
    queries, key_rows, value_rows, segment_row = block
    scores = low_back(jnp.einsum('qhe,khe->hqk', queries, key_rows, precision=HIGH))
    allowed = (segment_row[:, None] == segment_row[None, :]) & (segment_row[None, :] > 0)
    scores = jnp.where(allowed[None], scores, FLOOR_SCORE)
    highest = lax.optimization_barrier(jnp.max(scores, axis=-1, keepdims=True))
    expo = jnp.exp(scores - highest)
    probs = low(expo / lax.optimization_barrier(jnp.sum(expo, axis=-1, keepdims=True)))
    mixed = jnp.einsum('hqk,khe->qhe', probs, value_rows, precision=HIGH)
    return mixed * (segment_row > 0).astype(jnp.float32)[:, None, None]

def forward(weights, patch_rows, segment_rows, masked_rows):
    embed, gain_one, shift_one, w_project, bias_query, bias_value, w_out, bias_out, gain_two, shift_two, w_up, bias_up, w_down, bias_down = weights
    group_size = patch_rows.shape[0]
    embedded = jnp.where(masked_rows[..., None] == 1, embed, patch_rows)
    normed_one = low(layer_norm(embedded, gain_one, shift_one))
    projected = jnp.einsum('rld,df->rlf', normed_one, w_project, precision=HIGH)
    scale = HEAD_SIZE ** (-0.5)
    queries = low_back(low((projected[..., :D] + bias_query) * scale))
    key_rows = low_back(low(projected[..., D:2 * D]))
    value_rows = low_back(low(projected[..., 2 * D:] + bias_value))
    shape = (group_size, ROW_LEN, HEADS, HEAD_SIZE)
    mixed = lax.map(jax.checkpoint(attend), (queries.reshape(shape), key_rows.reshape(shape), value_rows.reshape(shape), segment_rows))
    mixed = low_back(low(mixed.reshape(group_size, ROW_LEN, D)))
    branch_one = low_back(jnp.einsum('rld,df->rlf', mixed, w_out, precision=HIGH) + bias_out)
    middle = embedded + branch_one
    normed_two = low(layer_norm(middle, gain_two, shift_two))
    hidden = low_back(jnp.einsum('rld,df->rlf', normed_two, w_up, precision=HIGH) + bias_up)
    activated = low(gelu_exact(hidden))
    branch_two = low_back(jnp.einsum('rlf,fd->rld', activated, w_down, precision=HIGH) + bias_down)
    return middle + branch_two

def reference(patches, segments, masked, mask_embedding, norm1_gain, norm1_bias, qkv_weight, query_bias, value_bias, out_weight, out_bias, norm2_gain, norm2_bias, up_weight, up_bias, down_weight, down_bias, cotangent):
    weights = tuple((w.astype(jnp.float32) for w in (mask_embedding, norm1_gain, norm1_bias, qkv_weight, query_bias, value_bias, out_weight, out_bias, norm2_gain, norm2_bias, up_weight, up_bias, down_weight, down_bias)))
    group_size = math.gcd(ROWS, max(1, 4096 // ROW_LEN))
    groups = ROWS // group_size

    def one_group(totals, block):
        patch_rows, segment_rows, masked_rows, cot_rows = block

        def run(wts, pts):
            return forward(wts, pts, segment_rows, masked_rows)
        result, pull = jax.vjp(run, weights, patch_rows.astype(jnp.float32))
        grad_weights, grad_patches = pull(cot_rows.astype(jnp.float32))
        totals = tuple((a + b for a, b in zip(totals, grad_weights)))
        return (totals, (result.astype(jnp.bfloat16), grad_patches))
    initial = tuple((jnp.zeros(w.shape, jnp.float32) for w in weights))
    inputs = (patches.reshape(groups, group_size, ROW_LEN, D), segments.reshape(groups, group_size, ROW_LEN), masked.reshape(groups, group_size, ROW_LEN), cotangent.reshape(groups, group_size, ROW_LEN, D))
    totals, (outputs, grads) = lax.scan(one_group, initial, inputs)
    return (outputs.reshape(ROWS, ROW_LEN, D), grads.reshape(ROWS, ROW_LEN, D), totals[0], totals[1], totals[2], totals[3], totals[4], totals[5], totals[6], totals[7], totals[8], totals[9], totals[10], totals[11], totals[12], totals[13])
```

```python
import jax
import jax.numpy as jnp
from jax import lax
from jax.experimental import pallas as pl
from jax.experimental.pallas import tpu as pltpu
from jax.sharding import PartitionSpec as P

HEAD_SIZE = 64
LANES = 128
EPSILON = 1e-06
FLOOR_SCORE = -1e30
HALF_ROOT = 0.7071067811865476
EVERY = ("seq", "rows")
BF16 = jnp.bfloat16
F32 = jnp.float32


def dot(left, right, left_dim, right_dim):
    return lax.dot_general(
        left, right, (((left_dim,), (right_dim,)), ((), ())), preferred_element_type=F32
    )


def split_heads(pair):
    lane = lax.broadcasted_iota(jnp.int32, pair.shape, 1)
    zero = jnp.zeros_like(pair)
    return jnp.concatenate(
        [jnp.where(lane < HEAD_SIZE, pair, zero), jnp.where(lane < HEAD_SIZE, zero, pair)], axis=0
    )


def join_heads(both, count):
    row = lax.broadcasted_iota(jnp.int32, (both.shape[0], count), 0)
    return jnp.where(row < HEAD_SIZE, both[:, :count], both[:, count:]).T


def set_bias(key_segment, query_segment, bias):
    keys, asked = key_segment[0], query_segment[0]
    bias[...] = jnp.where((keys == asked) & (keys > 0.0), 0.0, FLOOR_SCORE)


def attend_kernel(q_ref, k_ref, v_ref, ks_ref, qs_ref, mix_ref, full_ref, lse_ref, bias, held):
    count, blocks, size = q_ref.shape[1], k_ref.shape[0], k_ref.shape[2]

    @pl.when(pl.program_id(1) == 0)
    def _():
        set_bias(ks_ref, qs_ref, bias)

    asked = split_heads(q_ref[0])
    top = None
    for j in range(blocks):
        rows = pl.ds(j * size, size)
        part = bias[rows, :]
        scores = dot(k_ref[j, 0], asked, 1, 1) + jnp.concatenate([part, part], axis=1)
        held[rows, :] = scores
        high = jnp.max(scores, axis=0, keepdims=True)
        top = high if top is None else jnp.maximum(top, high)
    total, mixed = 0.0, 0.0
    for j in range(blocks):
        weights = jnp.exp(held[pl.ds(j * size, size), :] - top)
        total = total + jnp.sum(weights, axis=0, keepdims=True)
        mixed = mixed + dot(v_ref[j, 0].T, weights.astype(BF16), 1, 0)
    live = qs_ref[0] > 0.0
    live = jnp.concatenate([live, live], axis=1)
    result = join_heads(mixed * jnp.where(live, 1.0 / total, 0.0), count)
    mix_ref[0] = result.astype(BF16)
    full_ref[0] = result
    lse_ref[0, 0] = jnp.where(live, top + jnp.log(total), 0.0)


def attend_back_kernel(
    q_ref, k_ref, v_ref, dm_ref, full_ref, lse_ref, ks_ref, qs_ref,
    dq_ref, dk_ref, dv_ref, qsum_ref, vsum_ref, bias,
):
    count, blocks, size = q_ref.shape[1], k_ref.shape[0], k_ref.shape[2]

    @pl.when(pl.program_id(1) == 0)
    def _():
        set_bias(ks_ref, qs_ref, bias)

    d_mixed = dm_ref[0]
    asked, pulled = split_heads(q_ref[0]), split_heads(d_mixed)
    product = (d_mixed.astype(F32) * full_ref[0]).T
    delta = jnp.concatenate(
        [
            jnp.sum(product[:HEAD_SIZE], axis=0, keepdims=True),
            jnp.sum(product[HEAD_SIZE:], axis=0, keepdims=True),
        ],
        axis=1,
    )
    lse = lse_ref[0, 0]
    d_query, v_sum = 0.0, 0.0
    for j in range(blocks):
        keys = k_ref[j, 0]
        part = bias[pl.ds(j * size, size), :]
        scores = dot(keys, asked, 1, 1) + jnp.concatenate([part, part], axis=1)
        probs = jnp.exp(scores - lse)
        d_probs = dot(v_ref[j, 0], pulled, 1, 1)
        d_scores = (probs * (d_probs - delta)).astype(BF16)
        d_value = dot(probs.astype(BF16), pulled, 1, 0)
        dv_ref[j, 0] = d_value.astype(BF16)
        dk_ref[j, 0] = dot(d_scores, asked, 1, 0).astype(BF16)
        v_sum = v_sum + jnp.sum(d_value, axis=0, keepdims=True)
        d_query = d_query + dot(keys.T, d_scores, 1, 0)
    d_query = join_heads(d_query, count) * HEAD_SIZE**-0.5
    dq_ref[0] = d_query.astype(BF16)
    qsum_ref[0, 0] = jnp.sum(d_query, axis=0, keepdims=True)
    vsum_ref[0, 0] = v_sum


def attention_specs(queries, key_values):
    rows, count, width = queries.shape
    blocks, _, size, _ = key_values.shape
    pairs = width // LANES
    tile = pl.BlockSpec((1, count, LANES), lambda r, p: (r, 0, p))
    keys = pl.BlockSpec((blocks, 1, size, LANES), lambda r, p: (0, r, 0, p))
    values = pl.BlockSpec((blocks, 1, size, LANES), lambda r, p: (0, r, 0, pairs + p))
    norm = pl.BlockSpec((1, 1, 1, 2 * count), lambda r, p: (r, p, 0, 0))
    key_segment = pl.BlockSpec((1, blocks * size, 1), lambda r, p: (r, 0, 0))
    query_segment = pl.BlockSpec((1, 1, count), lambda r, p: (r, 0, 0))
    column = pl.BlockSpec((1, 1, 1, LANES), lambda r, p: (r, p, 0, 0))
    return (rows, count, width, blocks, size, pairs), (
        tile, keys, values, norm, key_segment, query_segment, column,
    )


def attend(queries, key_values, key_segment, query_segment):
    sizes, specs = attention_specs(queries, key_values)
    rows, count, width, blocks, size, pairs = sizes
    tile, keys, values, norm, ks, qs, _ = specs
    area = rows * count * blocks * size
    return pl.pallas_call(
        attend_kernel,
        grid=(rows, pairs),
        in_specs=[tile, keys, values, ks, qs],
        out_specs=[tile, tile, norm],
        out_shape=[
            jax.ShapeDtypeStruct(queries.shape, BF16),
            jax.ShapeDtypeStruct(queries.shape, F32),
            jax.ShapeDtypeStruct((rows, pairs, 1, 2 * count), F32),
        ],
        scratch_shapes=[
            pltpu.VMEM((blocks * size, count), F32),
            pltpu.VMEM((blocks * size, 2 * count), F32),
        ],
        compiler_params=pltpu.CompilerParams(vmem_limit_bytes=24 * 2**20),
        cost_estimate=pl.CostEstimate(
            flops=16 * area * width,
            bytes_accessed=8 * rows * blocks * size * width,
            transcendentals=area * 12,
        ),
        name="attend",
    )(queries, key_values, key_values, key_segment, query_segment)


def attend_back(queries, key_values, d_mixed, mixed_full, lse, key_segment, query_segment):
    sizes, specs = attention_specs(queries, key_values)
    rows, count, width, blocks, size, pairs = sizes
    tile, keys, values, norm, ks, qs, column = specs
    area = rows * count * blocks * size
    grads = jax.ShapeDtypeStruct((blocks, rows, size, width), BF16)
    sums = jax.ShapeDtypeStruct((rows, pairs, 1, LANES), F32)
    return pl.pallas_call(
        attend_back_kernel,
        grid=(rows, pairs),
        in_specs=[tile, keys, values, tile, tile, norm, ks, qs],
        out_specs=[tile, keys, keys, column, column],
        out_shape=[jax.ShapeDtypeStruct(queries.shape, BF16), grads, grads, sums, sums],
        scratch_shapes=[pltpu.VMEM((blocks * size, count), F32)],
        compiler_params=pltpu.CompilerParams(vmem_limit_bytes=24 * 2**20),
        cost_estimate=pl.CostEstimate(
            flops=32 * area * width,
            bytes_accessed=16 * rows * blocks * size * width,
            transcendentals=area * 12,
        ),
        name="attend_back",
    )(queries, key_values, key_values, d_mixed, mixed_full, lse, key_segment, query_segment)


class Links:
    def __init__(self, seq, rows):
        self.sizes = {"seq": seq, "rows": rows}
        self.names = {}
        order = []
        for axis in EVERY:
            mask = self.sizes[axis] // 2
            while mask:
                order.append((axis, mask))
                mask //= 2
        self.order = order
        place = {axis: lax.axis_index(axis) for axis in EVERY}
        self.value = {(a, m): (place[a] // m) % 2 for a, m in order}
        self.near = [b for b in order if b == ("seq", 1)]
        self.first = [b for b in order if b[0] == "seq" and b[1] > 1]
        self.second = [b for b in order if b == ("rows", 1)]
        self.others = [b for b in order if b[0] == "rows" and b[1] > 1]

    def swap(self, array, bit):
        axis, mask = bit
        return lax.ppermute(array, axis, [(i, i ^ mask) for i in range(self.sizes[axis])])

    def gather(self, shard, bits):
        held, have = shard, []
        for bit in bits:
            other = self.swap(held, bit)
            upper = self.value[bit] == 1
            low = jnp.where(upper, other, held)
            high = jnp.where(upper, held, other)
            have = sorted([*have, bit], key=self.order.index)
            held = jnp.stack([low, high], axis=have.index(bit))
        return held.reshape(-1, shard.shape[-1])

    def scatter(self, terms, bits):
        have = list(self.order)
        held = terms.reshape((2,) * len(have) + (terms.shape[0] >> len(have), terms.shape[-1]))
        for bit in bits:
            at = have.index(bit)
            have.pop(at)
            mine = self.value[bit]
            sent = lax.dynamic_index_in_dim(held, 1 - mine, at, keepdims=False)
            kept = lax.dynamic_index_in_dim(held, mine, at, keepdims=False)
            other = self.swap(sent.astype(BF16), bit)
            held = kept.astype(F32) + other.astype(F32)
            if have:
                held = held.astype(BF16)
        return held


def layer_norm(inputs, gain, shift):
    mean = jnp.mean(inputs, axis=-1, keepdims=True)
    centered = inputs - mean
    spread = jnp.mean(centered * centered, axis=-1, keepdims=True)
    return centered * lax.rsqrt(spread + EPSILON) * gain + shift


def gelu_exact(inputs):
    return 0.5 * inputs * (1.0 + lax.erf(inputs * HALF_ROOT))


def body(
    patches, segments, masked, mask_embedding, norm1_gain, norm1_bias, qkv_weight, query_bias,
    value_bias, out_weight, out_bias, norm2_gain, norm2_bias, up_weight, up_bias, down_weight,
    down_bias, cotangent, *, seq, rows,
):
    links = Links(seq, rows)
    row_count, patch_count, width = patches.shape
    tokens = row_count * patch_count
    n = qkv_weight.shape[0]
    devices = seq * rows
    hidden_width = up_weight.shape[1]
    groups = hidden_width // width
    scale = HEAD_SIZE**-0.5
    near, first, second, others = links.near, links.first, links.second, links.others

    seq_bits = [*first, *near]
    small = [
        mask_embedding, norm1_gain, norm1_bias, query_bias, value_bias, out_bias, norm2_gain,
        norm2_bias, down_bias,
    ]
    columns = jnp.concatenate([jnp.stack(small), up_bias.reshape(groups, n)], axis=0).T
    columns = jnp.pad(columns, ((0, 0), (0, LANES - columns.shape[1])))
    cut = 3 * width // 2
    left = links.gather(qkv_weight[:, :cut], [*others, *second, *first, *near])
    right = links.gather(
        jnp.concatenate([qkv_weight[:, cut:], columns], axis=1),
        [*others, *first, *second, *near],
    )
    flags = (segments + 16 * masked).astype(BF16)
    rows_all = patches.reshape(1, tokens, width)
    flags_all = flags.reshape(1, row_count, patch_count)
    for bit in seq_bits:
        rows_all = jnp.concatenate([rows_all, links.swap(rows_all, bit)], axis=0)
        flags_all = jnp.concatenate([flags_all, links.swap(flags_all, bit)], axis=0)
    packed = jnp.concatenate(
        [
            out_weight,
            up_weight.reshape(n, groups, width).transpose(1, 0, 2).reshape(groups * n, width),
            down_weight,
        ],
        axis=0,
    )
    rest = lax.all_gather(packed, EVERY, axis=0, tiled=False)
    rest = rest.reshape(devices, -1, width)
    w_out = rest[:, :n].reshape(width, width)
    w_up = (
        rest[:, n : n + groups * n]
        .reshape(devices, groups, n, width)
        .transpose(0, 2, 1, 3)
        .reshape(width, hidden_width)
    )
    w_down = rest[:, n + groups * n :].reshape(hidden_width, width)

    vectors = right[:, width + width // 2 :].astype(F32).T
    embed, gain_one, shift_one, bias_query, bias_value, bias_out, gain_two, shift_two, bias_down = (
        vectors[i] for i in range(9)
    )
    bias_up = vectors[9 : 9 + groups].reshape(groups, devices, n).transpose(1, 0, 2).reshape(-1)
    w_project = jnp.concatenate([left, right[:, : width + width // 2]], axis=1)

    blocks = seq
    flags_all = flags_all.reshape(blocks, row_count, patch_count).astype(jnp.int32)
    masked_all = (flags_all >= 16).reshape(-1, 1)
    segments_all = (flags_all % 16).astype(F32)
    embedded_all = jnp.where(
        masked_all, embed[None, :], rows_all.reshape(-1, width).astype(F32)
    )
    mean_one = jnp.mean(embedded_all, axis=-1, keepdims=True)
    centered_one = embedded_all - mean_one
    rate_one = lax.rsqrt(jnp.mean(centered_one * centered_one, axis=-1, keepdims=True) + EPSILON)
    hat_one = centered_one * rate_one
    normed_all = (hat_one * gain_one + shift_one).astype(BF16)
    embedded = embedded_all[:tokens]
    normed_one = normed_all[:tokens]
    queries = ((dot(normed_one, w_project[:, :width], 1, 0) + bias_query) * scale).astype(BF16)
    shift_values = jnp.concatenate([jnp.zeros_like(bias_value), bias_value])
    key_values = (dot(normed_all, w_project[:, width:], 1, 0) + shift_values).astype(BF16)
    queries = queries.reshape(row_count, patch_count, width)
    key_values = key_values.reshape(blocks, row_count, patch_count, 2 * width)
    key_segment = segments_all.transpose(1, 0, 2).reshape(row_count, -1, 1)
    query_segment = segments_all[0].reshape(row_count, 1, patch_count)
    mixed3, mixed_full, lse = attend(queries, key_values, key_segment, query_segment)
    mixed = mixed3.reshape(tokens, width)

    middle = embedded + dot(mixed, w_out, 1, 0) + bias_out
    normed_mid, pull_two = jax.vjp(layer_norm, middle, gain_two, shift_two)
    normed_two = normed_mid.astype(BF16)
    hidden = dot(normed_two, w_up, 1, 0) + bias_up
    activated_full, pull_act = jax.vjp(gelu_exact, hidden)
    activated = activated_full.astype(BF16)
    result = middle + dot(activated, w_down, 1, 0) + bias_down
    output = result.astype(BF16).reshape(row_count, patch_count, width)

    d_branch = cotangent.reshape(tokens, width)
    d_result = d_branch.astype(F32)
    grad_down = dot(activated, d_branch, 0, 0).astype(BF16)
    grad_down_bias = jnp.sum(d_result, axis=0)
    (d_hidden_full,) = pull_act(dot(d_branch, w_down, 1, 1))
    d_hidden = d_hidden_full.astype(BF16)
    grad_up = dot(normed_two, d_hidden, 0, 0).astype(BF16)
    grad_up_bias = jnp.sum(d_hidden.astype(F32), axis=0)
    down_sum = links.scatter(grad_down, [*near, *first, *second, *others[::-1]])
    up_sum = links.scatter(grad_up, [*near, *second, *first, *others[::-1]])
    d_norm_mid, grad_gain_two, grad_shift_two = pull_two(dot(d_hidden, w_up, 1, 1))
    d_middle = d_result + d_norm_mid
    d_attn = d_middle.astype(BF16)
    grad_out = dot(mixed, d_attn, 0, 0).astype(BF16)
    grad_out_bias = jnp.sum(d_attn.astype(F32), axis=0)
    d_mixed = dot(d_attn, w_out, 1, 1).astype(BF16).reshape(row_count, patch_count, width)

    d_query, d_key, d_value, query_sums, value_sums = attend_back(
        queries, key_values, d_mixed, mixed_full, lse, key_segment, query_segment
    )
    d_query = d_query.reshape(tokens, width)
    d_key = d_key.reshape(-1, width)
    d_value = d_value.reshape(-1, width)
    grad_key = dot(normed_all, d_key, 0, 0).astype(BF16)
    grad_value = dot(normed_all, d_value, 0, 0).astype(BF16)
    grad_query = dot(normed_one, d_query, 0, 0).astype(BF16)
    kv_sum = links.scatter(
        jnp.concatenate([grad_key, grad_value], axis=1), [*near, *second, *first, *others[::-1]]
    )
    grad_query_bias = jnp.sum(query_sums, axis=0).reshape(-1)
    grad_value_bias = jnp.sum(value_sums, axis=0).reshape(-1)

    d_norm = dot(d_key, w_project[:, width : 2 * width], 1, 1) + dot(
        d_value, w_project[:, 2 * width :], 1, 1
    )
    d_own = dot(d_query, w_project[:, :width], 1, 1)
    d_norm = d_norm.at[:tokens].add(d_own)
    grad_gain_one = jnp.sum(d_norm * hat_one, axis=0)
    grad_shift_one = jnp.sum(d_norm, axis=0)
    pulled = d_norm * gain_one
    d_embedded = rate_one * (
        pulled
        - jnp.mean(pulled, axis=-1, keepdims=True)
        - hat_one * jnp.mean(pulled * hat_one, axis=-1, keepdims=True)
    )
    grad_embed = jnp.sum(jnp.where(masked_all, d_embedded, 0.0), axis=0) + jnp.sum(
        jnp.where(masked_all[:tokens], d_middle, 0.0), axis=0
    )
    held = d_embedded.astype(BF16).reshape(blocks, tokens, width)
    for bit in seq_bits[::-1]:
        half = held.shape[0] // 2
        other = links.swap(held[half:], bit)
        held = held[:half].astype(F32) + other.astype(F32)
        if half > 1:
            held = held.astype(BF16)
    input_grad = jnp.where(masked_all[:tokens], 0.0, d_middle + held.reshape(tokens, width))
    input_grad = input_grad.reshape(row_count, patch_count, width)

    small_grads = jnp.stack(
        [
            grad_embed, grad_gain_one, grad_shift_one, grad_query_bias, grad_value_bias,
            grad_out_bias, grad_gain_two, grad_shift_two, grad_down_bias,
        ]
    )
    grad_up_bias = grad_up_bias.reshape(devices, groups, n).transpose(1, 0, 2).reshape(groups, -1)
    small_grads = jnp.concatenate([small_grads, grad_up_bias], axis=0)
    filler = jnp.zeros((LANES - small_grads.shape[0], width), F32)
    small_grads = jnp.concatenate([small_grads, filler], axis=0).T.astype(BF16)
    last_sum = links.scatter(
        jnp.concatenate([grad_query, grad_out, small_grads], axis=1),
        [*near, *first, *second, *others[::-1]],
    )
    project_sum = jnp.concatenate([last_sum[:, :width], kv_sum], axis=1)
    out_sum = last_sum[:, width : 2 * width]
    tail = last_sum[:, 2 * width :].T
    return (
        output, input_grad, tail[0], tail[1], tail[2], project_sum, tail[3], tail[4], out_sum,
        tail[5], tail[6], tail[7], up_sum, tail[9 : 9 + groups].reshape(-1), down_sum, tail[8],
    )


def solution(mesh):
    one, two = P(EVERY), P(EVERY, None)
    rows, flags = P("rows", "seq", None), P("rows", "seq")
    seq, row_groups = mesh.shape["seq"], mesh.shape["rows"]

    def run(*arguments):
        return body(*arguments, seq=seq, rows=row_groups)

    return jax.shard_map(
        run,
        mesh=mesh,
        in_specs=(
            rows, flags, flags, one, one, one, two, one, one, two, one, one, one, two, one, two,
            one, rows,
        ),
        out_specs=(
            rows, rows, one, one, one, two, one, one, two, one, one, one, two, one, two, one,
        ),
        check_vma=False,
    )
```

```python
import jax
import jax.numpy as jnp
from jax import lax
from jax.experimental import pallas as pl
from jax.experimental.pallas import tpu as pltpu
from jax.sharding import PartitionSpec as P

HEAD_SIZE = 64
LANES = 128
CHUNK = 256
MASKED = 16
EPSILON = 1e-06
FLOOR_SCORE = -1e30
HALF_ROOT = 0.7071067811865476
MIB = 2**20
EVERY = ("seq", "rows")
BF16 = jnp.bfloat16
F32 = jnp.float32
EMBED, GAIN1, SHIFT1, QBIAS, VBIAS, OBIAS, GAIN2, SHIFT2, DBIAS, UBIAS = range(10)
KINDS = 16


def dot(left, right, left_dim, right_dim):
    return lax.dot_general(
        left, right, (((left_dim,), (right_dim,)), ((), ())), preferred_element_type=F32
    )


def column(row):
    return jnp.broadcast_to(row, (8, row.shape[1])).T[:, :1]


def segment_of(flags):
    return flags - jnp.where(flags >= MASKED, float(MASKED), 0.0)


def norm_parts(values):
    mean = jnp.mean(values, axis=-1, keepdims=True)
    centered = values - mean
    rate = lax.rsqrt(jnp.mean(centered * centered, axis=-1, keepdims=True) + EPSILON)
    return centered * rate, rate


def norm_back(pulled, hat, rate):
    first = jnp.mean(pulled, axis=-1, keepdims=True)
    second = jnp.mean(pulled * hat, axis=-1, keepdims=True)
    return rate * (pulled - first - hat * second)


def parted(value, mine, depth):
    sent, kept = [], []
    for x in range(value.shape[0] // (2 * depth)):
        low = value[2 * x * depth : (2 * x + 1) * depth]
        high = value[(2 * x + 1) * depth : (2 * x + 2) * depth]
        sent.append(jnp.where(mine == 0, high, low))
        kept.append(jnp.where(mine == 0, low, high))
    return sent, kept


def whole(*shape):
    return pl.BlockSpec(shape, lambda *_: (0,) * len(shape))


ANYWHERE = pl.BlockSpec(memory_space=pl.ANY)


def shaped(dtype, *shape):
    return jax.ShapeDtypeStruct(shape, dtype)


def parameters(mib=32):
    return pltpu.CompilerParams(vmem_limit_bytes=mib * MIB)


def cost(flops, nbytes, transcendentals=0):
    return pl.CostEstimate(flops=flops, bytes_accessed=nbytes, transcendentals=transcendentals)


def split_heads(pair):
    lane = lax.broadcasted_iota(jnp.int32, pair.shape, 1)
    zero = jnp.zeros_like(pair)
    return jnp.concatenate(
        [jnp.where(lane < HEAD_SIZE, pair, zero), jnp.where(lane < HEAD_SIZE, zero, pair)], axis=0
    )


def join_heads(both, count):
    row = lax.broadcasted_iota(jnp.int32, (both.shape[0], count), 0)
    return jnp.where(row < HEAD_SIZE, both[:, :count], both[:, count:]).T


def set_bias(flags_ref, bias):
    blocks, size = flags_ref.shape[0], flags_ref.shape[3]
    asked = segment_of(flags_ref[0, 0])
    for j in range(blocks):
        keys = column(segment_of(flags_ref[j, 0]))
        bias[pl.ds(j * size, size), :] = jnp.where((keys == asked) & (keys > 0.0), 0.0, FLOOR_SCORE)


def attend_kernel(q_ref, k_ref, v_ref, flags_ref, mix_ref, full_ref, lse_ref, bias, held):
    count, blocks, size = q_ref.shape[1], k_ref.shape[0], k_ref.shape[2]

    @pl.when(pl.program_id(1) == 0)
    def _():
        set_bias(flags_ref, bias)

    asked = split_heads(q_ref[0])
    top = None
    for j in range(blocks):
        rows = pl.ds(j * size, size)
        part = bias[rows, :]
        scores = dot(k_ref[j, 0], asked, 1, 1) + jnp.concatenate([part, part], axis=1)
        held[rows, :] = scores
        high = jnp.max(scores, axis=0, keepdims=True)
        top = high if top is None else jnp.maximum(top, high)
    total, mixed = 0.0, 0.0
    for j in range(blocks):
        weights = jnp.exp(held[pl.ds(j * size, size), :] - top)
        total = total + jnp.sum(weights, axis=0, keepdims=True)
        mixed = mixed + dot(v_ref[j, 0].T, weights.astype(BF16), 1, 0)
    live = segment_of(flags_ref[0, 0]) > 0.0
    live = jnp.concatenate([live, live], axis=1)
    result = join_heads(mixed * jnp.where(live, 1.0 / total, 0.0), count)
    mix_ref[0] = result.astype(BF16)
    full_ref[0] = result
    lse_ref[0, 0] = jnp.where(live, top + jnp.log(total), 0.0)


def attend_back_kernel(
    q_ref, k_ref, v_ref, dm_ref, full_ref, lse_ref, flags_ref,
    dq_ref, dk_ref, dv_ref, qsum_ref, vsum_ref, bias,
):
    count, blocks, size = q_ref.shape[1], k_ref.shape[0], k_ref.shape[2]

    @pl.when(pl.program_id(0) == 0)
    def _():
        set_bias(flags_ref, bias)

    d_mixed = dm_ref[0]
    asked, pulled = split_heads(q_ref[0]), split_heads(d_mixed)
    product = (d_mixed.astype(F32) * full_ref[0]).T
    delta = jnp.concatenate(
        [
            jnp.sum(product[:HEAD_SIZE], axis=0, keepdims=True),
            jnp.sum(product[HEAD_SIZE:], axis=0, keepdims=True),
        ],
        axis=1,
    )
    lse = lse_ref[0, 0]
    d_query, v_sum = 0.0, 0.0
    for j in range(blocks):
        keys = k_ref[j, 0]
        part = bias[pl.ds(j * size, size), :]
        scores = dot(keys, asked, 1, 1) + jnp.concatenate([part, part], axis=1)
        probs = jnp.exp(scores - lse)
        d_probs = dot(v_ref[j, 0], pulled, 1, 1)
        d_scores = (probs * (d_probs - delta)).astype(BF16)
        d_value = dot(probs.astype(BF16), pulled, 1, 0)
        dv_ref[j, 0] = d_value.astype(BF16)
        dk_ref[j, 0] = dot(d_scores, asked, 1, 0).astype(BF16)
        v_sum = v_sum + jnp.sum(d_value, axis=0, keepdims=True)
        d_query = d_query + dot(keys.T, d_scores, 1, 0)
    d_query = join_heads(d_query, count) * HEAD_SIZE**-0.5
    dq_ref[0] = d_query.astype(BF16)
    qsum_ref[0, 0] = jnp.sum(d_query, axis=0, keepdims=True)
    vsum_ref[0, 0] = v_sum


def attend(queries, key_values, flags):
    rows, count, width = queries.shape
    blocks, _, size, _ = key_values.shape
    pairs = width // LANES
    tile = pl.BlockSpec((1, count, LANES), lambda r, p: (r, 0, p))
    area = rows * count * blocks * size
    return pl.pallas_call(
        attend_kernel,
        grid=(rows, pairs),
        in_specs=[
            tile,
            pl.BlockSpec((blocks, 1, size, LANES), lambda r, p: (0, r, 0, p)),
            pl.BlockSpec((blocks, 1, size, LANES), lambda r, p: (0, r, 0, pairs + p)),
            pl.BlockSpec((blocks, 1, 1, size), lambda r, p: (0, r, 0, 0)),
        ],
        out_specs=[tile, tile, pl.BlockSpec((1, 1, 1, 2 * count), lambda r, p: (r, p, 0, 0))],
        out_shape=[
            shaped(BF16, *queries.shape),
            shaped(F32, *queries.shape),
            shaped(F32, rows, pairs, 1, 2 * count),
        ],
        scratch_shapes=[
            pltpu.VMEM((blocks * size, count), F32),
            pltpu.VMEM((blocks * size, 2 * count), F32),
        ],
        compiler_params=parameters(),
        cost_estimate=cost(16 * area * width, 8 * rows * blocks * size * width, area * 12),
        name="attend",
    )(queries, key_values, key_values, flags)


def attend_back(row, held, queries, key_values, d_mixed, mixed_full, lse, flags, after):
    rows, count, width = queries.shape
    blocks, _, size, _ = key_values.shape
    pairs = width // LANES
    tile = pl.BlockSpec((1, count, LANES), lambda p: (row, 0, p))
    keys = pl.BlockSpec((blocks, 1, size, LANES), lambda p: (0, row, 0, p))
    line = lambda w: pl.BlockSpec((1, 1, 1, w), lambda p: (row, p, 0, 0))
    area = count * blocks * size
    grads = shaped(BF16, blocks, rows, size, width)
    sums = shaped(F32, rows, pairs, 1, LANES)
    given = [queries, key_values, key_values, d_mixed, mixed_full, lse, flags]
    extra = [*(held or []), *after]

    def kernel(*refs):
        attend_back_kernel(*refs[: len(given)], *refs[len(given) + len(extra) :])

    return pl.pallas_call(
        kernel,
        grid=(pairs,),
        in_specs=[
            tile, keys, pl.BlockSpec((blocks, 1, size, LANES), lambda p: (0, row, 0, pairs + p)),
            tile, tile, line(2 * count), pl.BlockSpec((blocks, 1, 1, size), lambda p: (0, row, 0, 0)),
            *[ANYWHERE] * len(extra),
        ],
        out_specs=[tile, keys, keys, line(LANES), line(LANES)],
        out_shape=[shaped(BF16, *queries.shape), grads, grads, sums, sums],
        scratch_shapes=[pltpu.VMEM((blocks * size, count), F32)],
        input_output_aliases={len(given) + i: i for i in range(len(held or []))},
        compiler_params=parameters(),
        cost_estimate=cost(32 * area * width, 16 * blocks * size * width, area * 12),
        name=f"attend_back_{row}",
    )(*given, *extra)


def project(near, sources, flags, left, left_other, right, right_other):
    own, width = sources[0].shape
    blocks, row_count, _, size = flags.shape
    total, steps = own * blocks, blocks
    halves, depth, part = left.shape
    half = width // 2

    def kernel(near_ref, *refs):
        first_ref, ahead_ref, lm_ref, lo_ref, rm_ref, ro_ref = refs[blocks : blocks + 6]
        rows_out, turned_ref, q_ref, kv_ref, w_out, vec_ref = refs[blocks + 6 : blocks + 12]
        rows, weights, normed, columns, sems, out_sems = refs[blocks + 12 :]
        step = pl.program_id(0)
        outward = [
            pltpu.make_async_copy(rows, rows_out, out_sems.at[0]),
            pltpu.make_async_copy(weights, w_out, out_sems.at[1]),
        ]

        def norm(at, slot, flags_ref):
            gain, shift = vec_ref[GAIN1 : GAIN1 + 1], vec_ref[SHIFT1 : SHIFT1 + 1]
            embed = vec_ref[EMBED : EMBED + 1]
            for r in range(row_count):
                masked = column(flags_ref[0, r]) >= MASKED
                here = rows[pl.ds(pl.multiple_of(at * own + r * size, size), size), :].astype(F32)
                hat, _ = norm_parts(jnp.where(masked, embed, here))
                normed[slot, r * size : (r + 1) * size, :] = (hat * gain + shift).astype(BF16)

        @pl.when(step == 0)
        def _():
            near_place = near_ref[0]
            later, first = [], []
            for which in range(2):
                mine = near_place if which == 0 else 1 - near_place
                low, high = (lm_ref, rm_ref) if which == 0 else (lo_ref, ro_ref)
                for x in range(halves):
                    at = pl.ds(pl.multiple_of(x * 2 * depth + mine * depth, depth), depth)
                    first.append((high.at[x, :, pl.ds(part, LANES)], columns.at[at, :]))
                    for side, source in enumerate((low, high)):
                        for kind in range(4):
                            later.append(
                                (
                                    source.at[x, :, pl.ds(kind * half, half)],
                                    weights.at[at, pl.ds(kind * width + side * half, half)],
                                )
                            )
            first += [(refs[i], rows.at[pl.ds(i * own, own), :]) for i in range(blocks)]
            copies = [
                pltpu.make_async_copy(a, b, sems.at[i]) for i, (a, b) in enumerate([*first, *later])
            ]
            for copy in copies:
                copy.start()
            for copy in copies[: len(first)]:
                copy.wait()
            outward[0].start()
            vec_ref[...] = columns[...].astype(F32).T[:KINDS]
            norm(0, 0, first_ref)
            for copy in copies[len(first) :]:
                copy.wait()
            outward[1].start()

        slot = lax.rem(step, 2)
        here = normed[slot]
        kv_ref[:, :width] = dot(here, weights[:, width : 2 * width], 1, 0).astype(BF16)
        values = dot(here, weights[:, 2 * width : 3 * width], 1, 0)
        kv_ref[:, width:] = (values + vec_ref[VBIAS : VBIAS + 1]).astype(BF16)
        turned_ref[...] = here.T
        norm(jnp.minimum(step + 1, steps - 1), 1 - slot, ahead_ref)

        @pl.when(step == 0)
        def _():
            asked = dot(here, weights[:, :width], 1, 0) + vec_ref[QBIAS : QBIAS + 1]
            q_ref[...] = (asked * HEAD_SIZE**-0.5).astype(BF16)

        @pl.when(step == steps - 1)
        def _():
            for copy in outward:
                copy.wait()

    def ahead(t, _):
        return (jnp.minimum(t + 1, steps - 1), 0, 0, 0)

    return pl.pallas_call(
        kernel,
        grid_spec=pltpu.PrefetchScalarGridSpec(
            num_scalar_prefetch=1,
            grid=(steps,),
            in_specs=[
                *[ANYWHERE] * blocks,
                whole(1, row_count, 1, size),
                pl.BlockSpec((1, row_count, 1, size), ahead),
                *[ANYWHERE] * 4,
            ],
            out_specs=[
                ANYWHERE,
                pl.BlockSpec((width, own), lambda t, _: (0, t)),
                whole(own, width),
                pl.BlockSpec((own, 2 * width), lambda t, _: (t, 0)),
                ANYWHERE,
                whole(KINDS, width),
            ],
            scratch_shapes=[
                pltpu.VMEM((total, width), BF16),
                pltpu.VMEM((width, 4 * width), BF16),
                pltpu.VMEM((2, own, width), BF16),
                pltpu.VMEM((width, LANES), BF16),
                pltpu.SemaphoreType.DMA((18 * halves + blocks,)),
                pltpu.SemaphoreType.DMA((2,)),
            ],
        ),
        out_shape=[
            shaped(BF16, total, width),
            shaped(BF16, width, total),
            shaped(BF16, own, width),
            shaped(BF16, total, 2 * width),
            shaped(BF16, width, 4 * width),
            shaped(F32, KINDS, width),
        ],
        compiler_params=parameters(40),
        cost_estimate=cost(5 * total * width * width, 8 * total * width + 16 * width * width, total),
        name="project",
    )(near, *sources, flags, flags, left, left_other, right, right_other)


def open_branch(mixed, rows_all, flags, vectors, weights):
    tokens, width = mixed.shape
    _, row_count, _, size = flags.shape

    def kernel(mixed_ref, rows_ref, flags_ref, vec_ref, w_ref, normed_ref, middle_ref):
        masked = column(flags_ref[0, 0]) >= MASKED
        embed, bias = vec_ref[EMBED : EMBED + 1], vec_ref[OBIAS : OBIAS + 1]
        gain, shift = vec_ref[GAIN2 : GAIN2 + 1], vec_ref[SHIFT2 : SHIFT2 + 1]
        added = dot(mixed_ref[...], w_ref[...], 1, 0)
        for c in range(0, size, CHUNK):
            cut = slice(c, c + CHUNK)
            values = jnp.where(masked[cut], embed, rows_ref[cut].astype(F32))
            middle = values + added[cut] + bias
            middle_ref[cut] = middle
            hat, _ = norm_parts(middle)
            normed_ref[cut] = (hat * gain + shift).astype(BF16)

    tile = pl.BlockSpec((size, width), lambda t: (t, 0))
    return pl.pallas_call(
        kernel,
        grid=(row_count,),
        in_specs=[
            tile, tile, pl.BlockSpec((1, 1, 1, size), lambda t: (0, t, 0, 0)), whole(KINDS, width),
            pl.BlockSpec((width, width), lambda t: (0, 3)),
        ],
        out_specs=[tile, tile],
        out_shape=[shaped(BF16, tokens, width), shaped(F32, tokens, width)],
        compiler_params=parameters(),
        cost_estimate=cost(2 * tokens * width * width, 10 * tokens * width),
        name="open_branch",
    )(mixed, rows_all, flags, vectors, weights)


def branch(places, normed, normed_other, pulled, pulled_other, vectors, rest):
    tokens, width = normed.shape
    groups = rest.shape[1] // 2
    cores, length = rest.shape[0], rest.shape[2]
    depth = length // 2
    both = 2 * tokens
    size = 256

    def kernel(
        places_ref, n_ref, no_ref, c_ref, co_ref, vec_ref, down_ref, up_ref,
        total_ref, dn_ref, away_ref, sdown_ref, kdown_ref, gup_ref, gbias_ref,
        normed_all, turned, pulled_all, totals, d_normed, activated, d_hidden, up, down,
    ):
        step = pl.program_id(0)

        @pl.when(step == 0)
        def _():
            normed_all[:tokens] = n_ref[...]
            normed_all[tokens:] = no_ref[...]
            turned[:, :tokens] = n_ref[...].T
            turned[:, tokens:] = no_ref[...].T
            pulled_all[:tokens] = c_ref[...]
            pulled_all[tokens:] = co_ref[...]

        at = 0
        for x in range(2):
            for core in range(cores):
                up[at : at + depth] = up_ref[core, 0, x * depth : (x + 1) * depth]
                down[at : at + depth] = down_ref[core, 0, x * depth : (x + 1) * depth]
                at += depth
        bias = vec_ref[pl.ds(UBIAS + groups * places_ref[0] + step, 1), :]
        bias_grad = 0.0
        for c in range(0, both, size):
            cut = slice(c, c + size)
            hidden = dot(normed_all[cut], up[...], 1, 0) + bias
            d_active = dot(pulled_all[cut], down[...], 1, 1)
            phi = 0.5 * (1.0 + lax.erf(hidden * HALF_ROOT))
            slope = phi + hidden * (0.3989422804014327 * jnp.exp(-0.5 * hidden * hidden))
            activated[cut] = (hidden * phi).astype(BF16)
            grad = (d_active * slope).astype(BF16)
            d_hidden[cut] = grad
            bias_grad += jnp.sum(grad.astype(F32), axis=0, keepdims=True)
        gbias_ref[0] = bias_grad
        for c in range(0, both, size):
            cut = slice(c, c + size)
            more = dot(activated[cut], down[...], 1, 0)
            more_back = dot(d_hidden[cut], up[...], 1, 1)

            @pl.when(step == 0)
            def _(cut=cut, more=more, more_back=more_back):
                totals[cut] = more
                d_normed[cut] = more_back

            @pl.when(step > 0)
            def _(cut=cut, more=more, more_back=more_back):
                totals[cut] += more
                d_normed[cut] += more_back

        gup_ref[0] = dot(turned[...], d_hidden[...], 1, 0).astype(BF16)
        grads = dot(activated[...], pulled_all[...], 0, 0).astype(BF16)
        (sent,), (kept,) = parted(grads, places_ref[1], length)
        for core in range(cores):
            sdown_ref[0, core] = sent[core * depth : (core + 1) * depth]
            kdown_ref[0, core] = kept[core * depth : (core + 1) * depth]

        @pl.when(step == pl.num_programs(0) - 1)
        def _():
            total_ref[...] = totals[:tokens]
            dn_ref[...] = d_normed[:tokens]
            away_ref[0] = totals[tokens:].astype(BF16)
            away_ref[1] = d_normed[tokens:].astype(BF16)

    weight = lambda f: pl.BlockSpec((cores, 1, length, width), lambda k, _: (0, f(k), 0, 0))
    piece = pl.BlockSpec((1, cores, depth, width), lambda k, _: (k, 0, 0, 0))
    square = pl.BlockSpec((1, width, width), lambda k, _: (k, 0, 0))
    patch = whole(tokens, width)
    return pl.pallas_call(
        kernel,
        grid_spec=pltpu.PrefetchScalarGridSpec(
            num_scalar_prefetch=1,
            grid=(groups,),
            in_specs=[
                patch, patch, patch, patch, whole(KINDS, width), weight(lambda k: k),
                weight(lambda k: groups + k),
            ],
            out_specs=[
                patch, patch, whole(2, tokens, width), piece, piece, square,
                pl.BlockSpec((1, 1, width), lambda k, _: (k, 0, 0)),
            ],
            scratch_shapes=[
                pltpu.VMEM((both, width), BF16),
                pltpu.VMEM((width, both), BF16),
                pltpu.VMEM((both, width), BF16),
                pltpu.VMEM((both, width), F32),
                pltpu.VMEM((both, width), F32),
                pltpu.VMEM((both, width), BF16),
                pltpu.VMEM((both, width), BF16),
                pltpu.VMEM((width, width), BF16),
                pltpu.VMEM((width, width), BF16),
            ],
        ),
        out_shape=[
            shaped(F32, tokens, width),
            shaped(F32, tokens, width),
            shaped(BF16, 2, tokens, width),
            shaped(BF16, groups, cores, depth, width),
            shaped(BF16, groups, cores, depth, width),
            shaped(BF16, groups, width, width),
            shaped(F32, groups, 1, width),
        ],
        compiler_params=parameters(52),
        cost_estimate=cost(
            12 * groups * both * width * width, 20 * width * width, 2 * both * width * groups
        ),
        name="branch",
    )(places, normed, normed_other, pulled, pulled_other, vectors, rest, rest)


def between(near, d_normed, d_normed_other, middle, pulled, vectors, mixed, weights, halves):
    tokens, width = mixed.shape
    depth = width // (2 * halves)
    size = tokens // 2

    def kernel(
        near_ref, dn_ref, more_ref, middle_ref, cot_ref, vec_ref, mixed_ref, w_ref,
        dmiddle_ref, dmixed_ref, sent_ref, kept_ref, sums_ref, d_attn, grads,
    ):
        step = pl.program_id(0)
        gain = vec_ref[GAIN2 : GAIN2 + 1]
        sums = 0.0
        for c in range(0, size, CHUNK):
            cut = slice(c, c + CHUNK)
            d_out = dn_ref[cut] + more_ref[0, cut].astype(F32)
            cot = cot_ref[cut].astype(F32)
            hat, rate = norm_parts(middle_ref[cut])
            d_middle = cot + norm_back(d_out * gain, hat, rate)
            dmiddle_ref[cut] = d_middle
            low = d_middle.astype(BF16)
            d_attn[cut] = low
            parts = [low.astype(F32), d_out * hat, d_out, cot]
            sums += jnp.concatenate([jnp.sum(s, axis=0, keepdims=True) for s in parts], axis=0)
        sums = jnp.concatenate([sums, jnp.zeros_like(sums)], axis=0)
        dmixed_ref[...] = dot(d_attn[...], w_ref[...], 1, 1).astype(BF16)
        more = dot(mixed_ref[...], d_attn[...], 0, 0)

        @pl.when(step == 0)
        def _():
            sums_ref[...] = sums
            grads[...] = more

        @pl.when(step == 1)
        def _():
            sums_ref[...] += sums
            value = (grads[...] + more).astype(BF16)
            for x, (sent, kept) in enumerate(zip(*parted(value, near_ref[0], depth), strict=True)):
                sent_ref[x] = sent
                kept_ref[x] = kept

    tile = pl.BlockSpec((size, width), lambda t, _: (t, 0))
    piece = whole(halves, depth, width)
    return pl.pallas_call(
        kernel,
        grid_spec=pltpu.PrefetchScalarGridSpec(
            num_scalar_prefetch=1,
            grid=(2,),
            in_specs=[
                tile, pl.BlockSpec((1, size, width), lambda t, _: (1, t, 0)), tile, tile,
                whole(KINDS, width), tile, pl.BlockSpec((width, width), lambda t, _: (0, 3)),
            ],
            out_specs=[tile, tile, piece, piece, whole(8, width)],
            scratch_shapes=[pltpu.VMEM((size, width), BF16), pltpu.VMEM((width, width), F32)],
        ),
        out_shape=[
            shaped(F32, tokens, width),
            shaped(BF16, tokens, width),
            shaped(BF16, halves, depth, width),
            shaped(BF16, halves, depth, width),
            shaped(F32, 8, width),
        ],
        compiler_params=parameters(),
        cost_estimate=cost(4 * tokens * width * width, 16 * tokens * width),
        name="between",
    )(near, d_normed, d_normed_other, middle, pulled, vectors, mixed, weights)


def weight_grads(near, turned, d_key, d_value, d_query, halves, after):
    width, total = turned.shape
    own = d_query.shape[0]
    depth = width // (2 * halves)

    def kernel(near_ref, turned_ref, dk_ref, dv_ref, dq_ref, *refs):
        sa_ref, ka_ref, sb_ref, kb_ref = refs[len(after) :]
        step = pl.program_id(0)

        def put(value, sent_ref, kept_ref, at):
            pieces = zip(*parted(value.astype(BF16), near_ref[0], depth), strict=True)
            for x, (sent, kept) in enumerate(pieces):
                sent_ref[x, :, at : at + width] = sent
                kept_ref[x, :, at : at + width] = kept

        @pl.when(step == 0)
        def _():
            put(dot(turned_ref[:, :own], dq_ref[...], 1, 0), sa_ref, ka_ref, 0)

        @pl.when(step == 1)
        def _():
            put(dot(turned_ref[...], dk_ref[...], 1, 0), sa_ref, ka_ref, width)

        @pl.when(step == 2)
        def _():
            put(dot(turned_ref[...], dv_ref[...], 1, 0), sb_ref, kb_ref, 0)

    pair, single = whole(halves, depth, 2 * width), whole(halves, depth, width)
    return pl.pallas_call(
        kernel,
        grid_spec=pltpu.PrefetchScalarGridSpec(
            num_scalar_prefetch=1,
            grid=(3,),
            in_specs=[
                whole(width, total), whole(total, width), whole(total, width), whole(own, width),
                *[ANYWHERE] * len(after),
            ],
            out_specs=[pair, pair, single, single],
        ),
        out_shape=[
            shaped(BF16, halves, depth, 2 * width),
            shaped(BF16, halves, depth, 2 * width),
            shaped(BF16, halves, depth, width),
            shaped(BF16, halves, depth, width),
        ],
        compiler_params=parameters(36),
        cost_estimate=cost(5 * total * width * width, 8 * total * width + 12 * width * width),
        name="weight_grads",
    )(near, turned, d_key, d_value, d_query, *after)


def first_norm(
    near, d_key, d_value, d_query, rows_all, flags, vectors, weights, d_middle, sums, gbias, qsum, vsum, halves, after,
):
    total, width = rows_all.shape
    blocks, row_count, _, size = flags.shape
    own = d_query.shape[0]
    depth = width // (2 * halves)
    groups = gbias.shape[0]

    def kernel(near_ref, *refs):
        (
            dk_ref, dv_ref, dq_ref, rows_ref, flags_ref, vec_ref, w_ref, dmiddle_ref, sums_ref,
            gbias_ref, qsum_ref, vsum_ref,
        ) = refs[:12]
        far_ref, near_share_ref, own_ref, sent_ref, kept_ref, totals = refs[12 + len(after) :]
        step = pl.program_id(0)

        def put_share(step, cut, value):
            @pl.when(step < blocks // 2)
            def _():
                far_ref[0, cut] = value

            @pl.when(step >= blocks // 2)
            def _():
                near_share_ref[0, cut] = value

        def one(mine):
            d_all = dot(dk_ref[...], w_ref[:, width : 2 * width], 1, 1)
            d_all += dot(dv_ref[...], w_ref[:, 2 * width :], 1, 1)
            if mine:
                d_all += dot(dq_ref[...], w_ref[:, :width], 1, 1)
            gain, embed = vec_ref[GAIN1 : GAIN1 + 1], vec_ref[EMBED : EMBED + 1]
            more = 0.0
            for r in range(row_count):
                cut = slice(r * size, (r + 1) * size)
                masked = column(flags_ref[0, r]) >= MASKED
                d_normed = d_all[cut]
                hat, rate = norm_parts(jnp.where(masked, embed, rows_ref[cut].astype(F32)))
                d_embedded = norm_back(d_normed * gain, hat, rate)
                if mine:
                    d_embedded = d_embedded + dmiddle_ref[cut]
                    own_ref[cut] = d_embedded
                else:
                    put_share(step, cut, d_embedded.astype(BF16))
                parts = [jnp.where(masked, d_embedded, 0.0), d_normed * hat, d_normed]
                more += jnp.concatenate([jnp.sum(s, axis=0, keepdims=True) for s in parts], axis=0)
            return more

        @pl.when(step == 0)
        def _():
            totals[:3] = one(True)

        @pl.when(step > 0)
        def _():
            totals[:3] += one(False)

        @pl.when(step == blocks - 1)
        def _():
            def line(ref):
                rows, pairs = ref.shape[0], ref.shape[1]
                return sum(
                    jnp.concatenate([ref[r, p] for p in range(pairs)], axis=1) for r in range(rows)
                )

            bias = jnp.concatenate([gbias_ref[k] for k in range(groups)], axis=0)
            none = jnp.zeros_like(bias)
            low = near_ref[0] == 0
            kinds = [
                totals[:3], line(qsum_ref), line(vsum_ref), sums_ref[:4],
                jnp.where(low, bias, none), jnp.where(low, none, bias),
            ]
            kinds.append(jnp.zeros((LANES - UBIAS - 2 * groups, width), F32))
            small = jnp.concatenate(kinds, axis=0).T.astype(BF16)
            for x, (sent, kept) in enumerate(zip(*parted(small, near_ref[0], depth), strict=True)):
                sent_ref[x] = sent
                kept_ref[x] = kept

    tile = pl.BlockSpec((own, width), lambda t, _: (t, 0))
    piece = whole(halves, depth, LANES)
    return pl.pallas_call(
        kernel,
        grid_spec=pltpu.PrefetchScalarGridSpec(
            num_scalar_prefetch=1,
            grid=(blocks,),
            in_specs=[
                tile, tile, whole(own, width), tile,
                pl.BlockSpec((1, row_count, 1, size), lambda t, _: (t, 0, 0, 0)),
                whole(KINDS, width), whole(width, 3 * width), whole(own, width),
                whole(*sums.shape), whole(*gbias.shape), whole(*qsum.shape), whole(*vsum.shape),
                *[ANYWHERE] * len(after),
            ],
            out_specs=[
                pl.BlockSpec((1, own, width), lambda t, _: (jnp.clip(t - 1, 0, blocks // 2 - 2), 0, 0)),
                pl.BlockSpec((1, own, width), lambda t, _: (jnp.maximum(t - blocks // 2, 0), 0, 0)),
                whole(own, width), piece, piece,
            ],
            scratch_shapes=[pltpu.VMEM((8, width), F32)],
        ),
        out_shape=[
            shaped(BF16, blocks // 2 - 1, own, width),
            shaped(BF16, blocks // 2, own, width),
            shaped(F32, own, width),
            shaped(BF16, halves, depth, LANES),
            shaped(BF16, halves, depth, LANES),
        ],
        compiler_params=parameters(36),
        cost_estimate=cost(5 * total * width * width, 8 * total * width + 12 * width * width, total),
        name="first_norm",
    )(near, d_key, d_value, d_query, rows_all, flags, vectors, weights, d_middle, sums, gbias, qsum, vsum, *after)


def after(value, *others):
    return lax.optimization_barrier((value, *others))[0]


class Links:
    def __init__(self, seq, rows):
        self.sizes = {"seq": seq, "rows": rows}
        order = []
        for axis in EVERY:
            mask = self.sizes[axis] // 2
            while mask:
                order.append((axis, mask))
                mask //= 2
        self.order = order
        place = {axis: lax.axis_index(axis) for axis in EVERY}
        self.value = {(a, m): ((place[a] // m) % 2).astype(jnp.int32) for a, m in order}
        self.near = ("seq", 1)
        self.first = ("seq", 2)
        self.second = ("rows", 1)
        self.others = [b for b in order if b[0] == "rows" and b[1] > 1]

    def swap(self, array, bit):
        axis, mask = bit
        return lax.ppermute(array, axis, [(i, i ^ mask) for i in range(self.sizes[axis])])

    def pick(self, array, bit, other=False, axis=0):
        at = 1 - self.value[bit] if other else self.value[bit]
        return lax.dynamic_index_in_dim(array, at, axis, keepdims=False)

    def gather(self, shard, bits, wanted):
        held, have = shard, []
        for i, bit in enumerate(bits):
            if i in wanted:
                held = after(held, *wanted[i])
            have = sorted([*have, bit], key=self.order.index)
            parts = held.reshape(2 ** have.index(bit), -1, held.shape[-1])
            other = self.swap(held, bit).reshape(parts.shape)
            upper = self.value[bit] == 1
            low = jnp.where(upper, other, parts)
            high = jnp.where(upper, parts, other)
            held = jnp.stack([low, high], axis=1).reshape(-1, held.shape[-1])
        return held

    def half(self, held, have, bit, other):
        before = 1
        for key in have[: have.index(bit)]:
            before *= key if isinstance(key, int) else 2
        parts = held.reshape(before, 2, -1, held.shape[-1])
        return self.pick(parts, bit, other, 1).reshape(-1, held.shape[-1])

    def add(self, kept, came, have, bit):
        def part(other):
            first, second = (self.half(a, have, bit, other) for a in (kept, came))
            return (first.astype(F32) + second.astype(F32)).astype(BF16)

        return part(True), part(False), [b for b in have if b != bit]


def body(
    patches, segments, masked, mask_embedding, norm1_gain, norm1_bias, qkv_weight, query_bias,
    value_bias, out_weight, out_bias, norm2_gain, norm2_bias, up_weight, up_bias, down_weight,
    down_bias, cotangent, *, seq, rows,
):
    links = Links(seq, rows)
    row_count, patch_count, width = patches.shape
    tokens = row_count * patch_count
    n = qkv_weight.shape[0]
    devices = seq * rows
    groups = up_weight.shape[1] // width
    mine = groups // 2
    half = width // 2
    halves = seq // 2
    depth = rows * n
    near, first, second, others = links.near, links.first, links.second, links.others
    near_place = links.value[near].reshape(1)

    flags = (segments + MASKED * masked).astype(BF16).reshape(1, row_count, patch_count)
    sources = [patches.reshape(tokens, width)]
    for bit in (first, near):
        flags = jnp.concatenate([flags, links.swap(flags, bit)], axis=0)
        sources += [links.swap(source, bit) for source in sources]
    early_ones, late_ones = [sources[1], flags], sources[2:]
    flags = flags.astype(F32).reshape(seq, row_count, 1, patch_count)
    small = [
        mask_embedding, norm1_gain, norm1_bias, query_bias, value_bias, out_bias, norm2_gain,
        norm2_bias, down_bias,
    ]
    columns = jnp.concatenate([jnp.stack(small), up_bias.reshape(groups, n)], axis=0).T
    columns = jnp.pad(columns, ((0, 0), (0, LANES - columns.shape[1])))
    fourths = [qkv_weight[:, i * half : (i + 1) * half] for i in range(6)]
    fourths += [out_weight[:, :half], out_weight[:, half:]]
    left = jnp.concatenate(fourths[::2], axis=1)
    right = jnp.concatenate([*fourths[1::2], columns], axis=1)
    left = links.gather(left, [*others, second, first], {2: early_ones, 3: late_ones}).reshape(halves, depth, -1)
    right = links.gather(right, [*others, first, second], {}).reshape(halves, depth, -1)
    left_other, right_other = links.swap(left, near), links.swap(right, near)

    packed = jnp.stack(
        [
            down_weight.reshape(2, mine, n, width),
            up_weight.reshape(n, devices, groups, n).transpose(2, 0, 1, 3).reshape(2, mine, n, width),
        ],
        axis=1,
    ).reshape(2, 2 * mine, n, width)
    kept, other = links.pick(packed, near), links.swap(links.pick(packed, near, True), near)
    low = links.value[near] == 0
    packed = jnp.stack([jnp.where(low, kept, other), jnp.where(low, other, kept)], axis=0)
    same_core = [
        [(x * 2 + core) * rows + r for x in range(halves) for r in range(rows)] for core in range(2)
    ]
    rest = lax.all_gather(packed, EVERY, axis=2, tiled=True, axis_index_groups=same_core)

    rows_all, turned, queries, key_values, weights, vectors = project(
        near_place, sources, flags, left, left_other, right, right_other
    )
    queries = queries.reshape(row_count, patch_count, width)
    key_values = key_values.reshape(seq, row_count, patch_count, 2 * width)
    mixed, mixed_full, lse = attend(queries, key_values, flags)
    mixed = mixed.reshape(tokens, width)
    d_branch = cotangent.reshape(tokens, width)
    d_branch_other = links.swap(d_branch, near)
    normed_two, middle = open_branch(mixed, rows_all, flags, vectors, weights)
    places = jnp.stack([links.value[near], links.value[first]])
    added, d_normed, away, down_sent, down_kept, grad_up, grad_up_bias = branch(
        places, normed_two, links.swap(normed_two, near), d_branch, d_branch_other, vectors, rest
    )

    row_bits = [*others, second]
    have = [first, *row_bits]
    flat = lambda held: held.reshape(-1, held.shape[-1])
    down_sent, down_kept = flat(down_sent), flat(down_kept)
    up_order = [mine, first, near, *row_bits]
    grad_up = flat(grad_up)
    up_sent = links.half(grad_up, up_order, second, True)
    up_kept = links.half(grad_up, up_order, second, False)
    up_order = [mine, first, near, *others]
    away = links.swap(away, near)
    down_came, up_came = links.swap(down_sent, first), links.swap(up_sent, second)
    d_middle, d_mixed, out_sent, out_kept, sums = between(
        near_place, d_normed, away, middle, d_branch, vectors, mixed, weights, halves
    )
    out_came = links.swap(out_sent, near)
    d_mixed = d_mixed.reshape(row_count, patch_count, width)

    given = (queries, key_values, d_mixed, mixed_full, lse, flags)
    grads = None
    for row in range(row_count):
        grads = list(attend_back(row, grads, *given, [down_sent, up_sent] if row == 0 else []))
    d_query, d_key, d_value, query_sums, value_sums = grads

    down_sent, down_kept, down_order = links.add(
        after(down_kept, d_query), down_came, [mine, near, *row_bits], second
    )
    down_came = links.swap(down_sent, second)
    up_sent, up_kept, up_order = links.add(after(up_kept, down_sent), up_came, up_order, first)
    up_came = links.swap(up_sent, first)
    d_query = d_query.reshape(tokens, width)
    d_key = d_key.reshape(-1, width)
    d_value = d_value.reshape(-1, width)
    pair_sent, pair_kept, value_sent, value_kept = weight_grads(
        near_place, turned, d_key, d_value, d_query, halves, [down_sent, up_sent]
    )
    early_kept = jnp.concatenate([after(down_kept, pair_sent), up_kept], axis=0)
    early_came = jnp.concatenate([down_came, up_came], axis=0)
    early_order = [2 * mine, near, *others]
    early_sent, early_kept, early_order = links.add(early_kept, early_came, early_order, others[-1])
    early_came = links.swap(early_sent, others[-1])
    pair_came = links.swap(flat(after(pair_sent, early_sent)), near)
    value_came = links.swap(flat(after(value_sent, early_sent)), near)
    pair_sent, pair_kept, pair_order = links.add(flat(pair_kept), pair_came, have, second)
    pair_came = links.swap(pair_sent, second)
    last_kept = jnp.concatenate([flat(value_kept), flat(out_kept)], axis=1)
    last_came = jnp.concatenate([value_came, flat(out_came)], axis=1)
    last_sent, last_kept, last_order = links.add(after(last_kept, pair_sent), last_came, have, first)
    last_came = links.swap(last_sent, first)
    far_share, near_share, own, small_sent, small_kept = first_norm(
        near_place, d_key, d_value, d_query, rows_all, flags, vectors, weights, d_middle, sums,
        grad_up_bias, query_sums, value_sums, halves, [early_sent, pair_sent, last_sent],
    )

    early, pair = [early_kept, early_came, early_order], [pair_kept, pair_came, pair_order]
    last = [last_kept, last_came, last_order]

    def go(item, bit, gone):
        gone, item[0], item[2] = links.add(after(item[0], gone), item[1], item[2], bit)
        item[1] = links.swap(gone, bit)
        return gone

    rest_bits = others[-2::-1]
    gone = own
    for bit in rest_bits[:1]:
        gone = go(early, bit, gone)
    gone = go(pair, first, gone)
    gone = go(last, second, gone)
    near_share = links.swap(after(near_share, gone), near)
    small = [flat(small_kept), links.swap(flat(after(small_sent, gone)), near), have]
    gone = go(small, first, gone)
    gone = (after(far_share, gone).astype(F32) + near_share[1:].astype(F32)).astype(BF16)
    far_share = links.swap(gone, first)
    gone = go(small, second, gone)
    gone = go(pair, others[-1], gone)
    last[0] = jnp.concatenate([last[0], small[0]], axis=1)
    last[1] = jnp.concatenate([last[1], small[1]], axis=1)
    gone = go(last, others[-1], gone)
    for bit in rest_bits:
        gone = go(pair, bit, gone)
        gone = go(last, bit, gone)
    for bit in rest_bits[1:]:
        gone = go(early, bit, gone)
    early[0] = after(early[0], gone)
    added = after(added, gone)
    early, pair, last = (a.astype(F32) + b.astype(F32) for a, b, _ in (early, pair, last))
    early = early.reshape(2 * mine, 2, n, width)
    far = links.swap(links.pick(early, near, True, 1).astype(BF16), near).astype(F32)
    early = links.pick(early, near, False, 1)
    low = links.value[near] == 0
    joined = jnp.stack([jnp.where(low, early, far), jnp.where(low, far, early)], axis=0)
    output = middle + added + away[0].astype(F32) + vectors[DBIAS]
    output = output.astype(BF16)
    down_sum = joined[:, :mine].reshape(-1, width)
    up_sum = joined[:, mine:].reshape(groups, n, devices, n).transpose(1, 2, 0, 3).reshape(n, -1)
    input_grad = own + near_share[0].astype(F32) + far_share[0].astype(F32)
    is_masked = masked.reshape(tokens, 1) == 1
    input_grad = jnp.where(is_masked, 0.0, input_grad)
    project_sum = jnp.concatenate([pair, last[:, :width]], axis=1)
    out_sum = last[:, width : 2 * width]
    tail = last[:, 2 * width :].T
    shape = (row_count, patch_count, width)
    return (
        output.reshape(shape), input_grad.reshape(shape), tail[EMBED], tail[GAIN1], tail[SHIFT1],
        project_sum, tail[QBIAS], tail[VBIAS], out_sum, tail[OBIAS], tail[GAIN2], tail[SHIFT2],
        up_sum, tail[UBIAS : UBIAS + groups].reshape(-1), down_sum, tail[DBIAS],
    )


def solution(mesh):
    one, two = P(EVERY), P(EVERY, None)
    rows, flags = P("rows", "seq", None), P("rows", "seq")
    seq, row_groups = mesh.shape["seq"], mesh.shape["rows"]

    def run(*arguments):
        return body(*arguments, seq=seq, rows=row_groups)

    return jax.shard_map(
        run,
        mesh=mesh,
        in_specs=(
            rows, flags, flags, one, one, one, two, one, one, two, one, one, one, two, one, two,
            one, rows,
        ),
        out_specs=(
            rows, rows, one, one, one, two, one, one, two, one, one, one, two, one, two, one,
        ),
        check_vma=False,
    )
```

```python
import jax
import jax.numpy as jnp
from jax import lax
from jax.experimental import pallas as pl
from jax.experimental.pallas import tpu as pltpu
from jax.sharding import PartitionSpec as P

HEAD_SIZE = 64
LANES = 128
CHUNK = 256
PAIRS = 6
PAIRS_BACK = 6
MASKED = 16
EPSILON = 1e-06
FLOOR_SCORE = -1e30
HALF_ROOT = 0.7071067811865476
MIB = 2**20
EVERY = ("seq", "rows")
BF16 = jnp.bfloat16
F32 = jnp.float32
EMBED, GAIN1, SHIFT1, QBIAS, VBIAS, OBIAS, GAIN2, SHIFT2, DBIAS, UBIAS = range(10)
KINDS = 16


def dot(left, right, left_dim, right_dim):
    return lax.dot_general(
        left, right, (((left_dim,), (right_dim,)), ((), ())), preferred_element_type=F32
    )


def column(row):
    return jnp.broadcast_to(row, (8, row.shape[1])).T[:, :1]


def segment_of(flags):
    return flags - jnp.where(flags >= MASKED, float(MASKED), 0.0)


def norm_parts(values):
    mean = jnp.mean(values, axis=-1, keepdims=True)
    centered = values - mean
    rate = lax.rsqrt(jnp.mean(centered * centered, axis=-1, keepdims=True) + EPSILON)
    return centered * rate, rate


def norm_back(pulled, hat, rate):
    first = jnp.mean(pulled, axis=-1, keepdims=True)
    second = jnp.mean(pulled * hat, axis=-1, keepdims=True)
    return rate * (pulled - first - hat * second)


def parted(value, mine, depth):
    sent, kept = [], []
    for x in range(value.shape[0] // (2 * depth)):
        low = value[2 * x * depth : (2 * x + 1) * depth]
        high = value[(2 * x + 1) * depth : (2 * x + 2) * depth]
        sent.append(jnp.where(mine == 0, high, low))
        kept.append(jnp.where(mine == 0, low, high))
    return sent, kept


def whole(*shape):
    return pl.BlockSpec(shape, lambda *_: (0,) * len(shape))


ANYWHERE = pl.BlockSpec(memory_space=pl.ANY)


def shaped(dtype, *shape):
    return jax.ShapeDtypeStruct(shape, dtype)


def placed(dtype, *shape):
    return pltpu.HBM(shape, dtype)


def far(array):
    return pltpu.with_memory_space_constraint(array, pltpu.HBM)


def parameters(mib=32):
    return pltpu.CompilerParams(vmem_limit_bytes=mib * MIB)


def cost(flops, nbytes, transcendentals=0):
    return pl.CostEstimate(flops=flops, bytes_accessed=nbytes, transcendentals=transcendentals)


def split_heads(pair):
    lane = lax.broadcasted_iota(jnp.int32, pair.shape, 1)
    zero = jnp.zeros_like(pair)
    return jnp.concatenate(
        [jnp.where(lane < HEAD_SIZE, pair, zero), jnp.where(lane < HEAD_SIZE, zero, pair)], axis=0
    )


def join_heads(both, count):
    row = lax.broadcasted_iota(jnp.int32, (both.shape[0], count), 0)
    return jnp.where(row < HEAD_SIZE, both[:, :count], both[:, count:]).T


def set_bias(flags_ref, bias):
    blocks, size = flags_ref.shape[0], flags_ref.shape[3]
    asked = segment_of(flags_ref[0, 0])
    for j in range(blocks):
        keys = column(segment_of(flags_ref[j, 0]))
        bias[pl.ds(j * size, size), :] = jnp.where((keys == asked) & (keys > 0.0), 0.0, FLOOR_SCORE)


def attend_kernel(q_ref, k_ref, v_ref, flags_ref, mix_ref, full_ref, lse_ref, bias, held):
    count, blocks, size = q_ref.shape[1], k_ref.shape[0], k_ref.shape[2]

    @pl.when(pl.program_id(1) == 0)
    def _():
        set_bias(flags_ref, bias)

    live = segment_of(flags_ref[0, 0]) > 0.0
    live = jnp.concatenate([live, live], axis=1)
    for u in range(PAIRS):
        lanes = slice(u * LANES, (u + 1) * LANES)
        asked = split_heads(q_ref[0, :, lanes])
        top = None
        for j in range(blocks):
            rows = pl.ds(j * size, size)
            part = bias[rows, :]
            scores = dot(k_ref[j, 0, :, lanes], asked, 1, 1) + jnp.concatenate([part, part], axis=1)
            held[u % 2, rows, :] = scores
            high = jnp.max(scores, axis=0, keepdims=True)
            top = high if top is None else jnp.maximum(top, high)
        total, mixed = 0.0, 0.0
        for j in range(blocks):
            weights = jnp.exp(held[u % 2, pl.ds(j * size, size), :] - top)
            total = total + jnp.sum(weights, axis=0, keepdims=True)
            mixed = mixed + dot(v_ref[j, 0, :, lanes].T, weights.astype(BF16), 1, 0)
        result = join_heads(mixed * jnp.where(live, 1.0 / total, 0.0), count)
        mix_ref[0, :, lanes] = result.astype(BF16)
        full_ref[0, :, lanes] = result
        lse_ref[0, u] = jnp.where(live, top + jnp.log(total), 0.0)


def attend_back_kernel(
    q_ref, k_ref, v_ref, dm_ref, full_ref, lse_ref, flags_ref,
    dq_ref, dk_ref, dv_ref, qsum_ref, vsum_ref, bias,
):
    count, blocks, size = q_ref.shape[1], k_ref.shape[0], k_ref.shape[2]

    @pl.when(pl.program_id(0) == 0)
    def _():
        set_bias(flags_ref, bias)

    for u in range(PAIRS_BACK):
        lanes = slice(u * LANES, (u + 1) * LANES)
        d_mixed = dm_ref[0, :, lanes]
        asked, pulled = split_heads(q_ref[0, :, lanes]), split_heads(d_mixed)
        product = (d_mixed.astype(F32) * full_ref[0, :, lanes]).T
        delta = jnp.concatenate(
            [
                jnp.sum(product[:HEAD_SIZE], axis=0, keepdims=True),
                jnp.sum(product[HEAD_SIZE:], axis=0, keepdims=True),
            ],
            axis=1,
        )
        lse = lse_ref[0, u]
        d_query, v_sum = 0.0, 0.0
        for j in range(blocks):
            keys = k_ref[j, 0, :, lanes]
            part = bias[pl.ds(j * size, size), :]
            scores = dot(keys, asked, 1, 1) + jnp.concatenate([part, part], axis=1)
            probs = jnp.exp(scores - lse)
            d_probs = dot(v_ref[j, 0, :, lanes], pulled, 1, 1)
            d_scores = (probs * (d_probs - delta)).astype(BF16)
            d_value = dot(probs.astype(BF16), pulled, 1, 0)
            dv_ref[j, 0, :, lanes] = d_value.astype(BF16)
            dk_ref[j, 0, :, lanes] = dot(d_scores, asked, 1, 0).astype(BF16)
            v_sum = v_sum + jnp.sum(d_value, axis=0, keepdims=True)
            d_query = d_query + dot(keys.T, d_scores, 1, 0)
        d_query = join_heads(d_query, count) * HEAD_SIZE**-0.5
        dq_ref[0, :, lanes] = d_query.astype(BF16)
        qsum_ref[0, u] = jnp.sum(d_query, axis=0, keepdims=True)
        vsum_ref[0, u] = v_sum


def attend(queries, key_values, flags):
    rows, count, width = queries.shape
    blocks, _, size, _ = key_values.shape
    pairs = width // LANES
    tile = pl.BlockSpec((1, count, PAIRS * LANES), lambda r, p: (r, 0, p))
    steps = pairs // PAIRS
    area = rows * count * blocks * size
    return pl.pallas_call(
        attend_kernel,
        grid=(rows, steps),
        in_specs=[
            tile,
            pl.BlockSpec((blocks, 1, size, PAIRS * LANES), lambda r, p: (0, r, 0, p)),
            pl.BlockSpec((blocks, 1, size, PAIRS * LANES), lambda r, p: (0, r, 0, steps + p)),
            pl.BlockSpec((blocks, 1, 1, size), lambda r, p: (0, r, 0, 0)),
        ],
        out_specs=[tile, tile, pl.BlockSpec((1, PAIRS, 1, 2 * count), lambda r, p: (r, p, 0, 0))],
        out_shape=[
            shaped(BF16, *queries.shape),
            placed(F32, *queries.shape),
            shaped(F32, rows, pairs, 1, 2 * count),
        ],
        scratch_shapes=[
            pltpu.VMEM((blocks * size, count), F32),
            pltpu.VMEM((2, blocks * size, 2 * count), F32),
        ],
        compiler_params=parameters(),
        cost_estimate=cost(16 * area * width, 8 * rows * blocks * size * width, area * 12),
        name="attend",
    )(far(queries), far(key_values), far(key_values), flags)


def attend_back(row, held, queries, key_values, d_mixed, mixed_full, lse, flags, after):
    rows, count, width = queries.shape
    blocks, _, size, _ = key_values.shape
    pairs = width // LANES
    tile = pl.BlockSpec((1, count, PAIRS_BACK * LANES), lambda p: (row, 0, p))
    steps = pairs // PAIRS_BACK
    keys = pl.BlockSpec((blocks, 1, size, PAIRS_BACK * LANES), lambda p: (0, row, 0, p))
    line = lambda w: pl.BlockSpec((1, PAIRS_BACK, 1, w), lambda p: (row, p, 0, 0))
    area = count * blocks * size
    grads = placed(BF16, blocks, rows, size, width)
    sums = shaped(F32, rows, pairs, 1, LANES)
    given = [queries, key_values, key_values, d_mixed, mixed_full, lse, flags]
    extra = [*(held or []), *after]

    def kernel(*refs):
        attend_back_kernel(*refs[: len(given)], *refs[len(given) + len(extra) :])

    return pl.pallas_call(
        kernel,
        grid=(steps,),
        in_specs=[
            tile, keys, pl.BlockSpec((blocks, 1, size, PAIRS_BACK * LANES), lambda p: (0, row, 0, steps + p)),
            tile, tile, line(2 * count), pl.BlockSpec((blocks, 1, 1, size), lambda p: (0, row, 0, 0)),
            *[ANYWHERE] * len(extra),
        ],
        out_specs=[tile, keys, keys, line(LANES), line(LANES)],
        out_shape=[placed(BF16, *queries.shape), grads, grads, sums, sums],
        scratch_shapes=[pltpu.VMEM((blocks * size, count), F32)],
        input_output_aliases={len(given) + i: i for i in range(len(held or []))},
        compiler_params=parameters(),
        cost_estimate=cost(32 * area * width, 16 * blocks * size * width, area * 12),
        name=f"attend_back_{row}",
    )(*given, *extra)


def project(near, sources, flags, left, left_other, right, right_other):
    own, width = sources[0].shape
    blocks, row_count, _, size = flags.shape
    total, steps = own * blocks, blocks
    halves, depth, part = left.shape
    half = width // 2

    def kernel(near_ref, *refs):
        first_ref, ahead_ref, lm_ref, lo_ref, rm_ref, ro_ref = refs[blocks : blocks + 6]
        rows_out, turned_ref, q_ref, kv_ref, w_out, vec_ref = refs[blocks + 6 : blocks + 12]
        rows, weights, normed, columns, sems, out_sems = refs[blocks + 12 :]
        step = pl.program_id(0)
        outward = [
            pltpu.make_async_copy(rows, rows_out, out_sems.at[0]),
            pltpu.make_async_copy(weights, w_out, out_sems.at[1]),
        ]

        def norm(at, slot, flags_ref):
            gain, shift = vec_ref[GAIN1 : GAIN1 + 1], vec_ref[SHIFT1 : SHIFT1 + 1]
            embed = vec_ref[EMBED : EMBED + 1]
            for r in range(row_count):
                masked = column(flags_ref[0, r]) >= MASKED
                here = rows[pl.ds(pl.multiple_of(at * own + r * size, size), size), :].astype(F32)
                hat, _ = norm_parts(jnp.where(masked, embed, here))
                normed[slot, r * size : (r + 1) * size, :] = (hat * gain + shift).astype(BF16)

        @pl.when(step == 0)
        def _():
            near_place = near_ref[0]
            later, first = [], []
            for which in range(2):
                mine = near_place if which == 0 else 1 - near_place
                low, high = (lm_ref, rm_ref) if which == 0 else (lo_ref, ro_ref)
                for x in range(halves):
                    at = pl.ds(pl.multiple_of(x * 2 * depth + mine * depth, depth), depth)
                    first.append((high.at[x, :, pl.ds(part, LANES)], columns.at[at, :]))
                    for side, source in enumerate((low, high)):
                        for kind in range(4):
                            later.append(
                                (
                                    source.at[x, :, pl.ds(kind * half, half)],
                                    weights.at[at, pl.ds(kind * width + side * half, half)],
                                )
                            )
            first += [(refs[i], rows.at[pl.ds(i * own, own), :]) for i in range(blocks)]
            copies = [
                pltpu.make_async_copy(a, b, sems.at[i]) for i, (a, b) in enumerate([*first, *later])
            ]
            for copy in copies:
                copy.start()
            for copy in copies[: len(first)]:
                copy.wait()
            outward[0].start()
            vec_ref[...] = columns[...].astype(F32).T[:KINDS]
            norm(0, 0, first_ref)
            for copy in copies[len(first) :]:
                copy.wait()
            outward[1].start()

        slot = lax.rem(step, 2)
        here = normed[slot]
        kv_ref[:, :width] = dot(here, weights[:, width : 2 * width], 1, 0).astype(BF16)
        values = dot(here, weights[:, 2 * width : 3 * width], 1, 0)
        kv_ref[:, width:] = (values + vec_ref[VBIAS : VBIAS + 1]).astype(BF16)
        turned_ref[...] = here.T
        norm(jnp.minimum(step + 1, steps - 1), 1 - slot, ahead_ref)

        @pl.when(step == 0)
        def _():
            asked = dot(here, weights[:, :width], 1, 0) + vec_ref[QBIAS : QBIAS + 1]
            q_ref[...] = (asked * HEAD_SIZE**-0.5).astype(BF16)

        @pl.when(step == steps - 1)
        def _():
            for copy in outward:
                copy.wait()

    def ahead(t, _):
        return (jnp.minimum(t + 1, steps - 1), 0, 0, 0)

    return pl.pallas_call(
        kernel,
        grid_spec=pltpu.PrefetchScalarGridSpec(
            num_scalar_prefetch=1,
            grid=(steps,),
            in_specs=[
                *[ANYWHERE] * blocks,
                whole(1, row_count, 1, size),
                pl.BlockSpec((1, row_count, 1, size), ahead),
                *[ANYWHERE] * 4,
            ],
            out_specs=[
                ANYWHERE,
                pl.BlockSpec((width, own), lambda t, _: (0, t)),
                whole(own, width),
                pl.BlockSpec((own, 2 * width), lambda t, _: (t, 0)),
                ANYWHERE,
                whole(KINDS, width),
            ],
            scratch_shapes=[
                pltpu.VMEM((total, width), BF16),
                pltpu.VMEM((width, 4 * width), BF16),
                pltpu.VMEM((2, own, width), BF16),
                pltpu.VMEM((width, LANES), BF16),
                pltpu.SemaphoreType.DMA((18 * halves + blocks,)),
                pltpu.SemaphoreType.DMA((2,)),
            ],
        ),
        out_shape=[
            placed(BF16, total, width),
            placed(BF16, width, total),
            placed(BF16, own, width),
            placed(BF16, total, 2 * width),
            placed(BF16, width, 4 * width),
            shaped(F32, KINDS, width),
        ],
        compiler_params=parameters(40),
        cost_estimate=cost(5 * total * width * width, 8 * total * width + 16 * width * width, total),
        name="project",
    )(near, *sources, flags, flags, left, left_other, right, right_other)


def open_branch(mixed, rows_all, flags, vectors, weights):
    tokens, width = mixed.shape
    _, row_count, _, size = flags.shape

    def kernel(mixed_ref, rows_ref, flags_ref, vec_ref, w_ref, normed_ref, middle_ref):
        masked = column(flags_ref[0, 0]) >= MASKED
        embed, bias = vec_ref[EMBED : EMBED + 1], vec_ref[OBIAS : OBIAS + 1]
        gain, shift = vec_ref[GAIN2 : GAIN2 + 1], vec_ref[SHIFT2 : SHIFT2 + 1]
        added = dot(mixed_ref[...], w_ref[...], 1, 0)
        for c in range(0, size, CHUNK):
            cut = slice(c, c + CHUNK)
            values = jnp.where(masked[cut], embed, rows_ref[cut].astype(F32))
            middle = values + added[cut] + bias
            middle_ref[cut] = middle
            hat, _ = norm_parts(middle)
            normed_ref[cut] = (hat * gain + shift).astype(BF16)

    tile = pl.BlockSpec((size, width), lambda t: (t, 0))
    return pl.pallas_call(
        kernel,
        grid=(row_count,),
        in_specs=[
            tile, tile, pl.BlockSpec((1, 1, 1, size), lambda t: (0, t, 0, 0)), whole(KINDS, width),
            pl.BlockSpec((width, width), lambda t: (0, 3)),
        ],
        out_specs=[tile, tile],
        out_shape=[placed(BF16, tokens, width), placed(F32, tokens, width)],
        compiler_params=parameters(),
        cost_estimate=cost(2 * tokens * width * width, 10 * tokens * width),
        name="open_branch",
    )(mixed, rows_all, flags, vectors, weights)


def branch(places, normed, normed_other, pulled, pulled_other, vectors, rest):
    tokens, width = normed.shape
    groups = rest.shape[1] // 2
    cores, length = rest.shape[0], rest.shape[2]
    depth = length // 2
    both = 2 * tokens
    size = both

    def kernel(
        places_ref, n_ref, no_ref, c_ref, co_ref, vec_ref, down_ref, up_ref,
        total_ref, dn_ref, away_ref, sdown_ref, kdown_ref, gup_ref, gbias_ref,
        normed_all, turned, pulled_all, totals, d_normed, activated, d_hidden, up, down,
    ):
        step = pl.program_id(0)

        @pl.when(step == 0)
        def _():
            normed_all[:tokens] = n_ref[...]
            normed_all[tokens:] = no_ref[...]
            turned[:, :tokens] = n_ref[...].T
            turned[:, tokens:] = no_ref[...].T
            pulled_all[:tokens] = c_ref[...]
            pulled_all[tokens:] = co_ref[...]

        at = 0
        for x in range(2):
            for core in range(cores):
                up[at : at + depth] = up_ref[core, 0, x * depth : (x + 1) * depth]
                down[at : at + depth] = down_ref[core, 0, x * depth : (x + 1) * depth]
                at += depth
        bias = vec_ref[pl.ds(UBIAS + groups * places_ref[0] + step, 1), :]
        bias_grad = 0.0
        for c in range(0, both, size):
            cut = slice(c, c + size)
            hidden = dot(normed_all[cut], up[...], 1, 0) + bias
            d_active = dot(pulled_all[cut], down[...], 1, 1)
            phi = 0.5 * (1.0 + lax.erf(hidden * HALF_ROOT))
            slope = phi + hidden * (0.3989422804014327 * jnp.exp(-0.5 * hidden * hidden))
            activated[cut] = (hidden * phi).astype(BF16)
            grad = (d_active * slope).astype(BF16)
            d_hidden[cut] = grad
            bias_grad += jnp.sum(grad.astype(F32), axis=0, keepdims=True)
        gbias_ref[0] = bias_grad
        for c in range(0, both, size):
            cut = slice(c, c + size)
            more = dot(activated[cut], down[...], 1, 0)
            more_back = dot(d_hidden[cut], up[...], 1, 1)

            @pl.when(step == 0)
            def _(cut=cut, more=more, more_back=more_back):
                totals[cut] = more
                d_normed[cut] = more_back

            @pl.when(step > 0)
            def _(cut=cut, more=more, more_back=more_back):
                totals[cut] += more
                d_normed[cut] += more_back

        gup_ref[0] = dot(turned[...], d_hidden[...], 1, 0).astype(BF16)
        grads = dot(activated[...], pulled_all[...], 0, 0).astype(BF16)
        (sent,), (kept,) = parted(grads, places_ref[1], length)
        for core in range(cores):
            sdown_ref[0, core] = sent[core * depth : (core + 1) * depth]
            kdown_ref[0, core] = kept[core * depth : (core + 1) * depth]

        @pl.when(step == pl.num_programs(0) - 1)
        def _():
            total_ref[...] = totals[:tokens]
            dn_ref[...] = d_normed[:tokens]
            away_ref[0] = totals[tokens:].astype(BF16)
            away_ref[1] = d_normed[tokens:].astype(BF16)

    weight = lambda f: pl.BlockSpec((cores, 1, length, width), lambda k, _: (0, f(k), 0, 0))
    piece = pl.BlockSpec((1, cores, depth, width), lambda k, _: (k, 0, 0, 0))
    square = pl.BlockSpec((1, width, width), lambda k, _: (k, 0, 0))
    patch = whole(tokens, width)
    return pl.pallas_call(
        kernel,
        grid_spec=pltpu.PrefetchScalarGridSpec(
            num_scalar_prefetch=1,
            grid=(groups,),
            in_specs=[
                patch, patch, patch, patch, whole(KINDS, width), weight(lambda k: k),
                weight(lambda k: groups + k),
            ],
            out_specs=[
                patch, patch, whole(2, tokens, width), piece, piece, square,
                pl.BlockSpec((1, 1, width), lambda k, _: (k, 0, 0)),
            ],
            scratch_shapes=[
                pltpu.VMEM((both, width), BF16),
                pltpu.VMEM((width, both), BF16),
                pltpu.VMEM((both, width), BF16),
                pltpu.VMEM((both, width), F32),
                pltpu.VMEM((both, width), F32),
                pltpu.VMEM((both, width), BF16),
                pltpu.VMEM((both, width), BF16),
                pltpu.VMEM((width, width), BF16),
                pltpu.VMEM((width, width), BF16),
            ],
        ),
        out_shape=[
            placed(F32, tokens, width),
            placed(F32, tokens, width),
            placed(BF16, 2, tokens, width),
            placed(BF16, groups, cores, depth, width),
            placed(BF16, groups, cores, depth, width),
            placed(BF16, groups, width, width),
            shaped(F32, groups, 1, width),
        ],
        compiler_params=parameters(52),
        cost_estimate=cost(
            12 * groups * both * width * width, 20 * width * width, 2 * both * width * groups
        ),
        name="branch",
    )(places, normed, normed_other, pulled, pulled_other, vectors, rest, rest)


def between(near, d_normed, d_normed_other, middle, pulled, vectors, mixed, weights, halves):
    tokens, width = mixed.shape
    depth = width // (2 * halves)
    size = tokens // 2

    def kernel(
        near_ref, dn_ref, more_ref, middle_ref, cot_ref, vec_ref, mixed_ref, w_ref,
        dmiddle_ref, dmixed_ref, sent_ref, kept_ref, sums_ref, d_attn, grads,
    ):
        step = pl.program_id(0)
        gain = vec_ref[GAIN2 : GAIN2 + 1]
        sums = 0.0
        for c in range(0, size, CHUNK):
            cut = slice(c, c + CHUNK)
            d_out = dn_ref[cut] + more_ref[0, cut].astype(F32)
            cot = cot_ref[cut].astype(F32)
            hat, rate = norm_parts(middle_ref[cut])
            d_middle = cot + norm_back(d_out * gain, hat, rate)
            dmiddle_ref[cut] = d_middle
            low = d_middle.astype(BF16)
            d_attn[cut] = low
            parts = [low.astype(F32), d_out * hat, d_out, cot]
            sums += jnp.concatenate([jnp.sum(s, axis=0, keepdims=True) for s in parts], axis=0)
        sums = jnp.concatenate([sums, jnp.zeros_like(sums)], axis=0)
        dmixed_ref[...] = dot(d_attn[...], w_ref[...], 1, 1).astype(BF16)
        more = dot(mixed_ref[...], d_attn[...], 0, 0)

        @pl.when(step == 0)
        def _():
            sums_ref[...] = sums
            grads[...] = more

        @pl.when(step == 1)
        def _():
            sums_ref[...] += sums
            value = (grads[...] + more).astype(BF16)
            for x, (sent, kept) in enumerate(zip(*parted(value, near_ref[0], depth), strict=True)):
                sent_ref[x] = sent
                kept_ref[x] = kept

    tile = pl.BlockSpec((size, width), lambda t, _: (t, 0))
    piece = whole(halves, depth, width)
    return pl.pallas_call(
        kernel,
        grid_spec=pltpu.PrefetchScalarGridSpec(
            num_scalar_prefetch=1,
            grid=(2,),
            in_specs=[
                tile, pl.BlockSpec((1, size, width), lambda t, _: (1, t, 0)), tile, tile,
                whole(KINDS, width), tile, pl.BlockSpec((width, width), lambda t, _: (0, 3)),
            ],
            out_specs=[tile, tile, piece, piece, whole(8, width)],
            scratch_shapes=[pltpu.VMEM((size, width), BF16), pltpu.VMEM((width, width), F32)],
        ),
        out_shape=[
            placed(F32, tokens, width),
            shaped(BF16, tokens, width),
            placed(BF16, halves, depth, width),
            placed(BF16, halves, depth, width),
            shaped(F32, 8, width),
        ],
        compiler_params=parameters(),
        cost_estimate=cost(4 * tokens * width * width, 16 * tokens * width),
        name="between",
    )(near, d_normed, d_normed_other, middle, pulled, vectors, mixed, far(weights))


def weight_grads(near, turned, d_key, d_value, d_query, halves, after):
    width, total = turned.shape
    own = d_query.shape[0]
    depth = width // (2 * halves)

    def kernel(near_ref, turned_ref, dk_ref, dv_ref, dq_ref, *refs):
        sa_ref, ka_ref, sb_ref, kb_ref = refs[len(after) :]
        step = pl.program_id(0)

        def put(value, sent_ref, kept_ref, at):
            pieces = zip(*parted(value.astype(BF16), near_ref[0], depth), strict=True)
            for x, (sent, kept) in enumerate(pieces):
                sent_ref[x, :, at : at + width] = sent
                kept_ref[x, :, at : at + width] = kept

        @pl.when(step == 0)
        def _():
            put(dot(turned_ref[:, :own], dq_ref[...], 1, 0), sa_ref, ka_ref, 0)

        @pl.when(step == 1)
        def _():
            put(dot(turned_ref[...], dk_ref[...], 1, 0), sa_ref, ka_ref, width)

        @pl.when(step == 2)
        def _():
            put(dot(turned_ref[...], dv_ref[...], 1, 0), sb_ref, kb_ref, 0)

    pair, single = whole(halves, depth, 2 * width), whole(halves, depth, width)
    return pl.pallas_call(
        kernel,
        grid_spec=pltpu.PrefetchScalarGridSpec(
            num_scalar_prefetch=1,
            grid=(3,),
            in_specs=[
                whole(width, total), whole(total, width), whole(total, width), whole(own, width),
                *[ANYWHERE] * len(after),
            ],
            out_specs=[pair, pair, single, single],
        ),
        out_shape=[
            placed(BF16, halves, depth, 2 * width),
            placed(BF16, halves, depth, 2 * width),
            placed(BF16, halves, depth, width),
            placed(BF16, halves, depth, width),
        ],
        compiler_params=parameters(36),
        cost_estimate=cost(5 * total * width * width, 8 * total * width + 12 * width * width),
        name="weight_grads",
    )(near, turned, d_key, d_value, d_query, *after)


def first_norm(
    near, d_key, d_value, d_query, rows_all, flags, vectors, weights, d_middle, sums, gbias, qsum, vsum, halves, after,
):
    total, width = rows_all.shape
    blocks, row_count, _, size = flags.shape
    own = d_query.shape[0]
    depth = width // (2 * halves)
    groups = gbias.shape[0]

    def kernel(near_ref, *refs):
        (
            dk_ref, dv_ref, dq_ref, rows_ref, flags_ref, vec_ref, w_ref, dmiddle_ref, sums_ref,
            gbias_ref, qsum_ref, vsum_ref,
        ) = refs[:12]
        far_ref, near_share_ref, own_ref, sent_ref, kept_ref, totals = refs[12 + len(after) :]
        step = pl.program_id(0)

        def put_share(step, cut, value):
            @pl.when(step < blocks // 2)
            def _():
                far_ref[0, cut] = value

            @pl.when(step >= blocks // 2)
            def _():
                near_share_ref[0, cut] = value

        def one(mine):
            d_all = dot(dk_ref[...], w_ref[:, width : 2 * width], 1, 1)
            d_all += dot(dv_ref[...], w_ref[:, 2 * width :], 1, 1)
            if mine:
                d_all += dot(dq_ref[...], w_ref[:, :width], 1, 1)
            gain, embed = vec_ref[GAIN1 : GAIN1 + 1], vec_ref[EMBED : EMBED + 1]
            more = 0.0
            for r in range(row_count):
                cut = slice(r * size, (r + 1) * size)
                masked = column(flags_ref[0, r]) >= MASKED
                d_normed = d_all[cut]
                hat, rate = norm_parts(jnp.where(masked, embed, rows_ref[cut].astype(F32)))
                d_embedded = norm_back(d_normed * gain, hat, rate)
                if mine:
                    d_embedded = d_embedded + dmiddle_ref[cut]
                    own_ref[cut] = d_embedded
                else:
                    put_share(step, cut, d_embedded.astype(BF16))
                parts = [jnp.where(masked, d_embedded, 0.0), d_normed * hat, d_normed]
                more += jnp.concatenate([jnp.sum(s, axis=0, keepdims=True) for s in parts], axis=0)
            return more

        @pl.when(step == 0)
        def _():
            totals[:3] = one(True)

        @pl.when(step > 0)
        def _():
            totals[:3] += one(False)

        @pl.when(step == blocks - 1)
        def _():
            def line(ref):
                rows, pairs = ref.shape[0], ref.shape[1]
                return sum(
                    jnp.concatenate([ref[r, p] for p in range(pairs)], axis=1) for r in range(rows)
                )

            bias = jnp.concatenate([gbias_ref[k] for k in range(groups)], axis=0)
            none = jnp.zeros_like(bias)
            low = near_ref[0] == 0
            kinds = [
                totals[:3], line(qsum_ref), line(vsum_ref), sums_ref[:4],
                jnp.where(low, bias, none), jnp.where(low, none, bias),
            ]
            kinds.append(jnp.zeros((LANES - UBIAS - 2 * groups, width), F32))
            small = jnp.concatenate(kinds, axis=0).T.astype(BF16)
            for x, (sent, kept) in enumerate(zip(*parted(small, near_ref[0], depth), strict=True)):
                sent_ref[x] = sent
                kept_ref[x] = kept

    tile = pl.BlockSpec((own, width), lambda t, _: (t, 0))
    piece = whole(halves, depth, LANES)
    return pl.pallas_call(
        kernel,
        grid_spec=pltpu.PrefetchScalarGridSpec(
            num_scalar_prefetch=1,
            grid=(blocks,),
            in_specs=[
                tile, tile, whole(own, width), tile,
                pl.BlockSpec((1, row_count, 1, size), lambda t, _: (t, 0, 0, 0)),
                whole(KINDS, width), whole(width, 3 * width), whole(own, width),
                whole(*sums.shape), whole(*gbias.shape), whole(*qsum.shape), whole(*vsum.shape),
                *[ANYWHERE] * len(after),
            ],
            out_specs=[
                pl.BlockSpec((1, own, width), lambda t, _: (jnp.clip(t - 1, 0, blocks // 2 - 2), 0, 0)),
                pl.BlockSpec((1, own, width), lambda t, _: (jnp.maximum(t - blocks // 2, 0), 0, 0)),
                whole(own, width), piece, piece,
            ],
            scratch_shapes=[pltpu.VMEM((8, width), F32)],
        ),
        out_shape=[
            placed(BF16, blocks // 2 - 1, own, width),
            placed(BF16, blocks // 2, own, width),
            placed(F32, own, width),
            shaped(BF16, halves, depth, LANES),
            shaped(BF16, halves, depth, LANES),
        ],
        compiler_params=parameters(36),
        cost_estimate=cost(5 * total * width * width, 8 * total * width + 12 * width * width, total),
        name="first_norm",
    )(near, far(d_key), far(d_value), d_query, rows_all, flags, vectors, weights, d_middle, sums, gbias, qsum, vsum, *after)


def after(value, *others):
    return lax.optimization_barrier((value, *others))[0]


class Links:
    def __init__(self, seq, rows):
        self.sizes = {"seq": seq, "rows": rows}
        order = []
        for axis in EVERY:
            mask = self.sizes[axis] // 2
            while mask:
                order.append((axis, mask))
                mask //= 2
        self.order = order
        place = {axis: lax.axis_index(axis) for axis in EVERY}
        self.value = {(a, m): ((place[a] // m) % 2).astype(jnp.int32) for a, m in order}
        self.near = ("seq", 1)
        self.first = ("seq", 2)
        self.second = ("rows", 1)
        self.others = [b for b in order if b[0] == "rows" and b[1] > 1]

    def swap(self, array, bit):
        axis, mask = bit
        return lax.ppermute(array, axis, [(i, i ^ mask) for i in range(self.sizes[axis])])

    def pick(self, array, bit, other=False, axis=0):
        at = 1 - self.value[bit] if other else self.value[bit]
        return lax.dynamic_index_in_dim(array, at, axis, keepdims=False)

    def gather(self, shard, bits, wanted):
        held, have = shard, []
        for i, bit in enumerate(bits):
            if i in wanted:
                held = after(held, *wanted[i])
            have = sorted([*have, bit], key=self.order.index)
            parts = held.reshape(2 ** have.index(bit), -1, held.shape[-1])
            other = self.swap(held, bit).reshape(parts.shape)
            upper = self.value[bit] == 1
            low = jnp.where(upper, other, parts)
            high = jnp.where(upper, parts, other)
            held = jnp.stack([low, high], axis=1).reshape(-1, held.shape[-1])
        return held

    def half(self, held, have, bit, other):
        before = 1
        for key in have[: have.index(bit)]:
            before *= key if isinstance(key, int) else 2
        parts = held.reshape(before, 2, -1, held.shape[-1])
        return self.pick(parts, bit, other, 1).reshape(-1, held.shape[-1])

    def add(self, kept, came, have, bit):
        def part(other):
            first, second = (self.half(a, have, bit, other) for a in (kept, came))
            return (first.astype(F32) + second.astype(F32)).astype(BF16)

        return part(True), part(False), [b for b in have if b != bit]


def body(
    patches, segments, masked, mask_embedding, norm1_gain, norm1_bias, qkv_weight, query_bias,
    value_bias, out_weight, out_bias, norm2_gain, norm2_bias, up_weight, up_bias, down_weight,
    down_bias, cotangent, *, seq, rows,
):
    links = Links(seq, rows)
    row_count, patch_count, width = patches.shape
    tokens = row_count * patch_count
    n = qkv_weight.shape[0]
    devices = seq * rows
    groups = up_weight.shape[1] // width
    mine = groups // 2
    half = width // 2
    halves = seq // 2
    depth = rows * n
    near, first, second, others = links.near, links.first, links.second, links.others
    near_place = links.value[near].reshape(1)

    packed = jnp.stack(
        [
            down_weight.reshape(2, mine, n, width),
            up_weight.reshape(n, devices, groups, n).transpose(2, 0, 1, 3).reshape(2, mine, n, width),
        ],
        axis=1,
    ).reshape(2, 2 * mine, n, width)
    packed_kept, packed_sent = links.pick(packed, near), links.pick(packed, near, True)
    packed_came = links.swap(packed_sent, near)

    flags = (segments + MASKED * masked).astype(BF16).reshape(1, row_count, patch_count)
    sources = [after(patches.reshape(tokens, width), packed_sent)]
    for bit in (first, near):
        flags = jnp.concatenate([flags, links.swap(flags, bit)], axis=0)
        sources += [links.swap(source, bit) for source in sources]
    early_ones, late_ones = [sources[1], flags], sources[2:]
    flags = flags.astype(F32).reshape(seq, row_count, 1, patch_count)
    small = [
        mask_embedding, norm1_gain, norm1_bias, query_bias, value_bias, out_bias, norm2_gain,
        norm2_bias, down_bias,
    ]
    columns = jnp.concatenate([jnp.stack(small), up_bias.reshape(groups, n)], axis=0).T
    columns = jnp.pad(columns, ((0, 0), (0, LANES - columns.shape[1])))
    fourths = [qkv_weight[:, i * half : (i + 1) * half] for i in range(6)]
    fourths += [out_weight[:, :half], out_weight[:, half:]]
    left = jnp.concatenate(fourths[::2], axis=1)
    right = jnp.concatenate([*fourths[1::2], columns], axis=1)
    left = links.gather(left, [*others, second, first], {2: early_ones, 3: late_ones}).reshape(halves, depth, -1)
    right = links.gather(right, [*others, first, second], {}).reshape(halves, depth, -1)
    left_other, right_other = links.swap(left, near), links.swap(right, near)

    low = links.value[near] == 0
    packed = jnp.stack([jnp.where(low, packed_kept, packed_came), jnp.where(low, packed_came, packed_kept)], axis=0)
    same_core = [
        [(x * 2 + core) * rows + r for x in range(halves) for r in range(rows)] for core in range(2)
    ]
    rest = lax.all_gather(packed, EVERY, axis=2, tiled=True, axis_index_groups=same_core)

    rows_all, turned, queries, key_values, weights, vectors = project(
        near_place, sources, flags, left, left_other, right, right_other
    )
    queries = queries.reshape(row_count, patch_count, width)
    key_values = key_values.reshape(seq, row_count, patch_count, 2 * width)
    mixed, mixed_full, lse = attend(queries, key_values, flags)
    mixed = mixed.reshape(tokens, width)
    d_branch = cotangent.reshape(tokens, width)
    d_branch_other = links.swap(d_branch, near)
    normed_two, middle = open_branch(mixed, rows_all, flags, vectors, weights)
    places = jnp.stack([links.value[near], links.value[first]])
    added, d_normed, away, down_sent, down_kept, grad_up, grad_up_bias = branch(
        places, normed_two, links.swap(normed_two, near), d_branch, d_branch_other, vectors, rest
    )

    row_bits = [*others, second]
    have = [first, *row_bits]
    flat = lambda held: held.reshape(-1, held.shape[-1])
    down_sent, down_kept = flat(down_sent), flat(down_kept)
    up_order = [mine, first, near, *row_bits]
    grad_up = flat(grad_up)
    up_sent = links.half(grad_up, up_order, second, True)
    up_kept = links.half(grad_up, up_order, second, False)
    up_order = [mine, first, near, *others]
    away = links.swap(away, near)
    down_came, up_came = links.swap(down_sent, first), links.swap(up_sent, second)
    d_middle, d_mixed, out_sent, out_kept, sums = between(
        near_place, d_normed, away, middle, d_branch, vectors, mixed, weights, halves
    )
    out_came = links.swap(out_sent, near)
    d_mixed = d_mixed.reshape(row_count, patch_count, width)

    given = (queries, key_values, d_mixed, mixed_full, lse, flags)
    grads = None
    for row in range(row_count):
        grads = list(attend_back(row, grads, *given, [down_sent, up_sent] if row == 0 else []))
    d_query, d_key, d_value, query_sums, value_sums = grads

    down_sent, down_kept, down_order = links.add(
        after(down_kept, d_query), down_came, [mine, near, *row_bits], second
    )
    down_came = links.swap(down_sent, second)
    up_sent, up_kept, up_order = links.add(after(up_kept, down_sent), up_came, up_order, first)
    up_came = links.swap(up_sent, first)
    d_query = d_query.reshape(tokens, width)
    d_key = d_key.reshape(-1, width)
    d_value = d_value.reshape(-1, width)
    pair_sent, pair_kept, value_sent, value_kept = weight_grads(
        near_place, turned, d_key, d_value, d_query, halves, [down_sent, up_sent]
    )
    early_kept = jnp.concatenate([after(down_kept, pair_sent), up_kept], axis=0)
    early_came = jnp.concatenate([after(down_came, pair_sent), up_came], axis=0)
    early_order = [2 * mine, near, *others]
    early_sent, early_kept, early_order = links.add(early_kept, early_came, early_order, others[-1])
    early = [early_kept, links.swap(early_sent, others[-1]), early_order]
    pair_came = links.swap(flat(after(pair_sent, early_sent)), near)
    value_came = links.swap(flat(after(value_sent, early_sent)), near)
    pair_sent, pair_kept, pair_order = links.add(flat(pair_kept), pair_came, have, second)
    pair_came = links.swap(pair_sent, second)
    last_kept = jnp.concatenate([flat(value_kept), flat(out_kept)], axis=1)
    last_came = jnp.concatenate([value_came, flat(out_came)], axis=1)
    last_sent, last_kept, last_order = links.add(after(last_kept, pair_sent), last_came, have, first)
    last_came = links.swap(last_sent, first)
    far_share, near_share, own, small_sent, small_kept = first_norm(
        near_place, d_key, d_value, d_query, rows_all, flags, vectors, weights, d_middle, sums,
        grad_up_bias, query_sums, value_sums, halves, [early_sent, pair_sent, last_sent],
    )

    pair = [pair_kept, pair_came, pair_order]
    last = [last_kept, last_came, last_order]

    def go(item, bit, gone):
        gone, item[0], item[2] = links.add(after(item[0], gone), item[1], item[2], bit)
        item[1] = links.swap(gone, bit)
        return gone

    rest_bits = others[-2::-1]
    gone = own
    for bit in rest_bits:
        gone = go(early, bit, gone)
    gone = go(pair, first, gone)
    gone = go(last, second, gone)
    near_share = links.swap(after(near_share, gone), near)
    small = [flat(small_kept), links.swap(flat(after(small_sent, gone)), near), have]
    gone = go(small, first, gone)
    gone = (after(far_share, gone).astype(F32) + near_share[1:].astype(F32)).astype(BF16)
    far_share = links.swap(gone, first)
    gone = go(small, second, gone)
    gone = go(pair, others[-1], gone)
    output = after(middle, gone) + added + away[0].astype(F32) + vectors[DBIAS]
    output = output.astype(BF16)
    last[0] = jnp.concatenate([after(last[0], output), small[0]], axis=1)
    last[1] = jnp.concatenate([last[1], small[1]], axis=1)
    gone = go(last, others[-1], gone)
    low = links.value[near] == 0
    for i, bit in enumerate(rest_bits):
        gone = go(pair, bit, gone)
        if i == len(rest_bits) - 1:
            early_sum = after(early[0], gone).astype(F32) + early[1].astype(F32)
            early_sum = early_sum.reshape(2 * mine, 2, n, width)
            far_sum = links.pick(early_sum, near, True, 1).astype(BF16)
            far_sum = links.swap(far_sum, near).astype(F32)
            early_sum = links.pick(early_sum, near, False, 1)
            joined = jnp.stack(
                [jnp.where(low, early_sum, far_sum), jnp.where(low, far_sum, early_sum)], axis=0
            )
            down_sum = joined[:, :mine].reshape(-1, width)
            up_sum = joined[:, mine:].reshape(groups, n, devices, n)
            up_sum = up_sum.transpose(1, 2, 0, 3).reshape(n, -1)
            gone = up_sum
        gone = go(last, bit, gone)
    pair, last = (a.astype(F32) + b.astype(F32) for a, b, _ in (pair, last))
    input_grad = after(own, up_sum, gone) + near_share[0].astype(F32) + far_share[0].astype(F32)
    is_masked = masked.reshape(tokens, 1) == 1
    input_grad = jnp.where(is_masked, 0.0, input_grad)
    project_sum = jnp.concatenate([pair, last[:, :width]], axis=1)
    out_sum = last[:, width : 2 * width]
    tail = last[:, 2 * width :].T
    shape = (row_count, patch_count, width)
    return (
        output.reshape(shape), input_grad.reshape(shape), tail[EMBED], tail[GAIN1], tail[SHIFT1],
        project_sum, tail[QBIAS], tail[VBIAS], out_sum, tail[OBIAS], tail[GAIN2], tail[SHIFT2],
        up_sum, tail[UBIAS : UBIAS + groups].reshape(-1), down_sum, tail[DBIAS],
    )


def solution(mesh):
    one, two = P(EVERY), P(EVERY, None)
    rows, flags = P("rows", "seq", None), P("rows", "seq")
    seq, row_groups = mesh.shape["seq"], mesh.shape["rows"]

    def run(*arguments):
        return body(*arguments, seq=seq, rows=row_groups)

    return jax.shard_map(
        run,
        mesh=mesh,
        in_specs=(
            rows, flags, flags, one, one, one, two, one, one, two, one, one, one, two, one, two,
            one, rows,
        ),
        out_specs=(
            rows, rows, one, one, one, two, one, one, two, one, one, one, two, one, two, one,
        ),
        check_vma=False,
    )
```

```python
import jax
import jax.numpy as jnp
from jax import lax
from jax.experimental import pallas as pl
from jax.experimental.pallas import tpu as pltpu
from jax.sharding import PartitionSpec as P

HEAD_SIZE = 64
LANES = 128
CHUNK = 256
PAIRS = 6
MASKED = 16
EPSILON = 1e-06
FLOOR_SCORE = -1e30
HALF_ROOT = 0.7071067811865476
MIB = 2**20
EVERY = ("seq", "rows")
BF16 = jnp.bfloat16
F32 = jnp.float32
EMBED, GAIN1, SHIFT1, QBIAS, VBIAS, OBIAS, GAIN2, SHIFT2, DBIAS, UBIAS = range(10)
KINDS = 16


def dot(left, right, left_dim, right_dim):
    return lax.dot_general(
        left, right, (((left_dim,), (right_dim,)), ((), ())), preferred_element_type=F32
    )


def column(row):
    return jnp.broadcast_to(row, (8, row.shape[1])).T[:, :1]


def segment_of(flags):
    return flags - jnp.where(flags >= MASKED, float(MASKED), 0.0)


def norm_parts(values):
    mean = jnp.mean(values, axis=-1, keepdims=True)
    centered = values - mean
    rate = lax.rsqrt(jnp.mean(centered * centered, axis=-1, keepdims=True) + EPSILON)
    return centered * rate, rate


def norm_back(pulled, hat, rate):
    first = jnp.mean(pulled, axis=-1, keepdims=True)
    second = jnp.mean(pulled * hat, axis=-1, keepdims=True)
    return rate * (pulled - first - hat * second)


def parted(value, mine, depth):
    sent, kept = [], []
    for x in range(value.shape[0] // (2 * depth)):
        low = value[2 * x * depth : (2 * x + 1) * depth]
        high = value[(2 * x + 1) * depth : (2 * x + 2) * depth]
        sent.append(jnp.where(mine == 0, high, low))
        kept.append(jnp.where(mine == 0, low, high))
    return sent, kept


def whole(*shape):
    return pl.BlockSpec(shape, lambda *_: (0,) * len(shape))


ANYWHERE = pl.BlockSpec(memory_space=pl.ANY)


def shaped(dtype, *shape):
    return jax.ShapeDtypeStruct(shape, dtype)


def placed(dtype, *shape):
    return pltpu.HBM(shape, dtype)


def far(array):
    return pltpu.with_memory_space_constraint(array, pltpu.HBM)


def parameters(mib=32):
    return pltpu.CompilerParams(vmem_limit_bytes=mib * MIB)


def cost(flops, nbytes, transcendentals=0):
    return pl.CostEstimate(flops=flops, bytes_accessed=nbytes, transcendentals=transcendentals)


def split_heads(pair):
    lane = lax.broadcasted_iota(jnp.int32, pair.shape, 1)
    zero = jnp.zeros_like(pair)
    return jnp.concatenate(
        [jnp.where(lane < HEAD_SIZE, pair, zero), jnp.where(lane < HEAD_SIZE, zero, pair)], axis=0
    )


def join_heads(both, count):
    row = lax.broadcasted_iota(jnp.int32, (both.shape[0], count), 0)
    return jnp.where(row < HEAD_SIZE, both[:, :count], both[:, count:]).T


def set_bias(flags_ref, bias):
    blocks, size = flags_ref.shape[0], flags_ref.shape[3]
    asked = segment_of(flags_ref[0, 0])
    for j in range(blocks):
        keys = column(segment_of(flags_ref[j, 0]))
        bias[pl.ds(j * size, size), :] = jnp.where((keys == asked) & (keys > 0.0), 0.0, FLOOR_SCORE)


def attend_kernel(q_ref, k_ref, v_ref, flags_ref, mix_ref, full_ref, lse_ref, bias, held):
    count, blocks, size = q_ref.shape[1], k_ref.shape[0], k_ref.shape[2]

    @pl.when(pl.program_id(1) == 0)
    def _():
        set_bias(flags_ref, bias)

    live = segment_of(flags_ref[0, 0]) > 0.0
    live = jnp.concatenate([live, live], axis=1)
    for u in range(PAIRS):
        lanes = slice(u * LANES, (u + 1) * LANES)
        asked = split_heads(q_ref[0, :, lanes])
        top = None
        for j in range(blocks):
            rows = pl.ds(j * size, size)
            part = bias[rows, :]
            scores = dot(k_ref[j, 0, :, lanes], asked, 1, 1) + jnp.concatenate([part, part], axis=1)
            held[u % 2, rows, :] = scores
            high = jnp.max(scores, axis=0, keepdims=True)
            top = high if top is None else jnp.maximum(top, high)
        total, mixed = 0.0, 0.0
        for j in range(blocks):
            weights = jnp.exp(held[u % 2, pl.ds(j * size, size), :] - top)
            total = total + jnp.sum(weights, axis=0, keepdims=True)
            mixed = mixed + dot(v_ref[j, 0, :, lanes].T, weights.astype(BF16), 1, 0)
        result = join_heads(mixed * jnp.where(live, 1.0 / total, 0.0), count)
        mix_ref[0, :, lanes] = result.astype(BF16)
        full_ref[0, :, lanes] = result
        lse_ref[0, u] = jnp.where(live, top + jnp.log(total), 0.0)


def attend_back_kernel(
    q_ref, k_ref, v_ref, dm_ref, full_ref, lse_ref, flags_ref,
    dq_ref, dk_ref, dv_ref, qsum_ref, vsum_ref, bias,
):
    count, blocks, size = q_ref.shape[1], k_ref.shape[0], k_ref.shape[2]

    set_bias(flags_ref, bias)
    for u in range(q_ref.shape[2] // LANES):
        lanes = slice(u * LANES, (u + 1) * LANES)
        d_mixed = dm_ref[0, :, lanes]
        asked, pulled = split_heads(q_ref[0, :, lanes]), split_heads(d_mixed)
        product = (d_mixed.astype(F32) * full_ref[0, :, lanes]).T
        delta = jnp.concatenate(
            [
                jnp.sum(product[:HEAD_SIZE], axis=0, keepdims=True),
                jnp.sum(product[HEAD_SIZE:], axis=0, keepdims=True),
            ],
            axis=1,
        )
        lse = lse_ref[0, u]
        d_query, v_sum = 0.0, 0.0
        for j in range(blocks):
            keys = k_ref[j, 0, :, lanes]
            part = bias[pl.ds(j * size, size), :]
            scores = dot(keys, asked, 1, 1) + jnp.concatenate([part, part], axis=1)
            probs = jnp.exp(scores - lse)
            d_probs = dot(v_ref[j, 0, :, lanes], pulled, 1, 1)
            d_scores = (probs * (d_probs - delta)).astype(BF16)
            d_value = dot(probs.astype(BF16), pulled, 1, 0)
            dv_ref[j, 0, :, lanes] = d_value.astype(BF16)
            dk_ref[j, 0, :, lanes] = dot(d_scores, asked, 1, 0).astype(BF16)
            v_sum = v_sum + jnp.sum(d_value, axis=0, keepdims=True)
            d_query = d_query + dot(keys.T, d_scores, 1, 0)
        d_query = join_heads(d_query, count) * HEAD_SIZE**-0.5
        dq_ref[0, :, lanes] = d_query.astype(BF16)
        qsum_ref[0, u] = jnp.sum(d_query, axis=0, keepdims=True)
        vsum_ref[0, u] = v_sum


def attend(queries, key_values, flags):
    rows, count, width = queries.shape
    blocks, _, size, _ = key_values.shape
    pairs = width // LANES
    tile = pl.BlockSpec((1, count, PAIRS * LANES), lambda r, p: (r, 0, p))
    steps = pairs // PAIRS
    area = rows * count * blocks * size
    return pl.pallas_call(
        attend_kernel,
        grid=(rows, steps),
        in_specs=[
            tile,
            pl.BlockSpec((blocks, 1, size, PAIRS * LANES), lambda r, p: (0, r, 0, p)),
            pl.BlockSpec((blocks, 1, size, PAIRS * LANES), lambda r, p: (0, r, 0, steps + p)),
            pl.BlockSpec((blocks, 1, 1, size), lambda r, p: (0, r, 0, 0)),
        ],
        out_specs=[tile, tile, pl.BlockSpec((1, PAIRS, 1, 2 * count), lambda r, p: (r, p, 0, 0))],
        out_shape=[
            shaped(BF16, *queries.shape),
            placed(F32, *queries.shape),
            shaped(F32, rows, pairs, 1, 2 * count),
        ],
        scratch_shapes=[
            pltpu.VMEM((blocks * size, count), F32),
            pltpu.VMEM((2, blocks * size, 2 * count), F32),
        ],
        compiler_params=parameters(),
        cost_estimate=cost(16 * area * width, 8 * rows * blocks * size * width, area * 12),
        name="attend",
    )(far(queries), far(key_values), far(key_values), flags)


def attend_back(queries, key_values, d_mixed, mixed_full, lse, flags, after):
    rows, count, width = queries.shape
    blocks, _, size, _ = key_values.shape
    pairs = width // LANES
    tile = pl.BlockSpec((1, count, width), lambda r: (r, 0, 0))
    keys = pl.BlockSpec((blocks, 1, size, width), lambda r: (0, r, 0, 0))
    line = lambda w: pl.BlockSpec((1, pairs, 1, w), lambda r: (r, 0, 0, 0))
    area = rows * count * blocks * size
    grads = placed(BF16, blocks, rows, size, width)
    sums = shaped(F32, rows, pairs, 1, LANES)
    given = [queries, key_values, key_values, d_mixed, mixed_full, lse, flags]

    def kernel(*refs):
        attend_back_kernel(*refs[: len(given)], *refs[len(given) + len(after) :])

    return pl.pallas_call(
        kernel,
        grid=(rows,),
        in_specs=[
            tile, keys, pl.BlockSpec((blocks, 1, size, width), lambda r: (0, r, 0, 1)), tile, tile,
            line(2 * count), pl.BlockSpec((blocks, 1, 1, size), lambda r: (0, r, 0, 0)),
            *[ANYWHERE] * len(after),
        ],
        out_specs=[tile, keys, keys, line(LANES), line(LANES)],
        out_shape=[placed(BF16, *queries.shape), grads, grads, sums, sums],
        scratch_shapes=[pltpu.VMEM((blocks * size, count), F32)],
        compiler_params=parameters(40),
        cost_estimate=cost(32 * area * width, 16 * rows * blocks * size * width, area * 12),
        name="attend_back",
    )(*given, *after)


def project(near, sources, flags, left, left_other, right, right_other):
    own, width = sources[0].shape
    blocks, row_count, _, size = flags.shape
    total, steps = own * blocks, blocks
    halves, depth, part = left.shape
    half = width // 2

    def kernel(near_ref, *refs):
        first_ref, ahead_ref, lm_ref, lo_ref, rm_ref, ro_ref = refs[blocks : blocks + 6]
        rows_out, turned_ref, q_ref, kv_ref, w_out, vec_ref = refs[blocks + 6 : blocks + 12]
        rows, weights, normed, columns, sems, out_sems = refs[blocks + 12 :]
        step = pl.program_id(0)
        outward = [
            pltpu.make_async_copy(rows, rows_out, out_sems.at[0]),
            pltpu.make_async_copy(weights, w_out, out_sems.at[1]),
        ]

        def norm(at, slot, flags_ref):
            gain, shift = vec_ref[GAIN1 : GAIN1 + 1], vec_ref[SHIFT1 : SHIFT1 + 1]
            embed = vec_ref[EMBED : EMBED + 1]
            for r in range(row_count):
                masked = column(flags_ref[0, r]) >= MASKED
                here = rows[pl.ds(pl.multiple_of(at * own + r * size, size), size), :].astype(F32)
                hat, _ = norm_parts(jnp.where(masked, embed, here))
                normed[slot, r * size : (r + 1) * size, :] = (hat * gain + shift).astype(BF16)

        @pl.when(step == 0)
        def _():
            near_place = near_ref[0]
            later, first = [], []
            for which in range(2):
                mine = near_place if which == 0 else 1 - near_place
                low, high = (lm_ref, rm_ref) if which == 0 else (lo_ref, ro_ref)
                for x in range(halves):
                    at = pl.ds(pl.multiple_of(x * 2 * depth + mine * depth, depth), depth)
                    first.append((high.at[x, :, pl.ds(part, LANES)], columns.at[at, :]))
                    for side, source in enumerate((low, high)):
                        for kind in range(4):
                            later.append(
                                (
                                    source.at[x, :, pl.ds(kind * half, half)],
                                    weights.at[at, pl.ds(kind * width + side * half, half)],
                                )
                            )
            first += [(refs[i], rows.at[pl.ds(i * own, own), :]) for i in range(blocks)]
            copies = [
                pltpu.make_async_copy(a, b, sems.at[i]) for i, (a, b) in enumerate([*first, *later])
            ]
            for copy in copies:
                copy.start()
            for copy in copies[: len(first)]:
                copy.wait()
            outward[0].start()
            vec_ref[...] = columns[...].astype(F32).T[:KINDS]
            norm(0, 0, first_ref)
            for copy in copies[len(first) :]:
                copy.wait()
            outward[1].start()

        slot = lax.rem(step, 2)
        here = normed[slot]
        kv_ref[:, :width] = dot(here, weights[:, width : 2 * width], 1, 0).astype(BF16)
        values = dot(here, weights[:, 2 * width : 3 * width], 1, 0)
        kv_ref[:, width:] = (values + vec_ref[VBIAS : VBIAS + 1]).astype(BF16)
        turned_ref[...] = here.T
        norm(jnp.minimum(step + 1, steps - 1), 1 - slot, ahead_ref)

        @pl.when(step == 0)
        def _():
            asked = dot(here, weights[:, :width], 1, 0) + vec_ref[QBIAS : QBIAS + 1]
            q_ref[...] = (asked * HEAD_SIZE**-0.5).astype(BF16)

        @pl.when(step == steps - 1)
        def _():
            for copy in outward:
                copy.wait()

    def ahead(t, _):
        return (jnp.minimum(t + 1, steps - 1), 0, 0, 0)

    return pl.pallas_call(
        kernel,
        grid_spec=pltpu.PrefetchScalarGridSpec(
            num_scalar_prefetch=1,
            grid=(steps,),
            in_specs=[
                *[ANYWHERE] * blocks,
                whole(1, row_count, 1, size),
                pl.BlockSpec((1, row_count, 1, size), ahead),
                *[ANYWHERE] * 4,
            ],
            out_specs=[
                ANYWHERE,
                pl.BlockSpec((width, own), lambda t, _: (0, t)),
                whole(own, width),
                pl.BlockSpec((own, 2 * width), lambda t, _: (t, 0)),
                ANYWHERE,
                whole(KINDS, width),
            ],
            scratch_shapes=[
                pltpu.VMEM((total, width), BF16),
                pltpu.VMEM((width, 4 * width), BF16),
                pltpu.VMEM((2, own, width), BF16),
                pltpu.VMEM((width, LANES), BF16),
                pltpu.SemaphoreType.DMA((18 * halves + blocks,)),
                pltpu.SemaphoreType.DMA((2,)),
            ],
        ),
        out_shape=[
            placed(BF16, total, width),
            placed(BF16, width, total),
            placed(BF16, own, width),
            placed(BF16, total, 2 * width),
            placed(BF16, width, 4 * width),
            shaped(F32, KINDS, width),
        ],
        compiler_params=parameters(40),
        cost_estimate=cost(5 * total * width * width, 8 * total * width + 16 * width * width, total),
        name="project",
    )(near, *sources, flags, flags, left, left_other, right, right_other)


def open_branch(mixed, rows_all, flags, vectors, weights):
    tokens, width = mixed.shape
    _, row_count, _, size = flags.shape

    def kernel(mixed_ref, rows_ref, flags_ref, vec_ref, w_ref, normed_ref, middle_ref):
        masked = column(flags_ref[0, 0]) >= MASKED
        embed, bias = vec_ref[EMBED : EMBED + 1], vec_ref[OBIAS : OBIAS + 1]
        gain, shift = vec_ref[GAIN2 : GAIN2 + 1], vec_ref[SHIFT2 : SHIFT2 + 1]
        added = dot(mixed_ref[...], w_ref[...], 1, 0)
        for c in range(0, size, CHUNK):
            cut = slice(c, c + CHUNK)
            values = jnp.where(masked[cut], embed, rows_ref[cut].astype(F32))
            middle = values + added[cut] + bias
            middle_ref[cut] = middle
            hat, _ = norm_parts(middle)
            normed_ref[cut] = (hat * gain + shift).astype(BF16)

    tile = pl.BlockSpec((size, width), lambda t: (t, 0))
    return pl.pallas_call(
        kernel,
        grid=(row_count,),
        in_specs=[
            tile, tile, pl.BlockSpec((1, 1, 1, size), lambda t: (0, t, 0, 0)), whole(KINDS, width),
            pl.BlockSpec((width, width), lambda t: (0, 3)),
        ],
        out_specs=[tile, tile],
        out_shape=[placed(BF16, tokens, width), placed(F32, tokens, width)],
        compiler_params=parameters(),
        cost_estimate=cost(2 * tokens * width * width, 10 * tokens * width),
        name="open_branch",
    )(mixed, rows_all, flags, vectors, weights)


def branch(places, normed, normed_other, pulled, pulled_other, vectors, rest):
    tokens, width = normed.shape
    groups = rest.shape[1] // 2
    cores, length = rest.shape[0], rest.shape[2]
    depth = length // 2
    both = 2 * tokens
    size = both

    def kernel(
        places_ref, n_ref, no_ref, c_ref, co_ref, vec_ref, down_ref, up_ref,
        total_ref, dn_ref, away_ref, sdown_ref, kdown_ref, gup_ref, gbias_ref,
        normed_all, turned, pulled_all, totals, d_normed, activated, d_hidden, up, down,
    ):
        step = pl.program_id(0)

        @pl.when(step == 0)
        def _():
            normed_all[:tokens] = n_ref[...]
            normed_all[tokens:] = no_ref[...]
            turned[:, :tokens] = n_ref[...].T
            turned[:, tokens:] = no_ref[...].T
            pulled_all[:tokens] = c_ref[...]
            pulled_all[tokens:] = co_ref[...]

        at = 0
        for x in range(2):
            for core in range(cores):
                up[at : at + depth] = up_ref[core, 0, x * depth : (x + 1) * depth]
                down[at : at + depth] = down_ref[core, 0, x * depth : (x + 1) * depth]
                at += depth
        bias = vec_ref[pl.ds(UBIAS + groups * places_ref[0] + step, 1), :]
        bias_grad = 0.0
        for c in range(0, both, size):
            cut = slice(c, c + size)
            hidden = dot(normed_all[cut], up[...], 1, 0) + bias
            d_active = dot(pulled_all[cut], down[...], 1, 1)
            phi = 0.5 * (1.0 + lax.erf(hidden * HALF_ROOT))
            slope = phi + hidden * (0.3989422804014327 * jnp.exp(-0.5 * hidden * hidden))
            activated[cut] = (hidden * phi).astype(BF16)
            grad = (d_active * slope).astype(BF16)
            d_hidden[cut] = grad
            bias_grad += jnp.sum(grad.astype(F32), axis=0, keepdims=True)
        gbias_ref[0] = bias_grad
        for c in range(0, both, size):
            cut = slice(c, c + size)
            more = dot(activated[cut], down[...], 1, 0)
            more_back = dot(d_hidden[cut], up[...], 1, 1)

            @pl.when(step == 0)
            def _(cut=cut, more=more, more_back=more_back):
                totals[cut] = more
                d_normed[cut] = more_back

            @pl.when(step > 0)
            def _(cut=cut, more=more, more_back=more_back):
                totals[cut] += more
                d_normed[cut] += more_back

        gup_ref[0] = dot(turned[...], d_hidden[...], 1, 0).astype(BF16)
        grads = dot(activated[...], pulled_all[...], 0, 0).astype(BF16)
        (sent,), (kept,) = parted(grads, places_ref[1], length)
        for core in range(cores):
            sdown_ref[0, core] = sent[core * depth : (core + 1) * depth]
            kdown_ref[0, core] = kept[core * depth : (core + 1) * depth]

        @pl.when(step == pl.num_programs(0) - 1)
        def _():
            total_ref[...] = totals[:tokens]
            dn_ref[...] = d_normed[:tokens]
            away_ref[0] = totals[tokens:].astype(BF16)
            away_ref[1] = d_normed[tokens:].astype(BF16)

    weight = lambda f: pl.BlockSpec((cores, 1, length, width), lambda k, _: (0, f(k), 0, 0))
    piece = pl.BlockSpec((1, cores, depth, width), lambda k, _: (k, 0, 0, 0))
    square = pl.BlockSpec((1, width, width), lambda k, _: (k, 0, 0))
    patch = whole(tokens, width)
    return pl.pallas_call(
        kernel,
        grid_spec=pltpu.PrefetchScalarGridSpec(
            num_scalar_prefetch=1,
            grid=(groups,),
            in_specs=[
                patch, patch, patch, patch, whole(KINDS, width), weight(lambda k: k),
                weight(lambda k: groups + k),
            ],
            out_specs=[
                patch, patch, whole(2, tokens, width), piece, piece, square,
                pl.BlockSpec((1, 1, width), lambda k, _: (k, 0, 0)),
            ],
            scratch_shapes=[
                pltpu.VMEM((both, width), BF16),
                pltpu.VMEM((width, both), BF16),
                pltpu.VMEM((both, width), BF16),
                pltpu.VMEM((both, width), F32),
                pltpu.VMEM((both, width), F32),
                pltpu.VMEM((both, width), BF16),
                pltpu.VMEM((both, width), BF16),
                pltpu.VMEM((width, width), BF16),
                pltpu.VMEM((width, width), BF16),
            ],
        ),
        out_shape=[
            placed(F32, tokens, width),
            placed(F32, tokens, width),
            placed(BF16, 2, tokens, width),
            placed(BF16, groups, cores, depth, width),
            placed(BF16, groups, cores, depth, width),
            placed(BF16, groups, width, width),
            shaped(F32, groups, 1, width),
        ],
        compiler_params=parameters(52),
        cost_estimate=cost(
            12 * groups * both * width * width, 20 * width * width, 2 * both * width * groups
        ),
        name="branch",
    )(places, normed, normed_other, pulled, pulled_other, vectors, rest, rest)


def between(near, d_normed, d_normed_other, middle, pulled, vectors, mixed, weights, halves):
    tokens, width = mixed.shape
    depth = width // (2 * halves)
    size = tokens // 2

    def kernel(
        near_ref, dn_ref, more_ref, middle_ref, cot_ref, vec_ref, mixed_ref, w_ref,
        dmiddle_ref, dmixed_ref, sent_ref, kept_ref, sums_ref, d_attn, grads,
    ):
        step = pl.program_id(0)
        gain = vec_ref[GAIN2 : GAIN2 + 1]
        sums = 0.0
        for c in range(0, size, CHUNK):
            cut = slice(c, c + CHUNK)
            d_out = dn_ref[cut] + more_ref[0, cut].astype(F32)
            cot = cot_ref[cut].astype(F32)
            hat, rate = norm_parts(middle_ref[cut])
            d_middle = cot + norm_back(d_out * gain, hat, rate)
            dmiddle_ref[cut] = d_middle
            low = d_middle.astype(BF16)
            d_attn[cut] = low
            parts = [low.astype(F32), d_out * hat, d_out, cot]
            sums += jnp.concatenate([jnp.sum(s, axis=0, keepdims=True) for s in parts], axis=0)
        sums = jnp.concatenate([sums, jnp.zeros_like(sums)], axis=0)
        dmixed_ref[...] = dot(d_attn[...], w_ref[...], 1, 1).astype(BF16)
        more = dot(mixed_ref[...], d_attn[...], 0, 0)

        @pl.when(step == 0)
        def _():
            sums_ref[...] = sums
            grads[...] = more

        @pl.when(step == 1)
        def _():
            sums_ref[...] += sums
            value = (grads[...] + more).astype(BF16)
            for x, (sent, kept) in enumerate(zip(*parted(value, near_ref[0], depth), strict=True)):
                sent_ref[x] = sent
                kept_ref[x] = kept

    tile = pl.BlockSpec((size, width), lambda t, _: (t, 0))
    piece = whole(halves, depth, width)
    return pl.pallas_call(
        kernel,
        grid_spec=pltpu.PrefetchScalarGridSpec(
            num_scalar_prefetch=1,
            grid=(2,),
            in_specs=[
                tile, pl.BlockSpec((1, size, width), lambda t, _: (1, t, 0)), tile, tile,
                whole(KINDS, width), tile, pl.BlockSpec((width, width), lambda t, _: (0, 3)),
            ],
            out_specs=[tile, tile, piece, piece, whole(8, width)],
            scratch_shapes=[pltpu.VMEM((size, width), BF16), pltpu.VMEM((width, width), F32)],
        ),
        out_shape=[
            placed(F32, tokens, width),
            shaped(BF16, tokens, width),
            placed(BF16, halves, depth, width),
            placed(BF16, halves, depth, width),
            shaped(F32, 8, width),
        ],
        compiler_params=parameters(),
        cost_estimate=cost(4 * tokens * width * width, 16 * tokens * width),
        name="between",
    )(near, d_normed, d_normed_other, middle, pulled, vectors, mixed, far(weights))


def weight_grads(near, turned, d_key, d_value, d_query, halves, after):
    width, total = turned.shape
    own = d_query.shape[0]
    depth = width // (2 * halves)

    def kernel(near_ref, turned_ref, dk_ref, dv_ref, dq_ref, *refs):
        sa_ref, ka_ref, sb_ref, kb_ref = refs[len(after) :]
        step = pl.program_id(0)

        def put(value, sent_ref, kept_ref, at):
            pieces = zip(*parted(value.astype(BF16), near_ref[0], depth), strict=True)
            for x, (sent, kept) in enumerate(pieces):
                sent_ref[x, :, at : at + width] = sent
                kept_ref[x, :, at : at + width] = kept

        @pl.when(step == 0)
        def _():
            put(dot(turned_ref[:, :own], dq_ref[...], 1, 0), sa_ref, ka_ref, 0)

        @pl.when(step == 1)
        def _():
            put(dot(turned_ref[...], dk_ref[...], 1, 0), sa_ref, ka_ref, width)

        @pl.when(step == 2)
        def _():
            put(dot(turned_ref[...], dv_ref[...], 1, 0), sb_ref, kb_ref, 0)

    pair, single = whole(halves, depth, 2 * width), whole(halves, depth, width)
    return pl.pallas_call(
        kernel,
        grid_spec=pltpu.PrefetchScalarGridSpec(
            num_scalar_prefetch=1,
            grid=(3,),
            in_specs=[
                whole(width, total), whole(total, width), whole(total, width), whole(own, width),
                *[ANYWHERE] * len(after),
            ],
            out_specs=[pair, pair, single, single],
        ),
        out_shape=[
            placed(BF16, halves, depth, 2 * width),
            placed(BF16, halves, depth, 2 * width),
            placed(BF16, halves, depth, width),
            placed(BF16, halves, depth, width),
        ],
        compiler_params=parameters(36),
        cost_estimate=cost(5 * total * width * width, 8 * total * width + 12 * width * width),
        name="weight_grads",
    )(near, turned, d_key, d_value, d_query, *after)


def first_norm(
    near, d_key, d_value, d_query, rows_all, flags, vectors, weights, d_middle, sums, gbias, qsum, vsum, halves, after,
):
    total, width = rows_all.shape
    blocks, row_count, _, size = flags.shape
    own = d_query.shape[0]
    depth = width // (2 * halves)
    groups = gbias.shape[0]

    def kernel(near_ref, *refs):
        (
            dk_ref, dv_ref, dq_ref, rows_ref, flags_ref, vec_ref, w_ref, dmiddle_ref, sums_ref,
            gbias_ref, qsum_ref, vsum_ref,
        ) = refs[:12]
        far_ref, near_share_ref, own_ref, sent_ref, kept_ref, totals = refs[12 + len(after) :]
        step = pl.program_id(0)

        def put_share(step, cut, value):
            @pl.when(step < blocks // 2)
            def _():
                far_ref[0, cut] = value

            @pl.when(step >= blocks // 2)
            def _():
                near_share_ref[0, cut] = value

        def one(mine):
            d_all = dot(dk_ref[...], w_ref[:, width : 2 * width], 1, 1)
            d_all += dot(dv_ref[...], w_ref[:, 2 * width :], 1, 1)
            if mine:
                d_all += dot(dq_ref[...], w_ref[:, :width], 1, 1)
            gain, embed = vec_ref[GAIN1 : GAIN1 + 1], vec_ref[EMBED : EMBED + 1]
            more = 0.0
            for r in range(row_count):
                cut = slice(r * size, (r + 1) * size)
                masked = column(flags_ref[0, r]) >= MASKED
                d_normed = d_all[cut]
                hat, rate = norm_parts(jnp.where(masked, embed, rows_ref[cut].astype(F32)))
                d_embedded = norm_back(d_normed * gain, hat, rate)
                if mine:
                    d_embedded = d_embedded + dmiddle_ref[cut]
                    own_ref[cut] = d_embedded
                else:
                    put_share(step, cut, d_embedded.astype(BF16))
                parts = [jnp.where(masked, d_embedded, 0.0), d_normed * hat, d_normed]
                more += jnp.concatenate([jnp.sum(s, axis=0, keepdims=True) for s in parts], axis=0)
            return more

        @pl.when(step == 0)
        def _():
            totals[:3] = one(True)

        @pl.when(step > 0)
        def _():
            totals[:3] += one(False)

        @pl.when(step == blocks - 1)
        def _():
            def line(ref):
                rows, pairs = ref.shape[0], ref.shape[1]
                return sum(
                    jnp.concatenate([ref[r, p] for p in range(pairs)], axis=1) for r in range(rows)
                )

            bias = jnp.concatenate([gbias_ref[k] for k in range(groups)], axis=0)
            none = jnp.zeros_like(bias)
            low = near_ref[0] == 0
            kinds = [
                totals[:3], line(qsum_ref), line(vsum_ref), sums_ref[:4],
                jnp.where(low, bias, none), jnp.where(low, none, bias),
            ]
            kinds.append(jnp.zeros((LANES - UBIAS - 2 * groups, width), F32))
            small = jnp.concatenate(kinds, axis=0).T.astype(BF16)
            for x, (sent, kept) in enumerate(zip(*parted(small, near_ref[0], depth), strict=True)):
                sent_ref[x] = sent
                kept_ref[x] = kept

    tile = pl.BlockSpec((own, width), lambda t, _: (t, 0))
    piece = whole(halves, depth, LANES)
    return pl.pallas_call(
        kernel,
        grid_spec=pltpu.PrefetchScalarGridSpec(
            num_scalar_prefetch=1,
            grid=(blocks,),
            in_specs=[
                tile, tile, whole(own, width), tile,
                pl.BlockSpec((1, row_count, 1, size), lambda t, _: (t, 0, 0, 0)),
                whole(KINDS, width), whole(width, 3 * width), whole(own, width),
                whole(*sums.shape), whole(*gbias.shape), whole(*qsum.shape), whole(*vsum.shape),
                *[ANYWHERE] * len(after),
            ],
            out_specs=[
                pl.BlockSpec((1, own, width), lambda t, _: (jnp.clip(t - 1, 0, blocks // 2 - 2), 0, 0)),
                pl.BlockSpec((1, own, width), lambda t, _: (jnp.maximum(t - blocks // 2, 0), 0, 0)),
                whole(own, width), piece, piece,
            ],
            scratch_shapes=[pltpu.VMEM((8, width), F32)],
        ),
        out_shape=[
            placed(BF16, blocks // 2 - 1, own, width),
            placed(BF16, blocks // 2, own, width),
            placed(F32, own, width),
            shaped(BF16, halves, depth, LANES),
            shaped(BF16, halves, depth, LANES),
        ],
        compiler_params=parameters(36),
        cost_estimate=cost(5 * total * width * width, 8 * total * width + 12 * width * width, total),
        name="first_norm",
    )(near, far(d_key), far(d_value), d_query, rows_all, flags, vectors, weights, d_middle, sums, gbias, qsum, vsum, *after)


def after(value, *others):
    return lax.optimization_barrier((value, *others))[0]


class Links:
    def __init__(self, seq, rows):
        self.sizes = {"seq": seq, "rows": rows}
        order = []
        for axis in EVERY:
            mask = self.sizes[axis] // 2
            while mask:
                order.append((axis, mask))
                mask //= 2
        self.order = order
        place = {axis: lax.axis_index(axis) for axis in EVERY}
        self.value = {(a, m): ((place[a] // m) % 2).astype(jnp.int32) for a, m in order}
        self.near = ("seq", 1)
        self.first = ("seq", 2)
        self.second = ("rows", 1)
        self.others = [b for b in order if b[0] == "rows" and b[1] > 1]

    def swap(self, array, bit):
        axis, mask = bit
        return lax.ppermute(array, axis, [(i, i ^ mask) for i in range(self.sizes[axis])])

    def pick(self, array, bit, other=False, axis=0):
        at = 1 - self.value[bit] if other else self.value[bit]
        return lax.dynamic_index_in_dim(array, at, axis, keepdims=False)

    def gather(self, shard, bits, wanted):
        held, have = shard, []
        for i, bit in enumerate(bits):
            if i in wanted:
                held = after(held, *wanted[i])
            have = sorted([*have, bit], key=self.order.index)
            parts = held.reshape(2 ** have.index(bit), -1, held.shape[-1])
            other = self.swap(held, bit).reshape(parts.shape)
            upper = self.value[bit] == 1
            low = jnp.where(upper, other, parts)
            high = jnp.where(upper, parts, other)
            held = jnp.stack([low, high], axis=1).reshape(-1, held.shape[-1])
        return held

    def half(self, held, have, bit, other):
        before = 1
        for key in have[: have.index(bit)]:
            before *= key if isinstance(key, int) else 2
        parts = held.reshape(before, 2, -1, held.shape[-1])
        return self.pick(parts, bit, other, 1).reshape(-1, held.shape[-1])

    def add(self, kept, came, have, bit):
        def part(other):
            first, second = (self.half(a, have, bit, other) for a in (kept, came))
            return (first.astype(F32) + second.astype(F32)).astype(BF16)

        return part(True), part(False), [b for b in have if b != bit]


def body(
    patches, segments, masked, mask_embedding, norm1_gain, norm1_bias, qkv_weight, query_bias,
    value_bias, out_weight, out_bias, norm2_gain, norm2_bias, up_weight, up_bias, down_weight,
    down_bias, cotangent, *, seq, rows,
):
    links = Links(seq, rows)
    row_count, patch_count, width = patches.shape
    tokens = row_count * patch_count
    n = qkv_weight.shape[0]
    devices = seq * rows
    groups = up_weight.shape[1] // width
    mine = groups // 2
    half = width // 2
    halves = seq // 2
    depth = rows * n
    near, first, second, others = links.near, links.first, links.second, links.others
    near_place = links.value[near].reshape(1)

    packed = jnp.stack(
        [
            down_weight.reshape(2, mine, n, width),
            up_weight.reshape(n, devices, groups, n).transpose(2, 0, 1, 3).reshape(2, mine, n, width),
        ],
        axis=1,
    ).reshape(2, 2 * mine, n, width)
    packed_kept, packed_sent = links.pick(packed, near), links.pick(packed, near, True)
    packed_came = links.swap(packed_sent, near)

    flags = (segments + MASKED * masked).astype(BF16).reshape(1, row_count, patch_count)
    sources = [after(patches.reshape(tokens, width), packed_sent)]
    for bit in (first, near):
        flags = jnp.concatenate([flags, links.swap(flags, bit)], axis=0)
        sources += [links.swap(source, bit) for source in sources]
    early_ones, late_ones = [sources[1], flags], sources[2:]
    flags = flags.astype(F32).reshape(seq, row_count, 1, patch_count)
    small = [
        mask_embedding, norm1_gain, norm1_bias, query_bias, value_bias, out_bias, norm2_gain,
        norm2_bias, down_bias,
    ]
    columns = jnp.concatenate([jnp.stack(small), up_bias.reshape(groups, n)], axis=0).T
    columns = jnp.pad(columns, ((0, 0), (0, LANES - columns.shape[1])))
    fourths = [qkv_weight[:, i * half : (i + 1) * half] for i in range(6)]
    fourths += [out_weight[:, :half], out_weight[:, half:]]
    left = jnp.concatenate(fourths[::2], axis=1)
    right = jnp.concatenate([*fourths[1::2], columns], axis=1)
    left = links.gather(left, [*others, second, first], {2: early_ones, 3: late_ones}).reshape(halves, depth, -1)
    right = links.gather(right, [*others, first, second], {}).reshape(halves, depth, -1)
    left_other, right_other = links.swap(left, near), links.swap(right, near)

    low = links.value[near] == 0
    packed = jnp.stack([jnp.where(low, packed_kept, packed_came), jnp.where(low, packed_came, packed_kept)], axis=0)
    same_core = [
        [(x * 2 + core) * rows + r for x in range(halves) for r in range(rows)] for core in range(2)
    ]
    rest = lax.all_gather(packed, EVERY, axis=2, tiled=True, axis_index_groups=same_core)

    rows_all, turned, queries, key_values, weights, vectors = project(
        near_place, sources, flags, left, left_other, right, right_other
    )
    queries = queries.reshape(row_count, patch_count, width)
    key_values = key_values.reshape(seq, row_count, patch_count, 2 * width)
    mixed, mixed_full, lse = attend(queries, key_values, flags)
    mixed = mixed.reshape(tokens, width)
    d_branch = cotangent.reshape(tokens, width)
    d_branch_other = links.swap(d_branch, near)
    normed_two, middle = open_branch(mixed, rows_all, flags, vectors, weights)
    places = jnp.stack([links.value[near], links.value[first]])
    added, d_normed, away, down_sent, down_kept, grad_up, grad_up_bias = branch(
        places, normed_two, links.swap(normed_two, near), d_branch, d_branch_other, vectors, rest
    )

    row_bits = [*others, second]
    have = [first, *row_bits]
    flat = lambda held: held.reshape(-1, held.shape[-1])
    down_sent, down_kept = flat(down_sent), flat(down_kept)
    up_order = [mine, first, near, *row_bits]
    grad_up = flat(grad_up)
    up_sent = links.half(grad_up, up_order, second, True)
    up_kept = links.half(grad_up, up_order, second, False)
    up_order = [mine, first, near, *others]
    away = links.swap(away, near)
    down_came, up_came = links.swap(down_sent, first), links.swap(up_sent, second)
    d_middle, d_mixed, out_sent, out_kept, sums = between(
        near_place, d_normed, away, middle, d_branch, vectors, mixed, weights, halves
    )
    out_came = links.swap(out_sent, near)
    d_mixed = d_mixed.reshape(row_count, patch_count, width)

    given = (queries, key_values, d_mixed, mixed_full, lse, flags)
    d_query, d_key, d_value, query_sums, value_sums = attend_back(*given, [down_sent, up_sent])

    down_sent, down_kept, down_order = links.add(
        after(down_kept, d_query), down_came, [mine, near, *row_bits], second
    )
    down_came = links.swap(down_sent, second)
    up_sent, up_kept, up_order = links.add(after(up_kept, down_sent), up_came, up_order, first)
    up_came = links.swap(up_sent, first)
    d_query = d_query.reshape(tokens, width)
    d_key = d_key.reshape(-1, width)
    d_value = d_value.reshape(-1, width)
    pair_sent, pair_kept, value_sent, value_kept = weight_grads(
        near_place, turned, d_key, d_value, d_query, halves, [down_sent, up_sent]
    )
    output = after(middle, pair_sent) + added + away[0].astype(F32) + vectors[DBIAS]
    output = output.astype(BF16)
    early_kept = jnp.concatenate([after(down_kept, output), up_kept], axis=0)
    early_came = jnp.concatenate([after(down_came, output), up_came], axis=0)
    early_order = [2 * mine, near, *others]
    early_sent, early_kept, early_order = links.add(early_kept, early_came, early_order, others[-1])
    early = [early_kept, links.swap(early_sent, others[-1]), early_order]
    pair_came = links.swap(flat(after(pair_sent, early_sent)), near)
    value_came = links.swap(flat(after(value_sent, early_sent)), near)
    pair_sent, pair_kept, pair_order = links.add(flat(pair_kept), pair_came, have, second)
    pair_came = links.swap(pair_sent, second)
    last_kept = jnp.concatenate([flat(value_kept), flat(out_kept)], axis=1)
    last_came = jnp.concatenate([value_came, flat(out_came)], axis=1)
    last_sent, last_kept, last_order = links.add(after(last_kept, pair_sent), last_came, have, first)
    last_came = links.swap(last_sent, first)
    far_share, near_share, own, small_sent, small_kept = first_norm(
        near_place, d_key, d_value, d_query, rows_all, flags, vectors, weights, d_middle, sums,
        grad_up_bias, query_sums, value_sums, halves, [early_sent, pair_sent, last_sent],
    )

    pair = [pair_kept, pair_came, pair_order]
    last = [last_kept, last_came, last_order]

    def go(item, bit, gone):
        gone, item[0], item[2] = links.add(after(item[0], gone), item[1], item[2], bit)
        item[1] = links.swap(gone, bit)
        return gone

    rest_bits = others[-2::-1]
    gone = own
    for bit in rest_bits:
        gone = go(early, bit, gone)
    pair_sent, pair[0], pair[2] = links.add(after(pair[0], gone), pair[1], pair[2], first)
    gone = pair_sent
    gone = go(last, second, gone)
    near_share = links.swap(after(near_share, gone), near)
    small = [flat(small_kept), links.swap(flat(after(small_sent, gone)), near), have]
    gone = go(small, first, gone)
    pair[1] = links.swap(after(pair_sent, gone), first)
    gone = (after(far_share, gone).astype(F32) + near_share[1:].astype(F32)).astype(BF16)
    far_share = links.swap(gone, first)
    gone = go(small, second, gone)
    last[0] = jnp.concatenate([after(pair[0], gone), last[0], small[0]], axis=1)
    last[1] = jnp.concatenate([pair[1], last[1], small[1]], axis=1)
    gone = go(last, others[-1], gone)
    low = links.value[near] == 0
    early_sum = after(early[0], gone).astype(F32) + early[1].astype(F32)
    early_sum = early_sum.reshape(2 * mine, 2, n, width)
    far_sum = links.pick(early_sum, near, True, 1).astype(BF16)
    far_sum = links.swap(far_sum, near).astype(F32)
    early_sum = links.pick(early_sum, near, False, 1)
    for bit in rest_bits:
        gone = go(last, bit, gone)
    early_sum = after(early_sum, gone)
    joined = jnp.stack(
        [jnp.where(low, early_sum, far_sum), jnp.where(low, far_sum, early_sum)], axis=0
    )
    down_sum = joined[:, :mine].reshape(-1, width)
    up_sum = joined[:, mine:].reshape(groups, n, devices, n)
    up_sum = up_sum.transpose(1, 2, 0, 3).reshape(n, -1)
    input_grad = after(own, up_sum) + near_share[0].astype(F32) + far_share[0].astype(F32)
    is_masked = masked.reshape(tokens, 1) == 1
    input_grad = jnp.where(is_masked, 0.0, input_grad)
    last = after(last[0], input_grad).astype(F32) + last[1].astype(F32)
    pair, last = last[:, : 2 * width], last[:, 2 * width :]
    project_sum = jnp.concatenate([pair, last[:, :width]], axis=1)
    out_sum = last[:, width : 2 * width]
    tail = last[:, 2 * width :].T
    shape = (row_count, patch_count, width)
    return (
        output.reshape(shape), input_grad.reshape(shape), tail[EMBED], tail[GAIN1], tail[SHIFT1],
        project_sum, tail[QBIAS], tail[VBIAS], out_sum, tail[OBIAS], tail[GAIN2], tail[SHIFT2],
        up_sum, tail[UBIAS : UBIAS + groups].reshape(-1), down_sum, tail[DBIAS],
    )


def solution(mesh):
    one, two = P(EVERY), P(EVERY, None)
    rows, flags = P("rows", "seq", None), P("rows", "seq")
    seq, row_groups = mesh.shape["seq"], mesh.shape["rows"]

    def run(*arguments):
        return body(*arguments, seq=seq, rows=row_groups)

    return jax.shard_map(
        run,
        mesh=mesh,
        in_specs=(
            rows, flags, flags, one, one, one, two, one, one, two, one, one, one, two, one, two,
            one, rows,
        ),
        out_specs=(
            rows, rows, one, one, one, two, one, one, two, one, one, one, two, one, two, one,
        ),
        check_vma=False,
    )
```

```python
import jax
import jax.numpy as jnp
from jax import lax
from jax.experimental import pallas as pl
from jax.experimental.pallas import tpu as pltpu
from jax.sharding import PartitionSpec as P

HEAD_SIZE = 64
LANES = 128
CHUNK = 256
PAIRS = 6
MASKED = 16
EPSILON = 1e-06
FLOOR_SCORE = -1e30
HALF_ROOT = 0.7071067811865476
MIB = 2**20
EVERY = ("seq", "rows")
BF16 = jnp.bfloat16
F32 = jnp.float32
EMBED, GAIN1, SHIFT1, QBIAS, VBIAS, OBIAS, GAIN2, SHIFT2, DBIAS, UBIAS = range(10)
KINDS = 16


def dot(left, right, left_dim, right_dim):
    return lax.dot_general(
        left, right, (((left_dim,), (right_dim,)), ((), ())), preferred_element_type=F32
    )


def column(row):
    return jnp.broadcast_to(row, (8, row.shape[1])).T[:, :1]


def segment_of(flags):
    return flags - jnp.where(flags >= MASKED, float(MASKED), 0.0)


def norm_parts(values):
    mean = jnp.mean(values, axis=-1, keepdims=True)
    centered = values - mean
    rate = lax.rsqrt(jnp.mean(centered * centered, axis=-1, keepdims=True) + EPSILON)
    return centered * rate, rate


def norm_back(pulled, hat, rate):
    first = jnp.mean(pulled, axis=-1, keepdims=True)
    second = jnp.mean(pulled * hat, axis=-1, keepdims=True)
    return rate * (pulled - first - hat * second)


def parted(value, mine, depth):
    sent, kept = [], []
    for x in range(value.shape[0] // (2 * depth)):
        low = value[2 * x * depth : (2 * x + 1) * depth]
        high = value[(2 * x + 1) * depth : (2 * x + 2) * depth]
        sent.append(jnp.where(mine == 0, high, low))
        kept.append(jnp.where(mine == 0, low, high))
    return sent, kept


def whole(*shape):
    return pl.BlockSpec(shape, lambda *_: (0,) * len(shape))


ANYWHERE = pl.BlockSpec(memory_space=pl.ANY)


def shaped(dtype, *shape):
    return jax.ShapeDtypeStruct(shape, dtype)


def placed(dtype, *shape):
    return pltpu.HBM(shape, dtype)


def far(array):
    return pltpu.with_memory_space_constraint(array, pltpu.HBM)


def parameters(mib=32):
    return pltpu.CompilerParams(vmem_limit_bytes=mib * MIB)


def cost(flops, nbytes, transcendentals=0):
    return pl.CostEstimate(flops=flops, bytes_accessed=nbytes, transcendentals=transcendentals)


def split_heads(pair):
    lane = lax.broadcasted_iota(jnp.int32, pair.shape, 1)
    zero = jnp.zeros_like(pair)
    return jnp.concatenate(
        [jnp.where(lane < HEAD_SIZE, pair, zero), jnp.where(lane < HEAD_SIZE, zero, pair)], axis=0
    )


def join_heads(both, count):
    row = lax.broadcasted_iota(jnp.int32, (both.shape[0], count), 0)
    return jnp.where(row < HEAD_SIZE, both[:, :count], both[:, count:]).T


def set_bias(flags_ref, bias):
    blocks, size = flags_ref.shape[0], flags_ref.shape[3]
    asked = segment_of(flags_ref[0, 0])
    for j in range(blocks):
        keys = column(segment_of(flags_ref[j, 0]))
        bias[pl.ds(j * size, size), :] = jnp.where((keys == asked) & (keys > 0.0), 0.0, FLOOR_SCORE)


def attend_kernel(q_ref, k_ref, v_ref, flags_ref, mix_ref, full_ref, lse_ref, bias, held):
    count, blocks, size = q_ref.shape[1], k_ref.shape[0], k_ref.shape[2]

    @pl.when(pl.program_id(1) == 0)
    def _():
        set_bias(flags_ref, bias)

    live = segment_of(flags_ref[0, 0]) > 0.0
    live = jnp.concatenate([live, live], axis=1)
    for u in range(PAIRS):
        lanes = slice(u * LANES, (u + 1) * LANES)
        asked = split_heads(q_ref[0, :, lanes])
        top = None
        for j in range(blocks):
            rows = pl.ds(j * size, size)
            part = bias[rows, :]
            scores = dot(k_ref[j, 0, :, lanes], asked, 1, 1) + jnp.concatenate([part, part], axis=1)
            held[u % 2, rows, :] = scores
            high = jnp.max(scores, axis=0, keepdims=True)
            top = high if top is None else jnp.maximum(top, high)
        total, mixed = 0.0, 0.0
        for j in range(blocks):
            weights = jnp.exp(held[u % 2, pl.ds(j * size, size), :] - top)
            total = total + jnp.sum(weights, axis=0, keepdims=True)
            mixed = mixed + dot(v_ref[j, 0, :, lanes].T, weights.astype(BF16), 1, 0)
        result = join_heads(mixed * jnp.where(live, 1.0 / total, 0.0), count)
        mix_ref[0, :, lanes] = result.astype(BF16)
        full_ref[0, :, lanes] = result
        lse_ref[0, u] = jnp.where(live, top + jnp.log(total), 0.0)


def attend_back_kernel(
    q_ref, k_ref, v_ref, dm_ref, full_ref, lse_ref, flags_ref,
    dq_ref, dk_ref, dv_ref, qsum_ref, vsum_ref, bias,
):
    count, blocks, size = q_ref.shape[1], k_ref.shape[0], k_ref.shape[2]

    set_bias(flags_ref, bias)
    for u in range(q_ref.shape[2] // LANES):
        lanes = slice(u * LANES, (u + 1) * LANES)
        d_mixed = dm_ref[0, :, lanes]
        asked, pulled = split_heads(q_ref[0, :, lanes]), split_heads(d_mixed)
        product = (d_mixed.astype(F32) * full_ref[0, :, lanes]).T
        delta = jnp.concatenate(
            [
                jnp.sum(product[:HEAD_SIZE], axis=0, keepdims=True),
                jnp.sum(product[HEAD_SIZE:], axis=0, keepdims=True),
            ],
            axis=1,
        )
        lse = lse_ref[0, u]
        d_query, v_sum = 0.0, 0.0
        for j in range(blocks):
            keys = k_ref[j, 0, :, lanes]
            part = bias[pl.ds(j * size, size), :]
            scores = dot(keys, asked, 1, 1) + jnp.concatenate([part, part], axis=1)
            probs = jnp.exp(scores - lse)
            d_probs = dot(v_ref[j, 0, :, lanes], pulled, 1, 1)
            d_scores = (probs * (d_probs - delta)).astype(BF16)
            d_value = dot(probs.astype(BF16), pulled, 1, 0)
            dv_ref[j, 0, :, lanes] = d_value.astype(BF16)
            dk_ref[j, 0, :, lanes] = dot(d_scores, asked, 1, 0).astype(BF16)
            v_sum = v_sum + jnp.sum(d_value, axis=0, keepdims=True)
            d_query = d_query + dot(keys.T, d_scores, 1, 0)
        d_query = join_heads(d_query, count) * HEAD_SIZE**-0.5
        dq_ref[0, :, lanes] = d_query.astype(BF16)
        qsum_ref[0, u] = jnp.sum(d_query, axis=0, keepdims=True)
        vsum_ref[0, u] = v_sum


def attend(queries, key_values, flags):
    rows, count, width = queries.shape
    blocks, _, size, _ = key_values.shape
    pairs = width // LANES
    tile = pl.BlockSpec((1, count, PAIRS * LANES), lambda r, p: (r, 0, p))
    steps = pairs // PAIRS
    area = rows * count * blocks * size
    return pl.pallas_call(
        attend_kernel,
        grid=(rows, steps),
        in_specs=[
            tile,
            pl.BlockSpec((blocks, 1, size, PAIRS * LANES), lambda r, p: (0, r, 0, p)),
            pl.BlockSpec((blocks, 1, size, PAIRS * LANES), lambda r, p: (0, r, 0, steps + p)),
            pl.BlockSpec((blocks, 1, 1, size), lambda r, p: (0, r, 0, 0)),
        ],
        out_specs=[tile, tile, pl.BlockSpec((1, PAIRS, 1, 2 * count), lambda r, p: (r, p, 0, 0))],
        out_shape=[
            shaped(BF16, *queries.shape),
            placed(F32, *queries.shape),
            shaped(F32, rows, pairs, 1, 2 * count),
        ],
        scratch_shapes=[
            pltpu.VMEM((blocks * size, count), F32),
            pltpu.VMEM((2, blocks * size, 2 * count), F32),
        ],
        compiler_params=parameters(),
        cost_estimate=cost(16 * area * width, 8 * rows * blocks * size * width, area * 12),
        name="attend",
    )(far(queries), far(key_values), far(key_values), flags)


def attend_back(queries, key_values, d_mixed, mixed_full, lse, flags, after):
    rows, count, width = queries.shape
    blocks, _, size, _ = key_values.shape
    pairs = width // LANES
    tile = pl.BlockSpec((1, count, width), lambda r: (r, 0, 0))
    keys = pl.BlockSpec((blocks, 1, size, width), lambda r: (0, r, 0, 0))
    line = lambda w: pl.BlockSpec((1, pairs, 1, w), lambda r: (r, 0, 0, 0))
    area = rows * count * blocks * size
    grads = placed(BF16, blocks, rows, size, width)
    sums = shaped(F32, rows, pairs, 1, LANES)
    given = [queries, key_values, key_values, d_mixed, mixed_full, lse, flags]

    def kernel(*refs):
        attend_back_kernel(*refs[: len(given)], *refs[len(given) + len(after) :])

    return pl.pallas_call(
        kernel,
        grid=(rows,),
        in_specs=[
            tile, keys, pl.BlockSpec((blocks, 1, size, width), lambda r: (0, r, 0, 1)), tile, tile,
            line(2 * count), pl.BlockSpec((blocks, 1, 1, size), lambda r: (0, r, 0, 0)),
            *[ANYWHERE] * len(after),
        ],
        out_specs=[tile, keys, keys, line(LANES), line(LANES)],
        out_shape=[placed(BF16, *queries.shape), grads, grads, sums, sums],
        scratch_shapes=[pltpu.VMEM((blocks * size, count), F32)],
        compiler_params=parameters(40),
        cost_estimate=cost(32 * area * width, 16 * rows * blocks * size * width, area * 12),
        name="attend_back",
    )(*given, *after)


def project(near, sources, flags, left, left_other, right, right_other):
    own, width = sources[0].shape
    blocks, row_count, _, size = flags.shape
    total, steps = own * blocks, blocks
    halves, depth, part = left.shape
    half = width // 2

    def kernel(near_ref, *refs):
        first_ref, ahead_ref, lm_ref, lo_ref, rm_ref, ro_ref = refs[blocks : blocks + 6]
        rows_out, turned_ref, q_ref, kv_ref, w_out, vec_ref = refs[blocks + 6 : blocks + 12]
        rows, weights, normed, columns, sems, out_sems = refs[blocks + 12 :]
        step = pl.program_id(0)
        outward = [
            pltpu.make_async_copy(rows, rows_out, out_sems.at[0]),
            pltpu.make_async_copy(weights, w_out, out_sems.at[1]),
        ]

        def norm(at, slot, flags_ref):
            gain, shift = vec_ref[GAIN1 : GAIN1 + 1], vec_ref[SHIFT1 : SHIFT1 + 1]
            embed = vec_ref[EMBED : EMBED + 1]
            for r in range(row_count):
                masked = column(flags_ref[0, r]) >= MASKED
                here = rows[pl.ds(pl.multiple_of(at * own + r * size, size), size), :].astype(F32)
                hat, _ = norm_parts(jnp.where(masked, embed, here))
                normed[slot, r * size : (r + 1) * size, :] = (hat * gain + shift).astype(BF16)

        @pl.when(step == 0)
        def _():
            near_place = near_ref[0]
            later, first = [], []
            for which in range(2):
                mine = near_place if which == 0 else 1 - near_place
                low, high = (lm_ref, rm_ref) if which == 0 else (lo_ref, ro_ref)
                for x in range(halves):
                    at = pl.ds(pl.multiple_of(x * 2 * depth + mine * depth, depth), depth)
                    first.append((high.at[x, :, pl.ds(part, LANES)], columns.at[at, :]))
                    for side, source in enumerate((low, high)):
                        for kind in range(4):
                            later.append(
                                (
                                    source.at[x, :, pl.ds(kind * half, half)],
                                    weights.at[at, pl.ds(kind * width + side * half, half)],
                                )
                            )
            first.append((refs[0], rows.at[pl.ds(0, own), :]))
            later += [(refs[i], rows.at[pl.ds(i * own, own), :]) for i in range(1, blocks)]
            copies = [
                pltpu.make_async_copy(a, b, sems.at[i]) for i, (a, b) in enumerate([*first, *later])
            ]
            for copy in copies:
                copy.start()
            for copy in copies[: len(first)]:
                copy.wait()
            vec_ref[...] = columns[...].astype(F32).T[:KINDS]
            norm(0, 0, first_ref)
            for copy in copies[len(first) :]:
                copy.wait()
            for copy in outward:
                copy.start()

        slot = lax.rem(step, 2)
        here = normed[slot]
        kv_ref[:, :width] = dot(here, weights[:, width : 2 * width], 1, 0).astype(BF16)
        values = dot(here, weights[:, 2 * width : 3 * width], 1, 0)
        kv_ref[:, width:] = (values + vec_ref[VBIAS : VBIAS + 1]).astype(BF16)
        turned_ref[...] = here.T
        norm(jnp.minimum(step + 1, steps - 1), 1 - slot, ahead_ref)

        @pl.when(step == 0)
        def _():
            asked = dot(here, weights[:, :width], 1, 0) + vec_ref[QBIAS : QBIAS + 1]
            q_ref[...] = (asked * HEAD_SIZE**-0.5).astype(BF16)

        @pl.when(step == steps - 1)
        def _():
            for copy in outward:
                copy.wait()

    def ahead(t, _):
        return (jnp.minimum(t + 1, steps - 1), 0, 0, 0)

    return pl.pallas_call(
        kernel,
        grid_spec=pltpu.PrefetchScalarGridSpec(
            num_scalar_prefetch=1,
            grid=(steps,),
            in_specs=[
                *[ANYWHERE] * blocks,
                whole(1, row_count, 1, size),
                pl.BlockSpec((1, row_count, 1, size), ahead),
                *[ANYWHERE] * 4,
            ],
            out_specs=[
                ANYWHERE,
                pl.BlockSpec((width, own), lambda t, _: (0, t)),
                whole(own, width),
                pl.BlockSpec((own, 2 * width), lambda t, _: (t, 0)),
                ANYWHERE,
                whole(KINDS, width),
            ],
            scratch_shapes=[
                pltpu.VMEM((total, width), BF16),
                pltpu.VMEM((width, 4 * width), BF16),
                pltpu.VMEM((2, own, width), BF16),
                pltpu.VMEM((width, LANES), BF16),
                pltpu.SemaphoreType.DMA((18 * halves + blocks,)),
                pltpu.SemaphoreType.DMA((2,)),
            ],
        ),
        out_shape=[
            placed(BF16, total, width),
            placed(BF16, width, total),
            placed(BF16, own, width),
            placed(BF16, total, 2 * width),
            placed(BF16, width, 4 * width),
            shaped(F32, KINDS, width),
        ],
        compiler_params=parameters(40),
        cost_estimate=cost(5 * total * width * width, 8 * total * width + 16 * width * width, total),
        name="project",
    )(near, *sources, flags, flags, left, left_other, right, right_other)


def open_branch(mixed, rows_all, flags, vectors, weights):
    tokens, width = mixed.shape
    _, row_count, _, size = flags.shape

    def kernel(mixed_ref, rows_ref, flags_ref, vec_ref, w_ref, normed_ref, middle_ref):
        masked = column(flags_ref[0, 0]) >= MASKED
        embed, bias = vec_ref[EMBED : EMBED + 1], vec_ref[OBIAS : OBIAS + 1]
        gain, shift = vec_ref[GAIN2 : GAIN2 + 1], vec_ref[SHIFT2 : SHIFT2 + 1]
        added = dot(mixed_ref[...], w_ref[...], 1, 0)
        for c in range(0, size, CHUNK):
            cut = slice(c, c + CHUNK)
            values = jnp.where(masked[cut], embed, rows_ref[cut].astype(F32))
            middle = values + added[cut] + bias
            middle_ref[cut] = middle
            hat, _ = norm_parts(middle)
            normed_ref[cut] = (hat * gain + shift).astype(BF16)

    tile = pl.BlockSpec((size, width), lambda t: (t, 0))
    return pl.pallas_call(
        kernel,
        grid=(row_count,),
        in_specs=[
            tile, tile, pl.BlockSpec((1, 1, 1, size), lambda t: (0, t, 0, 0)), whole(KINDS, width),
            pl.BlockSpec((width, width), lambda t: (0, 3)),
        ],
        out_specs=[tile, tile],
        out_shape=[placed(BF16, tokens, width), placed(F32, tokens, width)],
        compiler_params=parameters(),
        cost_estimate=cost(2 * tokens * width * width, 10 * tokens * width),
        name="open_branch",
    )(mixed, rows_all, flags, vectors, weights)


def branch(places, normed, normed_other, pulled, pulled_other, vectors, rest):
    tokens, width = normed.shape
    groups = rest.shape[1] // 2
    cores, length = rest.shape[0], rest.shape[2]
    depth = length // 2
    both = 2 * tokens
    size = both

    def kernel(
        places_ref, n_ref, no_ref, c_ref, co_ref, vec_ref, down_ref, up_ref,
        total_ref, dn_ref, away_ref, sdown_ref, kdown_ref, gup_ref, gbias_ref,
        normed_all, turned, pulled_all, totals, d_normed, activated, d_hidden, up, down, staged, sems,
    ):
        step = pl.program_id(0)

        @pl.when(step == 0)
        def _():
            normed_all[:tokens] = n_ref[...]
            normed_all[tokens:] = no_ref[...]
            turned[:, :tokens] = n_ref[...].T
            turned[:, tokens:] = no_ref[...].T
            pulled_all[:tokens] = c_ref[...]
            pulled_all[tokens:] = co_ref[...]

        at = 0
        for x in range(2):
            for core in range(cores):
                up[at : at + depth] = up_ref[core, 0, x * depth : (x + 1) * depth]
                down[at : at + depth] = down_ref[core, 0, x * depth : (x + 1) * depth]
                at += depth
        bias = vec_ref[pl.ds(UBIAS + groups * places_ref[0] + step, 1), :]
        bias_grad = 0.0
        for c in range(0, both, size):
            cut = slice(c, c + size)
            hidden = dot(normed_all[cut], up[...], 1, 0) + bias
            d_active = dot(pulled_all[cut], down[...], 1, 1)
            phi = 0.5 * (1.0 + lax.erf(hidden * HALF_ROOT))
            slope = phi + hidden * (0.3989422804014327 * jnp.exp(-0.5 * hidden * hidden))
            activated[cut] = (hidden * phi).astype(BF16)
            grad = (d_active * slope).astype(BF16)
            d_hidden[cut] = grad
            bias_grad += jnp.sum(grad.astype(F32), axis=0, keepdims=True)
        gbias_ref[0] = bias_grad
        for c in range(0, both, size):
            cut = slice(c, c + size)
            more = dot(activated[cut], down[...], 1, 0)
            more_back = dot(d_hidden[cut], up[...], 1, 1)

            @pl.when(step == 0)
            def _(cut=cut, more=more, more_back=more_back):
                totals[cut] = more
                d_normed[cut] = more_back

            @pl.when(step > 0)
            def _(cut=cut, more=more, more_back=more_back):
                totals[cut] += more
                d_normed[cut] += more_back

        last = step == pl.num_programs(0) - 1
        outward = [
            pltpu.make_async_copy(totals.at[pl.ds(0, tokens)], total_ref, sems.at[0]),
            pltpu.make_async_copy(d_normed.at[pl.ds(0, tokens)], dn_ref, sems.at[1]),
            pltpu.make_async_copy(staged, away_ref, sems.at[2]),
        ]

        @pl.when(last)
        def _():
            staged[0] = totals[tokens:].astype(BF16)
            staged[1] = d_normed[tokens:].astype(BF16)
            for copy in outward:
                copy.start()

        gup_ref[0] = dot(turned[...], d_hidden[...], 1, 0).astype(BF16)
        grads = dot(activated[...], pulled_all[...], 0, 0).astype(BF16)
        (sent,), (kept,) = parted(grads, places_ref[1], length)
        for core in range(cores):
            sdown_ref[0, core] = sent[core * depth : (core + 1) * depth]
            kdown_ref[0, core] = kept[core * depth : (core + 1) * depth]

        @pl.when(last)
        def _():
            for copy in outward:
                copy.wait()

    weight = lambda f: pl.BlockSpec((cores, 1, length, width), lambda k, _: (0, f(k), 0, 0))
    piece = pl.BlockSpec((1, cores, depth, width), lambda k, _: (k, 0, 0, 0))
    square = pl.BlockSpec((1, width, width), lambda k, _: (k, 0, 0))
    patch = whole(tokens, width)
    return pl.pallas_call(
        kernel,
        grid_spec=pltpu.PrefetchScalarGridSpec(
            num_scalar_prefetch=1,
            grid=(groups,),
            in_specs=[
                patch, patch, patch, patch, whole(KINDS, width), weight(lambda k: k),
                weight(lambda k: groups + k),
            ],
            out_specs=[
                ANYWHERE, ANYWHERE, ANYWHERE, piece, piece, square,
                pl.BlockSpec((1, 1, width), lambda k, _: (k, 0, 0)),
            ],
            scratch_shapes=[
                pltpu.VMEM((both, width), BF16),
                pltpu.VMEM((width, both), BF16),
                pltpu.VMEM((both, width), BF16),
                pltpu.VMEM((both, width), F32),
                pltpu.VMEM((both, width), F32),
                pltpu.VMEM((both, width), BF16),
                pltpu.VMEM((both, width), BF16),
                pltpu.VMEM((width, width), BF16),
                pltpu.VMEM((width, width), BF16),
                pltpu.VMEM((2, tokens, width), BF16),
                pltpu.SemaphoreType.DMA((3,)),
            ],
        ),
        out_shape=[
            placed(F32, tokens, width),
            placed(F32, tokens, width),
            placed(BF16, 2, tokens, width),
            placed(BF16, groups, cores, depth, width),
            placed(BF16, groups, cores, depth, width),
            placed(BF16, groups, width, width),
            shaped(F32, groups, 1, width),
        ],
        compiler_params=parameters(52),
        cost_estimate=cost(
            12 * groups * both * width * width, 20 * width * width, 2 * both * width * groups
        ),
        name="branch",
    )(places, far(normed), normed_other, pulled, pulled_other, vectors, rest, rest)


def between(near, d_normed, d_normed_other, middle, pulled, vectors, mixed, weights, halves):
    tokens, width = mixed.shape
    depth = width // (2 * halves)
    size = tokens // 2

    def kernel(
        near_ref, dn_ref, more_ref, middle_ref, cot_ref, vec_ref, mixed_ref, w_ref,
        dmiddle_ref, dmixed_ref, sent_ref, kept_ref, sums_ref, d_attn, grads,
    ):
        step = pl.program_id(0)
        gain = vec_ref[GAIN2 : GAIN2 + 1]
        sums = 0.0
        for c in range(0, size, CHUNK):
            cut = slice(c, c + CHUNK)
            d_out = dn_ref[cut] + more_ref[0, cut].astype(F32)
            cot = cot_ref[cut].astype(F32)
            hat, rate = norm_parts(middle_ref[cut])
            d_middle = cot + norm_back(d_out * gain, hat, rate)
            dmiddle_ref[cut] = d_middle
            low = d_middle.astype(BF16)
            d_attn[cut] = low
            parts = [low.astype(F32), d_out * hat, d_out, cot]
            sums += jnp.concatenate([jnp.sum(s, axis=0, keepdims=True) for s in parts], axis=0)
        sums = jnp.concatenate([sums, jnp.zeros_like(sums)], axis=0)
        dmixed_ref[...] = dot(d_attn[...], w_ref[...], 1, 1).astype(BF16)
        more = dot(mixed_ref[...], d_attn[...], 0, 0)

        @pl.when(step == 0)
        def _():
            sums_ref[...] = sums
            grads[...] = more

        @pl.when(step == 1)
        def _():
            sums_ref[...] += sums
            value = (grads[...] + more).astype(BF16)
            for x, (sent, kept) in enumerate(zip(*parted(value, near_ref[0], depth), strict=True)):
                sent_ref[x] = sent
                kept_ref[x] = kept

    tile = pl.BlockSpec((size, width), lambda t, _: (t, 0))
    piece = whole(halves, depth, width)
    return pl.pallas_call(
        kernel,
        grid_spec=pltpu.PrefetchScalarGridSpec(
            num_scalar_prefetch=1,
            grid=(2,),
            in_specs=[
                tile, pl.BlockSpec((1, size, width), lambda t, _: (1, t, 0)), tile, tile,
                whole(KINDS, width), tile, pl.BlockSpec((width, width), lambda t, _: (0, 3)),
            ],
            out_specs=[tile, tile, piece, piece, whole(8, width)],
            scratch_shapes=[pltpu.VMEM((size, width), BF16), pltpu.VMEM((width, width), F32)],
        ),
        out_shape=[
            placed(F32, tokens, width),
            shaped(BF16, tokens, width),
            placed(BF16, halves, depth, width),
            placed(BF16, halves, depth, width),
            shaped(F32, 8, width),
        ],
        compiler_params=parameters(),
        cost_estimate=cost(4 * tokens * width * width, 16 * tokens * width),
        name="between",
    )(near, d_normed, d_normed_other, middle, pulled, vectors, mixed, far(weights))


def weight_grads(near, turned, d_key, d_value, d_query, halves, after):
    width, total = turned.shape
    own = d_query.shape[0]
    depth = width // (2 * halves)

    def kernel(near_ref, turned_ref, dk_ref, dv_ref, dq_ref, *refs):
        sa_ref, ka_ref, sb_ref, kb_ref = refs[len(after) :]
        step = pl.program_id(0)

        def put(value, sent_ref, kept_ref, at):
            pieces = zip(*parted(value.astype(BF16), near_ref[0], depth), strict=True)
            for x, (sent, kept) in enumerate(pieces):
                sent_ref[x, :, at : at + width] = sent
                kept_ref[x, :, at : at + width] = kept

        @pl.when(step == 0)
        def _():
            put(dot(turned_ref[:, :own], dq_ref[...], 1, 0), sa_ref, ka_ref, 0)

        @pl.when(step == 1)
        def _():
            put(dot(turned_ref[...], dk_ref[...], 1, 0), sa_ref, ka_ref, width)

        @pl.when(step == 2)
        def _():
            put(dot(turned_ref[...], dv_ref[...], 1, 0), sb_ref, kb_ref, 0)

    pair, single = whole(halves, depth, 2 * width), whole(halves, depth, width)
    return pl.pallas_call(
        kernel,
        grid_spec=pltpu.PrefetchScalarGridSpec(
            num_scalar_prefetch=1,
            grid=(3,),
            in_specs=[
                whole(width, total), whole(total, width), whole(total, width), whole(own, width),
                *[ANYWHERE] * len(after),
            ],
            out_specs=[pair, pair, single, single],
        ),
        out_shape=[
            placed(BF16, halves, depth, 2 * width),
            placed(BF16, halves, depth, 2 * width),
            placed(BF16, halves, depth, width),
            placed(BF16, halves, depth, width),
        ],
        compiler_params=parameters(36),
        cost_estimate=cost(5 * total * width * width, 8 * total * width + 12 * width * width),
        name="weight_grads",
    )(near, turned, d_key, d_value, d_query, *after)


def first_norm(
    near, d_key, d_value, d_query, rows_all, flags, vectors, weights, d_middle, sums, gbias, qsum, vsum, halves, after,
):
    total, width = rows_all.shape
    blocks, row_count, _, size = flags.shape
    own = d_query.shape[0]
    depth = width // (2 * halves)
    groups = gbias.shape[0]

    def kernel(near_ref, *refs):
        (
            dk_ref, dv_ref, dq_ref, rows_ref, flags_ref, vec_ref, w_ref, dmiddle_ref, sums_ref,
            gbias_ref, qsum_ref, vsum_ref,
        ) = refs[:12]
        far_ref, near_share_ref, own_ref, sent_ref, kept_ref, totals = refs[12 + len(after) :]
        step = pl.program_id(0)

        def put_share(step, cut, value):
            @pl.when(step < blocks // 2)
            def _():
                far_ref[0, cut] = value

            @pl.when(step >= blocks // 2)
            def _():
                near_share_ref[0, cut] = value

        def one(mine):
            d_all = dot(dk_ref[...], w_ref[:, width : 2 * width], 1, 1)
            d_all += dot(dv_ref[...], w_ref[:, 2 * width :], 1, 1)
            if mine:
                d_all += dot(dq_ref[...], w_ref[:, :width], 1, 1)
            gain, embed = vec_ref[GAIN1 : GAIN1 + 1], vec_ref[EMBED : EMBED + 1]
            more = 0.0
            for r in range(row_count):
                cut = slice(r * size, (r + 1) * size)
                masked = column(flags_ref[0, r]) >= MASKED
                d_normed = d_all[cut]
                hat, rate = norm_parts(jnp.where(masked, embed, rows_ref[cut].astype(F32)))
                d_embedded = norm_back(d_normed * gain, hat, rate)
                if mine:
                    d_embedded = d_embedded + dmiddle_ref[cut]
                    own_ref[cut] = d_embedded
                else:
                    put_share(step, cut, d_embedded.astype(BF16))
                parts = [jnp.where(masked, d_embedded, 0.0), d_normed * hat, d_normed]
                more += jnp.concatenate([jnp.sum(s, axis=0, keepdims=True) for s in parts], axis=0)
            return more

        @pl.when(step == 0)
        def _():
            totals[:3] = one(True)

        @pl.when(step > 0)
        def _():
            totals[:3] += one(False)

        @pl.when(step == blocks - 1)
        def _():
            def line(ref):
                rows, pairs = ref.shape[0], ref.shape[1]
                return sum(
                    jnp.concatenate([ref[r, p] for p in range(pairs)], axis=1) for r in range(rows)
                )

            bias = jnp.concatenate([gbias_ref[k] for k in range(groups)], axis=0)
            none = jnp.zeros_like(bias)
            low = near_ref[0] == 0
            kinds = [
                totals[:3], line(qsum_ref), line(vsum_ref), sums_ref[:4],
                jnp.where(low, bias, none), jnp.where(low, none, bias),
            ]
            kinds.append(jnp.zeros((LANES - UBIAS - 2 * groups, width), F32))
            small = jnp.concatenate(kinds, axis=0).T.astype(BF16)
            for x, (sent, kept) in enumerate(zip(*parted(small, near_ref[0], depth), strict=True)):
                sent_ref[x] = sent
                kept_ref[x] = kept

    tile = pl.BlockSpec((own, width), lambda t, _: (t, 0))
    piece = whole(halves, depth, LANES)
    return pl.pallas_call(
        kernel,
        grid_spec=pltpu.PrefetchScalarGridSpec(
            num_scalar_prefetch=1,
            grid=(blocks,),
            in_specs=[
                tile, tile, whole(own, width), tile,
                pl.BlockSpec((1, row_count, 1, size), lambda t, _: (t, 0, 0, 0)),
                whole(KINDS, width), whole(width, 3 * width), whole(own, width),
                whole(*sums.shape), whole(*gbias.shape), whole(*qsum.shape), whole(*vsum.shape),
                *[ANYWHERE] * len(after),
            ],
            out_specs=[
                pl.BlockSpec((1, own, width), lambda t, _: (jnp.clip(t - 1, 0, blocks // 2 - 2), 0, 0)),
                pl.BlockSpec((1, own, width), lambda t, _: (jnp.maximum(t - blocks // 2, 0), 0, 0)),
                whole(own, width), piece, piece,
            ],
            scratch_shapes=[pltpu.VMEM((8, width), F32)],
        ),
        out_shape=[
            placed(BF16, blocks // 2 - 1, own, width),
            placed(BF16, blocks // 2, own, width),
            placed(F32, own, width),
            shaped(BF16, halves, depth, LANES),
            shaped(BF16, halves, depth, LANES),
        ],
        compiler_params=parameters(36),
        cost_estimate=cost(5 * total * width * width, 8 * total * width + 12 * width * width, total),
        name="first_norm",
    )(near, far(d_key), far(d_value), d_query, rows_all, flags, vectors, weights, d_middle, sums, gbias, qsum, vsum, *after)


def after(value, *others):
    return lax.optimization_barrier((value, *others))[0]


class Links:
    def __init__(self, seq, rows):
        self.sizes = {"seq": seq, "rows": rows}
        order = []
        for axis in EVERY:
            mask = self.sizes[axis] // 2
            while mask:
                order.append((axis, mask))
                mask //= 2
        self.order = order
        place = {axis: lax.axis_index(axis) for axis in EVERY}
        self.value = {(a, m): ((place[a] // m) % 2).astype(jnp.int32) for a, m in order}
        self.near = ("seq", 1)
        self.first = ("seq", 2)
        self.second = ("rows", 1)
        self.others = [b for b in order if b[0] == "rows" and b[1] > 1]

    def swap(self, array, bit):
        axis, mask = bit
        return lax.ppermute(array, axis, [(i, i ^ mask) for i in range(self.sizes[axis])])

    def pick(self, array, bit, other=False, axis=0):
        at = 1 - self.value[bit] if other else self.value[bit]
        return lax.dynamic_index_in_dim(array, at, axis, keepdims=False)

    def gather(self, shard, bits, wanted):
        held, have = shard, []
        for i, bit in enumerate(bits):
            if i in wanted:
                held = after(held, *wanted[i])
            have = sorted([*have, bit], key=self.order.index)
            parts = held.reshape(2 ** have.index(bit), -1, held.shape[-1])
            other = self.swap(held, bit).reshape(parts.shape)
            upper = self.value[bit] == 1
            low = jnp.where(upper, other, parts)
            high = jnp.where(upper, parts, other)
            held = jnp.stack([low, high], axis=1).reshape(-1, held.shape[-1])
        return held

    def half(self, held, have, bit, other):
        before = 1
        for key in have[: have.index(bit)]:
            before *= key if isinstance(key, int) else 2
        parts = held.reshape(before, 2, -1, held.shape[-1])
        return self.pick(parts, bit, other, 1).reshape(-1, held.shape[-1])

    def add(self, kept, came, have, bit):
        def part(other):
            first, second = (self.half(a, have, bit, other) for a in (kept, came))
            return (first.astype(F32) + second.astype(F32)).astype(BF16)

        return part(True), part(False), [b for b in have if b != bit]


def body(
    patches, segments, masked, mask_embedding, norm1_gain, norm1_bias, qkv_weight, query_bias,
    value_bias, out_weight, out_bias, norm2_gain, norm2_bias, up_weight, up_bias, down_weight,
    down_bias, cotangent, *, seq, rows,
):
    links = Links(seq, rows)
    row_count, patch_count, width = patches.shape
    tokens = row_count * patch_count
    n = qkv_weight.shape[0]
    devices = seq * rows
    groups = up_weight.shape[1] // width
    mine = groups // 2
    half = width // 2
    halves = seq // 2
    depth = rows * n
    near, first, second, others = links.near, links.first, links.second, links.others
    near_place = links.value[near].reshape(1)

    packed = jnp.stack(
        [
            down_weight.reshape(2, mine, n, width),
            up_weight.reshape(n, devices, groups, n).transpose(2, 0, 1, 3).reshape(2, mine, n, width),
        ],
        axis=1,
    ).reshape(2, 2 * mine, n, width)
    packed_kept, packed_sent = links.pick(packed, near), links.pick(packed, near, True)
    packed_came = links.swap(packed_sent, near)

    flags = (segments + MASKED * masked).astype(BF16).reshape(1, row_count, patch_count)
    sources = [after(patches.reshape(tokens, width), packed_sent)]
    for bit in (first, near):
        flags = jnp.concatenate([flags, links.swap(flags, bit)], axis=0)
        sources += [links.swap(source, bit) for source in sources]
    early_ones, late_ones = [sources[1], flags], sources[2:]
    flags = flags.astype(F32).reshape(seq, row_count, 1, patch_count)
    small = [
        mask_embedding, norm1_gain, norm1_bias, query_bias, value_bias, out_bias, norm2_gain,
        norm2_bias, down_bias,
    ]
    columns = jnp.concatenate([jnp.stack(small), up_bias.reshape(groups, n)], axis=0).T
    columns = jnp.pad(columns, ((0, 0), (0, LANES - columns.shape[1])))
    fourths = [qkv_weight[:, i * half : (i + 1) * half] for i in range(6)]
    fourths += [out_weight[:, :half], out_weight[:, half:]]
    left = jnp.concatenate(fourths[::2], axis=1)
    right = jnp.concatenate([*fourths[1::2], columns], axis=1)
    left = links.gather(left, [*others, second, first], {2: early_ones, 3: late_ones}).reshape(halves, depth, -1)
    right = links.gather(right, [*others, first, second], {}).reshape(halves, depth, -1)
    left_other, right_other = links.swap(left, near), links.swap(right, near)

    low = links.value[near] == 0
    packed = jnp.stack([jnp.where(low, packed_kept, packed_came), jnp.where(low, packed_came, packed_kept)], axis=0)
    same_core = [
        [(x * 2 + core) * rows + r for x in range(halves) for r in range(rows)] for core in range(2)
    ]
    rest = lax.all_gather(packed, EVERY, axis=2, tiled=True, axis_index_groups=same_core)

    rows_all, turned, queries, key_values, weights, vectors = project(
        near_place, sources, flags, left, left_other, right, right_other
    )
    queries = queries.reshape(row_count, patch_count, width)
    key_values = key_values.reshape(seq, row_count, patch_count, 2 * width)
    mixed, mixed_full, lse = attend(queries, key_values, flags)
    mixed = mixed.reshape(tokens, width)
    d_branch = cotangent.reshape(tokens, width)
    d_branch_other = links.swap(d_branch, near)
    normed_two, middle = open_branch(mixed, rows_all, flags, vectors, weights)
    places = jnp.stack([links.value[near], links.value[first]])
    added, d_normed, away, down_sent, down_kept, grad_up, grad_up_bias = branch(
        places, normed_two, links.swap(normed_two, near), d_branch, d_branch_other, vectors, rest
    )

    row_bits = [*others, second]
    have = [first, *row_bits]
    flat = lambda held: held.reshape(-1, held.shape[-1])
    down_sent, down_kept = flat(down_sent), flat(down_kept)
    up_order = [mine, first, near, *row_bits]
    grad_up = flat(grad_up)
    up_sent = links.half(grad_up, up_order, second, True)
    up_kept = links.half(grad_up, up_order, second, False)
    up_order = [mine, first, near, *others]
    away = links.swap(away, near)
    down_came, up_came = links.swap(down_sent, first), links.swap(up_sent, second)
    d_middle, d_mixed, out_sent, out_kept, sums = between(
        near_place, d_normed, away, middle, d_branch, vectors, mixed, weights, halves
    )
    out_came = links.swap(out_sent, near)
    d_mixed = d_mixed.reshape(row_count, patch_count, width)

    given = (queries, key_values, d_mixed, mixed_full, lse, flags)
    d_query, d_key, d_value, query_sums, value_sums = attend_back(*given, [down_sent, up_sent])

    down_sent, down_kept, down_order = links.add(
        after(down_kept, d_query), down_came, [mine, near, *row_bits], second
    )
    down_came = links.swap(down_sent, second)
    up_sent, up_kept, up_order = links.add(after(up_kept, down_sent), up_came, up_order, first)
    up_came = links.swap(up_sent, first)
    d_query = d_query.reshape(tokens, width)
    d_key = d_key.reshape(-1, width)
    d_value = d_value.reshape(-1, width)
    pair_sent, pair_kept, value_sent, value_kept = weight_grads(
        near_place, turned, d_key, d_value, d_query, halves, [down_sent, up_sent]
    )
    output = after(middle, pair_sent) + added + away[0].astype(F32) + vectors[DBIAS]
    output = output.astype(BF16)
    early_kept = jnp.concatenate([after(down_kept, output), up_kept], axis=0)
    early_came = jnp.concatenate([after(down_came, output), up_came], axis=0)
    early_order = [2 * mine, near, *others]
    early_sent, early_kept, early_order = links.add(early_kept, early_came, early_order, others[-1])
    early = [early_kept, links.swap(early_sent, others[-1]), early_order]
    pair_came = links.swap(flat(after(pair_sent, early_sent)), near)
    value_came = links.swap(flat(after(value_sent, early_sent)), near)
    pair_sent, pair_kept, pair_order = links.add(flat(pair_kept), pair_came, have, second)
    pair_came = links.swap(pair_sent, second)
    last_kept = jnp.concatenate([flat(value_kept), flat(out_kept)], axis=1)
    last_came = jnp.concatenate([value_came, flat(out_came)], axis=1)
    last_sent, last_kept, last_order = links.add(after(last_kept, pair_sent), last_came, have, first)
    last_came = links.swap(last_sent, first)
    far_share, near_share, own, small_sent, small_kept = first_norm(
        near_place, d_key, d_value, d_query, rows_all, flags, vectors, weights, d_middle, sums,
        grad_up_bias, query_sums, value_sums, halves, [early_sent, pair_sent, last_sent],
    )

    pair = [pair_kept, pair_came, pair_order]
    last = [last_kept, last_came, last_order]

    def go(item, bit, gone):
        gone, item[0], item[2] = links.add(after(item[0], gone), item[1], item[2], bit)
        item[1] = links.swap(gone, bit)
        return gone

    rest_bits = others[-2::-1]
    gone = own
    for bit in rest_bits:
        gone = go(early, bit, gone)
    pair_sent, pair[0], pair[2] = links.add(after(pair[0], gone), pair[1], pair[2], first)
    gone = pair_sent
    gone = go(last, second, gone)
    near_share = links.swap(after(near_share, gone), near)
    small = [flat(small_kept), links.swap(flat(after(small_sent, gone)), near), have]
    gone = go(small, first, gone)
    pair[1] = links.swap(after(pair_sent, gone), first)
    gone = (after(far_share, gone).astype(F32) + near_share[1:].astype(F32)).astype(BF16)
    far_share = links.swap(gone, first)
    gone = go(small, second, gone)
    last[0] = jnp.concatenate([after(pair[0], gone), last[0], small[0]], axis=1)
    last[1] = jnp.concatenate([pair[1], last[1], small[1]], axis=1)
    gone = go(last, others[-1], gone)
    low = links.value[near] == 0
    early_sum = after(early[0], gone).astype(F32) + early[1].astype(F32)
    early_sum = early_sum.reshape(2 * mine, 2, n, width)
    far_sum = links.pick(early_sum, near, True, 1).astype(BF16)
    far_sum = links.swap(far_sum, near).astype(F32)
    early_sum = links.pick(early_sum, near, False, 1)
    for bit in rest_bits:
        gone = go(last, bit, gone)
    early_sum = after(early_sum, gone)
    joined = jnp.stack(
        [jnp.where(low, early_sum, far_sum), jnp.where(low, far_sum, early_sum)], axis=0
    )
    down_sum = joined[:, :mine].reshape(-1, width)
    up_sum = joined[:, mine:].reshape(groups, n, devices, n)
    up_sum = up_sum.transpose(1, 2, 0, 3).reshape(n, -1)
    input_grad = after(own, up_sum) + near_share[0].astype(F32) + far_share[0].astype(F32)
    is_masked = masked.reshape(tokens, 1) == 1
    input_grad = jnp.where(is_masked, 0.0, input_grad)
    last = after(last[0], input_grad).astype(F32) + last[1].astype(F32)
    project_sum, out_sum = last[:, : 3 * width], last[:, 3 * width : 4 * width]
    tail = last[:, 4 * width :].T
    shape = (row_count, patch_count, width)
    return (
        output.reshape(shape), input_grad.reshape(shape), tail[EMBED], tail[GAIN1], tail[SHIFT1],
        project_sum, tail[QBIAS], tail[VBIAS], out_sum, tail[OBIAS], tail[GAIN2], tail[SHIFT2],
        up_sum, tail[UBIAS : UBIAS + groups].reshape(-1), down_sum, tail[DBIAS],
    )


def solution(mesh):
    one, two = P(EVERY), P(EVERY, None)
    rows, flags = P("rows", "seq", None), P("rows", "seq")
    seq, row_groups = mesh.shape["seq"], mesh.shape["rows"]

    def run(*arguments):
        return body(*arguments, seq=seq, rows=row_groups)

    return jax.shard_map(
        run,
        mesh=mesh,
        in_specs=(
            rows, flags, flags, one, one, one, two, one, one, two, one, one, one, two, one, two,
            one, rows,
        ),
        out_specs=(
            rows, rows, one, one, one, two, one, one, two, one, one, one, two, one, two, one,
        ),
        check_vma=False,
    )
```

```python
import jax
import jax.numpy as jnp
from jax import lax
from jax.experimental import pallas as pl
from jax.experimental.pallas import tpu as pltpu
from jax.sharding import PartitionSpec as P

HEAD_SIZE = 64
LANES = 128
CHUNK = 256
PAIRS = 6
MASKED = 16
EPSILON = 1e-06
FLOOR_SCORE = -1e30
HALF_ROOT = 0.7071067811865476
MIB = 2**20
EVERY = ("seq", "rows")
BF16 = jnp.bfloat16
F32 = jnp.float32
EMBED, GAIN1, SHIFT1, QBIAS, VBIAS, OBIAS, GAIN2, SHIFT2, DBIAS, UBIAS = range(10)
KINDS = 16


def dot(left, right, left_dim, right_dim):
    return lax.dot_general(
        left, right, (((left_dim,), (right_dim,)), ((), ())), preferred_element_type=F32
    )


def column(row):
    return jnp.broadcast_to(row, (8, row.shape[1])).T[:, :1]


def segment_of(flags):
    return flags - jnp.where(flags >= MASKED, float(MASKED), 0.0)


def norm_parts(values):
    mean = jnp.mean(values, axis=-1, keepdims=True)
    centered = values - mean
    rate = lax.rsqrt(jnp.mean(centered * centered, axis=-1, keepdims=True) + EPSILON)
    return centered * rate, rate


def norm_back(pulled, hat, rate):
    first = jnp.mean(pulled, axis=-1, keepdims=True)
    second = jnp.mean(pulled * hat, axis=-1, keepdims=True)
    return rate * (pulled - first - hat * second)


def parted(value, mine, depth):
    sent, kept = [], []
    for x in range(value.shape[0] // (2 * depth)):
        low = value[2 * x * depth : (2 * x + 1) * depth]
        high = value[(2 * x + 1) * depth : (2 * x + 2) * depth]
        sent.append(jnp.where(mine == 0, high, low))
        kept.append(jnp.where(mine == 0, low, high))
    return sent, kept


def whole(*shape):
    return pl.BlockSpec(shape, lambda *_: (0,) * len(shape))


ANYWHERE = pl.BlockSpec(memory_space=pl.ANY)


def shaped(dtype, *shape):
    return jax.ShapeDtypeStruct(shape, dtype)


def placed(dtype, *shape):
    return pltpu.HBM(shape, dtype)


def far(array):
    return pltpu.with_memory_space_constraint(array, pltpu.HBM)


def parameters(mib=32):
    return pltpu.CompilerParams(vmem_limit_bytes=mib * MIB)


def cost(flops, nbytes, transcendentals=0):
    return pl.CostEstimate(flops=flops, bytes_accessed=nbytes, transcendentals=transcendentals)


def split_heads(pair):
    lane = lax.broadcasted_iota(jnp.int32, pair.shape, 1)
    zero = jnp.zeros_like(pair)
    return jnp.concatenate(
        [jnp.where(lane < HEAD_SIZE, pair, zero), jnp.where(lane < HEAD_SIZE, zero, pair)], axis=0
    )


def join_heads(both, count):
    row = lax.broadcasted_iota(jnp.int32, (both.shape[0], count), 0)
    return jnp.where(row < HEAD_SIZE, both[:, :count], both[:, count:]).T


def set_bias(flags_ref, bias):
    blocks, size = flags_ref.shape[0], flags_ref.shape[3]
    asked = segment_of(flags_ref[0, 0])
    for j in range(blocks):
        keys = column(segment_of(flags_ref[j, 0]))
        bias[pl.ds(j * size, size), :] = jnp.where((keys == asked) & (keys > 0.0), 0.0, FLOOR_SCORE)


def attend_kernel(q_ref, k_ref, v_ref, flags_ref, mix_ref, full_ref, lse_ref, bias, held):
    count, blocks, size = q_ref.shape[1], k_ref.shape[0], k_ref.shape[2]

    @pl.when(pl.program_id(1) == 0)
    def _():
        set_bias(flags_ref, bias)

    live = segment_of(flags_ref[0, 0]) > 0.0
    live = jnp.concatenate([live, live], axis=1)
    for u in range(PAIRS):
        lanes = slice(u * LANES, (u + 1) * LANES)
        asked = split_heads(q_ref[0, :, lanes])
        top = None
        for j in range(blocks):
            rows = pl.ds(j * size, size)
            part = bias[rows, :]
            scores = dot(k_ref[j, 0, :, lanes], asked, 1, 1) + jnp.concatenate([part, part], axis=1)
            held[u % 2, rows, :] = scores
            high = jnp.max(scores, axis=0, keepdims=True)
            top = high if top is None else jnp.maximum(top, high)
        total, mixed = 0.0, 0.0
        for j in range(blocks):
            weights = jnp.exp(held[u % 2, pl.ds(j * size, size), :] - top)
            total = total + jnp.sum(weights, axis=0, keepdims=True)
            mixed = mixed + dot(v_ref[j, 0, :, lanes].T, weights.astype(BF16), 1, 0)
        result = join_heads(mixed * jnp.where(live, 1.0 / total, 0.0), count)
        mix_ref[0, :, lanes] = result.astype(BF16)
        full_ref[0, :, lanes] = result
        lse_ref[0, u] = jnp.where(live, top + jnp.log(total), 0.0)


def attend_back_kernel(
    q_ref, k_ref, v_ref, dm_ref, full_ref, lse_ref, flags_ref,
    dq_ref, dk_ref, dv_ref, qsum_ref, vsum_ref, bias,
):
    count, blocks, size = q_ref.shape[1], k_ref.shape[0], k_ref.shape[2]

    set_bias(flags_ref, bias)
    for u in range(q_ref.shape[2] // LANES):
        lanes = slice(u * LANES, (u + 1) * LANES)
        d_mixed = dm_ref[0, :, lanes]
        asked, pulled = split_heads(q_ref[0, :, lanes]), split_heads(d_mixed)
        product = (d_mixed.astype(F32) * full_ref[0, :, lanes]).T
        delta = jnp.concatenate(
            [
                jnp.sum(product[:HEAD_SIZE], axis=0, keepdims=True),
                jnp.sum(product[HEAD_SIZE:], axis=0, keepdims=True),
            ],
            axis=1,
        )
        lse = lse_ref[0, u]
        d_query, v_sum = 0.0, 0.0
        for j in range(blocks):
            keys = k_ref[j, 0, :, lanes]
            part = bias[pl.ds(j * size, size), :]
            scores = dot(keys, asked, 1, 1) + jnp.concatenate([part, part], axis=1)
            probs = jnp.exp(scores - lse)
            d_probs = dot(v_ref[j, 0, :, lanes], pulled, 1, 1)
            d_scores = (probs * (d_probs - delta)).astype(BF16)
            d_value = dot(probs.astype(BF16), pulled, 1, 0)
            dv_ref[j, 0, :, lanes] = d_value.astype(BF16)
            dk_ref[j, 0, :, lanes] = dot(d_scores, asked, 1, 0).astype(BF16)
            v_sum = v_sum + jnp.sum(d_value, axis=0, keepdims=True)
            d_query = d_query + dot(keys.T, d_scores, 1, 0)
        d_query = join_heads(d_query, count) * HEAD_SIZE**-0.5
        dq_ref[0, :, lanes] = d_query.astype(BF16)
        qsum_ref[0, u] = jnp.sum(d_query, axis=0, keepdims=True)
        vsum_ref[0, u] = v_sum


def attend(queries, key_values, flags):
    rows, count, width = queries.shape
    blocks, _, size, _ = key_values.shape
    pairs = width // LANES
    tile = pl.BlockSpec((1, count, PAIRS * LANES), lambda r, p: (r, 0, p))
    steps = pairs // PAIRS
    area = rows * count * blocks * size
    return pl.pallas_call(
        attend_kernel,
        grid=(rows, steps),
        in_specs=[
            tile,
            pl.BlockSpec((blocks, 1, size, PAIRS * LANES), lambda r, p: (0, r, 0, p)),
            pl.BlockSpec((blocks, 1, size, PAIRS * LANES), lambda r, p: (0, r, 0, steps + p)),
            pl.BlockSpec((blocks, 1, 1, size), lambda r, p: (0, r, 0, 0)),
        ],
        out_specs=[tile, tile, pl.BlockSpec((1, PAIRS, 1, 2 * count), lambda r, p: (r, p, 0, 0))],
        out_shape=[
            shaped(BF16, *queries.shape),
            placed(F32, *queries.shape),
            shaped(F32, rows, pairs, 1, 2 * count),
        ],
        scratch_shapes=[
            pltpu.VMEM((blocks * size, count), F32),
            pltpu.VMEM((2, blocks * size, 2 * count), F32),
        ],
        compiler_params=parameters(),
        cost_estimate=cost(16 * area * width, 8 * rows * blocks * size * width, area * 12),
        name="attend",
    )(far(queries), far(key_values), far(key_values), flags)


def attend_back(queries, key_values, d_mixed, mixed_full, lse, flags, after):
    rows, count, width = queries.shape
    blocks, _, size, _ = key_values.shape
    pairs = width // LANES
    tile = pl.BlockSpec((1, count, width), lambda r: (r, 0, 0))
    keys = pl.BlockSpec((blocks, 1, size, width), lambda r: (0, r, 0, 0))
    line = lambda w: pl.BlockSpec((1, pairs, 1, w), lambda r: (r, 0, 0, 0))
    area = rows * count * blocks * size
    grads = placed(BF16, blocks, rows, size, width)
    sums = shaped(F32, rows, pairs, 1, LANES)
    given = [queries, key_values, key_values, d_mixed, mixed_full, lse, flags]

    def kernel(*refs):
        attend_back_kernel(*refs[: len(given)], *refs[len(given) + len(after) :])

    return pl.pallas_call(
        kernel,
        grid=(rows,),
        in_specs=[
            tile, keys, pl.BlockSpec((blocks, 1, size, width), lambda r: (0, r, 0, 1)), tile, tile,
            line(2 * count), pl.BlockSpec((blocks, 1, 1, size), lambda r: (0, r, 0, 0)),
            *[ANYWHERE] * len(after),
        ],
        out_specs=[tile, keys, keys, line(LANES), line(LANES)],
        out_shape=[placed(BF16, *queries.shape), grads, grads, sums, sums],
        scratch_shapes=[pltpu.VMEM((blocks * size, count), F32)],
        compiler_params=parameters(40),
        cost_estimate=cost(32 * area * width, 16 * rows * blocks * size * width, area * 12),
        name="attend_back",
    )(*given, *after)


def project(near, sources, flags, left, left_other, right, right_other):
    own, width = sources[0].shape
    blocks, row_count, _, size = flags.shape
    total, steps = own * blocks, blocks
    halves, depth, part = left.shape
    half = width // 2

    def kernel(near_ref, *refs):
        first_ref, ahead_ref, lm_ref, lo_ref, rm_ref, ro_ref = refs[blocks : blocks + 6]
        rows_out, turned_ref, q_ref, kv_ref, w_out, vec_ref = refs[blocks + 6 : blocks + 12]
        rows, weights, normed, columns, sems, out_sems = refs[blocks + 12 :]
        step = pl.program_id(0)
        outward = [
            pltpu.make_async_copy(rows, rows_out, out_sems.at[0]),
            pltpu.make_async_copy(weights, w_out, out_sems.at[1]),
        ]

        def norm(at, slot, flags_ref):
            gain, shift = vec_ref[GAIN1 : GAIN1 + 1], vec_ref[SHIFT1 : SHIFT1 + 1]
            embed = vec_ref[EMBED : EMBED + 1]
            for r in range(row_count):
                masked = column(flags_ref[0, r]) >= MASKED
                here = rows[pl.ds(pl.multiple_of(at * own + r * size, size), size), :].astype(F32)
                hat, _ = norm_parts(jnp.where(masked, embed, here))
                normed[slot, r * size : (r + 1) * size, :] = (hat * gain + shift).astype(BF16)

        @pl.when(step == 0)
        def _():
            near_place = near_ref[0]
            later, first = [], []
            for which in range(2):
                mine = near_place if which == 0 else 1 - near_place
                low, high = (lm_ref, rm_ref) if which == 0 else (lo_ref, ro_ref)
                for x in range(halves):
                    at = pl.ds(pl.multiple_of(x * 2 * depth + mine * depth, depth), depth)
                    first.append((high.at[x, :, pl.ds(part, LANES)], columns.at[at, :]))
                    for side, source in enumerate((low, high)):
                        for kind in range(4):
                            later.append(
                                (
                                    source.at[x, :, pl.ds(kind * half, half)],
                                    weights.at[at, pl.ds(kind * width + side * half, half)],
                                )
                            )
            first.append((refs[0], rows.at[pl.ds(0, own), :]))
            later += [(refs[i], rows.at[pl.ds(i * own, own), :]) for i in range(1, blocks)]
            copies = [
                pltpu.make_async_copy(a, b, sems.at[i]) for i, (a, b) in enumerate([*first, *later])
            ]
            for copy in copies:
                copy.start()
            for copy in copies[: len(first)]:
                copy.wait()
            vec_ref[...] = columns[...].astype(F32).T[:KINDS]
            norm(0, 0, first_ref)
            for copy in copies[len(first) :]:
                copy.wait()
            for copy in outward:
                copy.start()

        slot = lax.rem(step, 2)
        here = normed[slot]
        kv_ref[:, :width] = dot(here, weights[:, width : 2 * width], 1, 0).astype(BF16)
        values = dot(here, weights[:, 2 * width : 3 * width], 1, 0)
        kv_ref[:, width:] = (values + vec_ref[VBIAS : VBIAS + 1]).astype(BF16)
        turned_ref[...] = here.T
        norm(jnp.minimum(step + 1, steps - 1), 1 - slot, ahead_ref)

        @pl.when(step == 0)
        def _():
            asked = dot(here, weights[:, :width], 1, 0) + vec_ref[QBIAS : QBIAS + 1]
            q_ref[...] = (asked * HEAD_SIZE**-0.5).astype(BF16)

        @pl.when(step == steps - 1)
        def _():
            for copy in outward:
                copy.wait()

    def ahead(t, _):
        return (jnp.minimum(t + 1, steps - 1), 0, 0, 0)

    return pl.pallas_call(
        kernel,
        grid_spec=pltpu.PrefetchScalarGridSpec(
            num_scalar_prefetch=1,
            grid=(steps,),
            in_specs=[
                *[ANYWHERE] * blocks,
                whole(1, row_count, 1, size),
                pl.BlockSpec((1, row_count, 1, size), ahead),
                *[ANYWHERE] * 4,
            ],
            out_specs=[
                ANYWHERE,
                pl.BlockSpec((width, own), lambda t, _: (0, t)),
                whole(own, width),
                pl.BlockSpec((own, 2 * width), lambda t, _: (t, 0)),
                ANYWHERE,
                whole(KINDS, width),
            ],
            scratch_shapes=[
                pltpu.VMEM((total, width), BF16),
                pltpu.VMEM((width, 4 * width), BF16),
                pltpu.VMEM((2, own, width), BF16),
                pltpu.VMEM((width, LANES), BF16),
                pltpu.SemaphoreType.DMA((18 * halves + blocks,)),
                pltpu.SemaphoreType.DMA((2,)),
            ],
        ),
        out_shape=[
            placed(BF16, total, width),
            placed(BF16, width, total),
            placed(BF16, own, width),
            placed(BF16, total, 2 * width),
            placed(BF16, width, 4 * width),
            shaped(F32, KINDS, width),
        ],
        compiler_params=parameters(40),
        cost_estimate=cost(5 * total * width * width, 8 * total * width + 16 * width * width, total),
        name="project",
    )(near, *sources, flags, flags, left, left_other, right, right_other)


def open_branch(mixed, rows_all, flags, vectors, weights):
    tokens, width = mixed.shape
    _, row_count, _, size = flags.shape

    def kernel(mixed_ref, rows_ref, flags_ref, vec_ref, w_ref, normed_ref, middle_ref):
        masked = column(flags_ref[0, 0]) >= MASKED
        embed, bias = vec_ref[EMBED : EMBED + 1], vec_ref[OBIAS : OBIAS + 1]
        gain, shift = vec_ref[GAIN2 : GAIN2 + 1], vec_ref[SHIFT2 : SHIFT2 + 1]
        added = dot(mixed_ref[...], w_ref[...], 1, 0)
        for c in range(0, size, CHUNK):
            cut = slice(c, c + CHUNK)
            values = jnp.where(masked[cut], embed, rows_ref[cut].astype(F32))
            middle = values + added[cut] + bias
            middle_ref[cut] = middle
            hat, _ = norm_parts(middle)
            normed_ref[cut] = (hat * gain + shift).astype(BF16)

    tile = pl.BlockSpec((size, width), lambda t: (t, 0))
    return pl.pallas_call(
        kernel,
        grid=(row_count,),
        in_specs=[
            tile, tile, pl.BlockSpec((1, 1, 1, size), lambda t: (0, t, 0, 0)), whole(KINDS, width),
            pl.BlockSpec((width, width), lambda t: (0, 3)),
        ],
        out_specs=[tile, tile],
        out_shape=[placed(BF16, tokens, width), placed(F32, tokens, width)],
        compiler_params=parameters(),
        cost_estimate=cost(2 * tokens * width * width, 10 * tokens * width),
        name="open_branch",
    )(mixed, rows_all, flags, vectors, weights)


def branch(places, normed, normed_other, pulled, pulled_other, vectors, rest):
    tokens, width = normed.shape
    groups = rest.shape[1] // 2
    cores, length = rest.shape[0], rest.shape[2]
    depth = length // 2
    both = 2 * tokens
    size = both

    def kernel(
        places_ref, n_ref, no_ref, c_ref, co_ref, vec_ref, down_ref, up_ref,
        total_ref, dn_ref, away_ref, sdown_ref, kdown_ref, gup_ref, gbias_ref,
        normed_all, turned, pulled_all, totals, d_normed, activated, d_hidden, up, down, staged, sems,
    ):
        step = pl.program_id(0)

        @pl.when(step == 0)
        def _():
            normed_all[:tokens] = n_ref[...]
            normed_all[tokens:] = no_ref[...]
            turned[:, :tokens] = n_ref[...].T
            turned[:, tokens:] = no_ref[...].T
            pulled_all[:tokens] = c_ref[...]
            pulled_all[tokens:] = co_ref[...]

        at = 0
        for x in range(2):
            for core in range(cores):
                up[at : at + depth] = up_ref[core, 0, x * depth : (x + 1) * depth]
                down[at : at + depth] = down_ref[core, 0, x * depth : (x + 1) * depth]
                at += depth
        bias = vec_ref[pl.ds(UBIAS + groups * places_ref[0] + step, 1), :]
        bias_grad = 0.0
        for c in range(0, both, size):
            cut = slice(c, c + size)
            hidden = dot(normed_all[cut], up[...], 1, 0) + bias
            d_active = dot(pulled_all[cut], down[...], 1, 1)
            phi = 0.5 * (1.0 + lax.erf(hidden * HALF_ROOT))
            slope = phi + hidden * (0.3989422804014327 * jnp.exp(-0.5 * hidden * hidden))
            activated[cut] = (hidden * phi).astype(BF16)
            grad = (d_active * slope).astype(BF16)
            d_hidden[cut] = grad
            bias_grad += jnp.sum(grad.astype(F32), axis=0, keepdims=True)
        gbias_ref[0] = bias_grad
        for c in range(0, both, size):
            cut = slice(c, c + size)
            more = dot(activated[cut], down[...], 1, 0)
            more_back = dot(d_hidden[cut], up[...], 1, 1)

            @pl.when(step == 0)
            def _(cut=cut, more=more, more_back=more_back):
                totals[cut] = more
                d_normed[cut] = more_back

            @pl.when(step > 0)
            def _(cut=cut, more=more, more_back=more_back):
                totals[cut] += more
                d_normed[cut] += more_back

        last = step == pl.num_programs(0) - 1
        outward = [
            pltpu.make_async_copy(totals.at[pl.ds(0, tokens)], total_ref, sems.at[0]),
            pltpu.make_async_copy(d_normed.at[pl.ds(0, tokens)], dn_ref, sems.at[1]),
            pltpu.make_async_copy(staged, away_ref, sems.at[2]),
        ]

        @pl.when(last)
        def _():
            staged[0] = totals[tokens:].astype(BF16)
            staged[1] = d_normed[tokens:].astype(BF16)
            for copy in outward:
                copy.start()

        gup_ref[0] = dot(turned[...], d_hidden[...], 1, 0).astype(BF16)
        grads = dot(activated[...], pulled_all[...], 0, 0).astype(BF16)
        (sent,), (kept,) = parted(grads, places_ref[1], length)
        for core in range(cores):
            sdown_ref[0, core] = sent[core * depth : (core + 1) * depth]
            kdown_ref[0, core] = kept[core * depth : (core + 1) * depth]

        @pl.when(last)
        def _():
            for copy in outward:
                copy.wait()

    weight = lambda f: pl.BlockSpec((cores, 1, length, width), lambda k, _: (0, f(k), 0, 0))
    piece = pl.BlockSpec((1, cores, depth, width), lambda k, _: (k, 0, 0, 0))
    square = pl.BlockSpec((1, width, width), lambda k, _: (k, 0, 0))
    patch = whole(tokens, width)
    return pl.pallas_call(
        kernel,
        grid_spec=pltpu.PrefetchScalarGridSpec(
            num_scalar_prefetch=1,
            grid=(groups,),
            in_specs=[
                patch, patch, patch, patch, whole(KINDS, width), weight(lambda k: k),
                weight(lambda k: groups + k),
            ],
            out_specs=[
                ANYWHERE, ANYWHERE, ANYWHERE, piece, piece, square,
                pl.BlockSpec((1, 1, width), lambda k, _: (k, 0, 0)),
            ],
            scratch_shapes=[
                pltpu.VMEM((both, width), BF16),
                pltpu.VMEM((width, both), BF16),
                pltpu.VMEM((both, width), BF16),
                pltpu.VMEM((both, width), F32),
                pltpu.VMEM((both, width), F32),
                pltpu.VMEM((both, width), BF16),
                pltpu.VMEM((both, width), BF16),
                pltpu.VMEM((width, width), BF16),
                pltpu.VMEM((width, width), BF16),
                pltpu.VMEM((2, tokens, width), BF16),
                pltpu.SemaphoreType.DMA((3,)),
            ],
        ),
        out_shape=[
            placed(F32, tokens, width),
            placed(F32, tokens, width),
            placed(BF16, 2, tokens, width),
            placed(BF16, groups, cores, depth, width),
            placed(BF16, groups, cores, depth, width),
            placed(BF16, groups, width, width),
            shaped(F32, groups, 1, width),
        ],
        compiler_params=parameters(52),
        cost_estimate=cost(
            12 * groups * both * width * width, 20 * width * width, 2 * both * width * groups
        ),
        name="branch",
    )(places, far(normed), normed_other, pulled, pulled_other, vectors, rest, rest)


def between(near, d_normed, d_normed_other, middle, pulled, vectors, mixed, weights, halves):
    tokens, width = mixed.shape
    depth = width // (2 * halves)
    size = tokens // 2

    def kernel(
        near_ref, dn_ref, more_ref, middle_ref, cot_ref, vec_ref, mixed_ref, w_ref,
        dmiddle_ref, dmixed_ref, sent_ref, kept_ref, sums_ref, d_attn, grads,
    ):
        step = pl.program_id(0)
        gain = vec_ref[GAIN2 : GAIN2 + 1]
        sums = 0.0
        for c in range(0, size, CHUNK):
            cut = slice(c, c + CHUNK)
            d_out = dn_ref[cut] + more_ref[0, cut].astype(F32)
            cot = cot_ref[cut].astype(F32)
            hat, rate = norm_parts(middle_ref[cut])
            d_middle = cot + norm_back(d_out * gain, hat, rate)
            dmiddle_ref[cut] = d_middle
            low = d_middle.astype(BF16)
            d_attn[cut] = low
            parts = [low.astype(F32), d_out * hat, d_out, cot]
            sums += jnp.concatenate([jnp.sum(s, axis=0, keepdims=True) for s in parts], axis=0)
        sums = jnp.concatenate([sums, jnp.zeros_like(sums)], axis=0)
        dmixed_ref[...] = dot(d_attn[...], w_ref[...], 1, 1).astype(BF16)
        more = dot(mixed_ref[...], d_attn[...], 0, 0)

        @pl.when(step == 0)
        def _():
            sums_ref[...] = sums
            grads[...] = more

        @pl.when(step == 1)
        def _():
            sums_ref[...] += sums
            value = (grads[...] + more).astype(BF16)
            for x, (sent, kept) in enumerate(zip(*parted(value, near_ref[0], depth), strict=True)):
                sent_ref[x] = sent
                kept_ref[x] = kept

    tile = pl.BlockSpec((size, width), lambda t, _: (t, 0))
    piece = whole(halves, depth, width)
    return pl.pallas_call(
        kernel,
        grid_spec=pltpu.PrefetchScalarGridSpec(
            num_scalar_prefetch=1,
            grid=(2,),
            in_specs=[
                tile, pl.BlockSpec((1, size, width), lambda t, _: (1, t, 0)), tile, tile,
                whole(KINDS, width), tile, pl.BlockSpec((width, width), lambda t, _: (0, 3)),
            ],
            out_specs=[tile, tile, piece, piece, whole(8, width)],
            scratch_shapes=[pltpu.VMEM((size, width), BF16), pltpu.VMEM((width, width), F32)],
        ),
        out_shape=[
            placed(F32, tokens, width),
            shaped(BF16, tokens, width),
            placed(BF16, halves, depth, width),
            placed(BF16, halves, depth, width),
            shaped(F32, 8, width),
        ],
        compiler_params=parameters(),
        cost_estimate=cost(4 * tokens * width * width, 16 * tokens * width),
        name="between",
    )(near, d_normed, d_normed_other, middle, pulled, vectors, mixed, far(weights))


def weight_grads(near, turned, d_key, d_value, d_query, halves, after):
    width, total = turned.shape
    own = d_query.shape[0]
    depth = width // (2 * halves)

    def kernel(near_ref, turned_ref, dk_ref, dv_ref, dq_ref, *refs):
        sa_ref, ka_ref, sb_ref, kb_ref = refs[len(after) :]
        step = pl.program_id(0)

        def put(value, sent_ref, kept_ref, at):
            pieces = zip(*parted(value.astype(BF16), near_ref[0], depth), strict=True)
            for x, (sent, kept) in enumerate(pieces):
                sent_ref[x, :, at : at + width] = sent
                kept_ref[x, :, at : at + width] = kept

        @pl.when(step == 0)
        def _():
            put(dot(turned_ref[:, :own], dq_ref[...], 1, 0), sa_ref, ka_ref, 0)

        @pl.when(step == 1)
        def _():
            put(dot(turned_ref[...], dk_ref[...], 1, 0), sa_ref, ka_ref, width)

        @pl.when(step == 2)
        def _():
            put(dot(turned_ref[...], dv_ref[...], 1, 0), sb_ref, kb_ref, 0)

    pair, single = whole(halves, depth, 2 * width), whole(halves, depth, width)
    return pl.pallas_call(
        kernel,
        grid_spec=pltpu.PrefetchScalarGridSpec(
            num_scalar_prefetch=1,
            grid=(3,),
            in_specs=[
                whole(width, total), whole(total, width), whole(total, width), whole(own, width),
                *[ANYWHERE] * len(after),
            ],
            out_specs=[pair, pair, single, single],
        ),
        out_shape=[
            placed(BF16, halves, depth, 2 * width),
            placed(BF16, halves, depth, 2 * width),
            placed(BF16, halves, depth, width),
            placed(BF16, halves, depth, width),
        ],
        compiler_params=parameters(36),
        cost_estimate=cost(5 * total * width * width, 8 * total * width + 12 * width * width),
        name="weight_grads",
    )(near, turned, d_key, d_value, d_query, *after)


def first_norm(
    near, d_key, d_value, d_query, rows_all, flags, vectors, weights, d_middle, sums, gbias, qsum, vsum, halves, after,
):
    total, width = rows_all.shape
    blocks, row_count, _, size = flags.shape
    own = d_query.shape[0]
    depth = width // (2 * halves)
    groups = gbias.shape[0]

    def kernel(near_ref, *refs):
        (
            dk_ref, dv_ref, dq_ref, rows_ref, flags_ref, vec_ref, w_ref, dmiddle_ref, sums_ref,
            gbias_ref, qsum_ref, vsum_ref,
        ) = refs[:12]
        far_ref, near_share_ref, own_ref, sent_ref, kept_ref, totals = refs[12 + len(after) :]
        step = pl.program_id(0)

        def put_share(step, cut, value):
            @pl.when(step < blocks // 2)
            def _():
                far_ref[0, cut] = value

            @pl.when(step >= blocks // 2)
            def _():
                near_share_ref[0, cut] = value

        def one(mine):
            d_all = dot(dk_ref[...], w_ref[:, width : 2 * width], 1, 1)
            d_all += dot(dv_ref[...], w_ref[:, 2 * width :], 1, 1)
            if mine:
                d_all += dot(dq_ref[...], w_ref[:, :width], 1, 1)
            gain, embed = vec_ref[GAIN1 : GAIN1 + 1], vec_ref[EMBED : EMBED + 1]
            more = 0.0
            for r in range(row_count):
                cut = slice(r * size, (r + 1) * size)
                masked = column(flags_ref[0, r]) >= MASKED
                d_normed = d_all[cut]
                hat, rate = norm_parts(jnp.where(masked, embed, rows_ref[cut].astype(F32)))
                d_embedded = norm_back(d_normed * gain, hat, rate)
                if mine:
                    d_embedded = d_embedded + dmiddle_ref[cut]
                    own_ref[cut] = d_embedded
                else:
                    put_share(step, cut, d_embedded.astype(BF16))
                parts = [jnp.where(masked, d_embedded, 0.0), d_normed * hat, d_normed]
                more += jnp.concatenate([jnp.sum(s, axis=0, keepdims=True) for s in parts], axis=0)
            return more

        @pl.when(step == 0)
        def _():
            totals[:3] = one(True)

        @pl.when(step > 0)
        def _():
            totals[:3] += one(False)

        @pl.when(step == blocks - 1)
        def _():
            def line(ref):
                rows, pairs = ref.shape[0], ref.shape[1]
                return sum(
                    jnp.concatenate([ref[r, p] for p in range(pairs)], axis=1) for r in range(rows)
                )

            bias = jnp.concatenate([gbias_ref[k] for k in range(groups)], axis=0)
            none = jnp.zeros_like(bias)
            low = near_ref[0] == 0
            kinds = [
                totals[:3], line(qsum_ref), line(vsum_ref), sums_ref[:4],
                jnp.where(low, bias, none), jnp.where(low, none, bias),
            ]
            kinds.append(jnp.zeros((LANES - UBIAS - 2 * groups, width), F32))
            small = jnp.concatenate(kinds, axis=0).T.astype(BF16)
            for x, (sent, kept) in enumerate(zip(*parted(small, near_ref[0], depth), strict=True)):
                sent_ref[x] = sent
                kept_ref[x] = kept

    tile = pl.BlockSpec((own, width), lambda t, _: (t, 0))
    piece = whole(halves, depth, LANES)
    return pl.pallas_call(
        kernel,
        grid_spec=pltpu.PrefetchScalarGridSpec(
            num_scalar_prefetch=1,
            grid=(blocks,),
            in_specs=[
                tile, tile, whole(own, width), tile,
                pl.BlockSpec((1, row_count, 1, size), lambda t, _: (t, 0, 0, 0)),
                whole(KINDS, width), whole(width, 3 * width), whole(own, width),
                whole(*sums.shape), whole(*gbias.shape), whole(*qsum.shape), whole(*vsum.shape),
                *[ANYWHERE] * len(after),
            ],
            out_specs=[
                pl.BlockSpec((1, own, width), lambda t, _: (jnp.clip(t - 1, 0, blocks // 2 - 2), 0, 0)),
                pl.BlockSpec((1, own, width), lambda t, _: (jnp.maximum(t - blocks // 2, 0), 0, 0)),
                whole(own, width), piece, piece,
            ],
            scratch_shapes=[pltpu.VMEM((8, width), F32)],
        ),
        out_shape=[
            placed(BF16, blocks // 2 - 1, own, width),
            placed(BF16, blocks // 2, own, width),
            placed(F32, own, width),
            shaped(BF16, halves, depth, LANES),
            shaped(BF16, halves, depth, LANES),
        ],
        compiler_params=parameters(36),
        cost_estimate=cost(5 * total * width * width, 8 * total * width + 12 * width * width, total),
        name="first_norm",
    )(near, far(d_key), far(d_value), d_query, rows_all, flags, vectors, weights, d_middle, sums, gbias, qsum, vsum, *after)


def after(value, *others):
    return lax.optimization_barrier((value, *others))[0]


class Links:
    def __init__(self, seq, rows):
        self.sizes = {"seq": seq, "rows": rows}
        order = []
        for axis in EVERY:
            mask = self.sizes[axis] // 2
            while mask:
                order.append((axis, mask))
                mask //= 2
        self.order = order
        place = {axis: lax.axis_index(axis) for axis in EVERY}
        self.value = {(a, m): ((place[a] // m) % 2).astype(jnp.int32) for a, m in order}
        self.near = ("seq", 1)
        self.first = ("seq", 2)
        self.second = ("rows", 1)
        self.others = [b for b in order if b[0] == "rows" and b[1] > 1]

    def swap(self, array, bit):
        axis, mask = bit
        return lax.ppermute(array, axis, [(i, i ^ mask) for i in range(self.sizes[axis])])

    def pick(self, array, bit, other=False, axis=0):
        at = 1 - self.value[bit] if other else self.value[bit]
        return lax.dynamic_index_in_dim(array, at, axis, keepdims=False)

    def gather(self, shard, bits, wanted):
        held, have = shard, []
        for i, bit in enumerate(bits):
            if i in wanted:
                held = after(held, *wanted[i])
            have = sorted([*have, bit], key=self.order.index)
            parts = held.reshape(2 ** have.index(bit), -1, held.shape[-1])
            other = self.swap(held, bit).reshape(parts.shape)
            upper = self.value[bit] == 1
            low = jnp.where(upper, other, parts)
            high = jnp.where(upper, parts, other)
            held = jnp.stack([low, high], axis=1).reshape(-1, held.shape[-1])
        return held

    def half(self, held, have, bit, other):
        before = 1
        for key in have[: have.index(bit)]:
            before *= key if isinstance(key, int) else 2
        parts = held.reshape(before, 2, -1, held.shape[-1])
        return self.pick(parts, bit, other, 1).reshape(-1, held.shape[-1])

    def add(self, kept, came, have, bit):
        def part(other):
            first, second = (self.half(a, have, bit, other) for a in (kept, came))
            return (first.astype(F32) + second.astype(F32)).astype(BF16)

        return part(True), part(False), [b for b in have if b != bit]


def body(
    patches, segments, masked, mask_embedding, norm1_gain, norm1_bias, qkv_weight, query_bias,
    value_bias, out_weight, out_bias, norm2_gain, norm2_bias, up_weight, up_bias, down_weight,
    down_bias, cotangent, *, seq, rows,
):
    links = Links(seq, rows)
    row_count, patch_count, width = patches.shape
    tokens = row_count * patch_count
    n = qkv_weight.shape[0]
    devices = seq * rows
    groups = up_weight.shape[1] // width
    mine = groups // 2
    half = width // 2
    halves = seq // 2
    depth = rows * n
    near, first, second, others = links.near, links.first, links.second, links.others
    near_place = links.value[near].reshape(1)

    packed = jnp.stack(
        [
            down_weight.reshape(2, mine, n, width),
            up_weight.reshape(n, devices, groups, n).transpose(2, 0, 1, 3).reshape(2, mine, n, width),
        ],
        axis=1,
    ).reshape(2, 2 * mine, n, width)
    packed_kept, packed_sent = links.pick(packed, near), links.pick(packed, near, True)
    packed_came = links.swap(packed_sent, near)
    low = links.value[near] == 0
    packed = jnp.stack([jnp.where(low, packed_kept, packed_came), jnp.where(low, packed_came, packed_kept)], axis=0)

    flags = (segments + MASKED * masked).astype(BF16).reshape(1, row_count, patch_count)
    sources = [after(patches.reshape(tokens, width), packed_came)]
    for bit in (first, near):
        flags = jnp.concatenate([flags, links.swap(flags, bit)], axis=0)
        sources += [links.swap(source, bit) for source in sources]
    early_ones, late_ones = [sources[1], flags], sources[2:]
    flags = flags.astype(F32).reshape(seq, row_count, 1, patch_count)
    small = [
        mask_embedding, norm1_gain, norm1_bias, query_bias, value_bias, out_bias, norm2_gain,
        norm2_bias, down_bias,
    ]
    columns = jnp.concatenate([jnp.stack(small), up_bias.reshape(groups, n)], axis=0).T
    columns = jnp.pad(columns, ((0, 0), (0, LANES - columns.shape[1])))
    fourths = [qkv_weight[:, i * half : (i + 1) * half] for i in range(6)]
    fourths += [out_weight[:, :half], out_weight[:, half:]]
    left = after(jnp.concatenate(fourths[::2], axis=1), packed)
    right = after(jnp.concatenate([*fourths[1::2], columns], axis=1), packed)
    left = links.gather(left, [*others, second, first], {2: early_ones, 3: late_ones}).reshape(halves, depth, -1)
    right = links.gather(right, [*others, first, second], {}).reshape(halves, depth, -1)
    left_other, right_other = links.swap(left, near), links.swap(right, near)

    same_core = [
        [(x * 2 + core) * rows + r for x in range(halves) for r in range(rows)] for core in range(2)
    ]
    rest = lax.all_gather(packed, EVERY, axis=2, tiled=True, axis_index_groups=same_core)

    rows_all, turned, queries, key_values, weights, vectors = project(
        near_place, sources, flags, left, left_other, right, right_other
    )
    queries = queries.reshape(row_count, patch_count, width)
    key_values = key_values.reshape(seq, row_count, patch_count, 2 * width)
    mixed, mixed_full, lse = attend(queries, key_values, flags)
    mixed = mixed.reshape(tokens, width)
    d_branch = cotangent.reshape(tokens, width)
    d_branch_other = links.swap(d_branch, near)
    normed_two, middle = open_branch(mixed, rows_all, flags, vectors, weights)
    places = jnp.stack([links.value[near], links.value[first]])
    added, d_normed, away, down_sent, down_kept, grad_up, grad_up_bias = branch(
        places, normed_two, links.swap(normed_two, near), d_branch, d_branch_other, vectors, rest
    )

    row_bits = [*others, second]
    have = [first, *row_bits]
    flat = lambda held: held.reshape(-1, held.shape[-1])
    down_sent, down_kept = flat(down_sent), flat(down_kept)
    up_order = [mine, first, near, *row_bits]
    grad_up = flat(grad_up)
    up_sent = links.half(grad_up, up_order, second, True)
    up_kept = links.half(grad_up, up_order, second, False)
    up_order = [mine, first, near, *others]
    away = links.swap(away, near)
    down_came, up_came = links.swap(down_sent, first), links.swap(up_sent, second)
    d_middle, d_mixed, out_sent, out_kept, sums = between(
        near_place, d_normed, away, middle, d_branch, vectors, mixed, weights, halves
    )
    out_came = links.swap(out_sent, near)
    d_mixed = d_mixed.reshape(row_count, patch_count, width)

    given = (queries, key_values, d_mixed, mixed_full, lse, flags)
    d_query, d_key, d_value, query_sums, value_sums = attend_back(*given, [down_sent, up_sent])

    down_sent, down_kept, down_order = links.add(
        after(down_kept, d_query), down_came, [mine, near, *row_bits], second
    )
    down_came = links.swap(down_sent, second)
    up_sent, up_kept, up_order = links.add(after(up_kept, down_sent), up_came, up_order, first)
    up_came = links.swap(up_sent, first)
    d_query = d_query.reshape(tokens, width)
    d_key = d_key.reshape(-1, width)
    d_value = d_value.reshape(-1, width)
    pair_sent, pair_kept, value_sent, value_kept = weight_grads(
        near_place, turned, d_key, d_value, d_query, halves, [down_sent, up_sent]
    )
    output = after(middle, pair_sent) + added + away[0].astype(F32) + vectors[DBIAS]
    output = output.astype(BF16)
    early_kept = jnp.concatenate([after(down_kept, output), up_kept], axis=0)
    early_came = jnp.concatenate([after(down_came, output), up_came], axis=0)
    early_order = [2 * mine, near, *others]
    early_sent, early_kept, early_order = links.add(early_kept, early_came, early_order, others[-1])
    early = [early_kept, links.swap(early_sent, others[-1]), early_order]
    pair_came = links.swap(flat(after(pair_sent, early_sent)), near)
    value_came = links.swap(flat(after(value_sent, early_sent)), near)
    pair_sent, pair_kept, pair_order = links.add(flat(pair_kept), pair_came, have, second)
    pair_came = links.swap(pair_sent, second)
    last_kept = jnp.concatenate([flat(value_kept), flat(out_kept)], axis=1)
    last_came = jnp.concatenate([value_came, flat(out_came)], axis=1)
    last_sent, last_kept, last_order = links.add(after(last_kept, pair_sent), last_came, have, first)
    last_came = links.swap(last_sent, first)
    far_share, near_share, own, small_sent, small_kept = first_norm(
        near_place, d_key, d_value, d_query, rows_all, flags, vectors, weights, d_middle, sums,
        grad_up_bias, query_sums, value_sums, halves, [early_sent, pair_sent, last_sent],
    )

    pair = [pair_kept, pair_came, pair_order]
    last = [last_kept, last_came, last_order]

    def go(item, bit, gone):
        gone, item[0], item[2] = links.add(after(item[0], gone), item[1], item[2], bit)
        item[1] = links.swap(gone, bit)
        return gone

    rest_bits = others[-2::-1]
    gone = own
    for bit in rest_bits:
        gone = go(early, bit, gone)
    pair_sent, pair[0], pair[2] = links.add(after(pair[0], gone), pair[1], pair[2], first)
    gone = pair_sent
    gone = go(last, second, gone)
    near_share = links.swap(after(near_share, gone), near)
    small = [flat(small_kept), links.swap(flat(after(small_sent, gone)), near), have]
    gone = go(small, first, gone)
    pair[1] = links.swap(after(pair_sent, gone), first)
    gone = (after(far_share, gone).astype(F32) + near_share[1:].astype(F32)).astype(BF16)
    far_share = links.swap(gone, first)
    gone = go(small, second, gone)
    last[0] = jnp.concatenate([after(pair[0], gone), last[0], small[0]], axis=1)
    last[1] = jnp.concatenate([pair[1], last[1], small[1]], axis=1)
    gone = go(last, others[-1], gone)
    low = links.value[near] == 0
    early_sum = after(early[0], gone).astype(F32) + early[1].astype(F32)
    early_sum = early_sum.reshape(2 * mine, 2, n, width)
    far_sum = links.pick(early_sum, near, True, 1).astype(BF16)
    far_sum = links.swap(far_sum, near).astype(F32)
    early_sum = links.pick(early_sum, near, False, 1)
    for bit in rest_bits:
        gone = go(last, bit, gone)
    early_sum = after(early_sum, gone)
    joined = jnp.stack(
        [jnp.where(low, early_sum, far_sum), jnp.where(low, far_sum, early_sum)], axis=0
    )
    down_sum = joined[:, :mine].reshape(-1, width)
    up_sum = joined[:, mine:].reshape(groups, n, devices, n)
    up_sum = up_sum.transpose(1, 2, 0, 3).reshape(n, -1)
    input_grad = after(own, up_sum) + near_share[0].astype(F32) + far_share[0].astype(F32)
    is_masked = masked.reshape(tokens, 1) == 1
    input_grad = jnp.where(is_masked, 0.0, input_grad)
    last = after(last[0], input_grad).astype(F32) + last[1].astype(F32)
    project_sum, out_sum = last[:, : 3 * width], last[:, 3 * width : 4 * width]
    tail = last[:, 4 * width :].T
    shape = (row_count, patch_count, width)
    return (
        output.reshape(shape), input_grad.reshape(shape), tail[EMBED], tail[GAIN1], tail[SHIFT1],
        project_sum, tail[QBIAS], tail[VBIAS], out_sum, tail[OBIAS], tail[GAIN2], tail[SHIFT2],
        up_sum, tail[UBIAS : UBIAS + groups].reshape(-1), down_sum, tail[DBIAS],
    )


def solution(mesh):
    one, two = P(EVERY), P(EVERY, None)
    rows, flags = P("rows", "seq", None), P("rows", "seq")
    seq, row_groups = mesh.shape["seq"], mesh.shape["rows"]

    def run(*arguments):
        return body(*arguments, seq=seq, rows=row_groups)

    return jax.shard_map(
        run,
        mesh=mesh,
        in_specs=(
            rows, flags, flags, one, one, one, two, one, one, two, one, one, one, two, one, two,
            one, rows,
        ),
        out_specs=(
            rows, rows, one, one, one, two, one, one, two, one, one, one, two, one, two, one,
        ),
        check_vma=False,
    )
```

```python
import jax
import jax.numpy as jnp
from jax import lax
from jax.experimental import pallas as pl
from jax.experimental.pallas import tpu as pltpu
from jax.sharding import PartitionSpec as P

HEAD_SIZE = 64
LANES = 128
CHUNK = 256
PAIRS = 6
MASKED = 16
EPSILON = 1e-06
FLOOR_SCORE = -1e30
HALF_ROOT = 0.7071067811865476
MIB = 2**20
EVERY = ("seq", "rows")
BF16 = jnp.bfloat16
F32 = jnp.float32
EMBED, GAIN1, SHIFT1, QBIAS, VBIAS, OBIAS, GAIN2, SHIFT2, DBIAS, UBIAS = range(10)
KINDS = 16


def dot(left, right, left_dim, right_dim):
    return lax.dot_general(
        left, right, (((left_dim,), (right_dim,)), ((), ())), preferred_element_type=F32
    )


def column(row):
    return jnp.broadcast_to(row, (8, row.shape[1])).T[:, :1]


def segment_of(flags):
    return flags - jnp.where(flags >= MASKED, float(MASKED), 0.0)


def norm_parts(values):
    mean = jnp.mean(values, axis=-1, keepdims=True)
    centered = values - mean
    rate = lax.rsqrt(jnp.mean(centered * centered, axis=-1, keepdims=True) + EPSILON)
    return centered * rate, rate


def norm_back(pulled, hat, rate):
    first = jnp.mean(pulled, axis=-1, keepdims=True)
    second = jnp.mean(pulled * hat, axis=-1, keepdims=True)
    return rate * (pulled - first - hat * second)


def parted(value, mine, depth):
    sent, kept = [], []
    for x in range(value.shape[0] // (2 * depth)):
        low = value[2 * x * depth : (2 * x + 1) * depth]
        high = value[(2 * x + 1) * depth : (2 * x + 2) * depth]
        sent.append(jnp.where(mine == 0, high, low))
        kept.append(jnp.where(mine == 0, low, high))
    return sent, kept


def whole(*shape):
    return pl.BlockSpec(shape, lambda *_: (0,) * len(shape))


ANYWHERE = pl.BlockSpec(memory_space=pl.ANY)


def shaped(dtype, *shape):
    return jax.ShapeDtypeStruct(shape, dtype)


def placed(dtype, *shape):
    return pltpu.HBM(shape, dtype)


def far(array):
    return pltpu.with_memory_space_constraint(array, pltpu.HBM)


def parameters(mib=32):
    return pltpu.CompilerParams(vmem_limit_bytes=mib * MIB)


def cost(flops, nbytes, transcendentals=0):
    return pl.CostEstimate(flops=flops, bytes_accessed=nbytes, transcendentals=transcendentals)


def split_heads(pair):
    lane = lax.broadcasted_iota(jnp.int32, pair.shape, 1)
    zero = jnp.zeros_like(pair)
    return jnp.concatenate(
        [jnp.where(lane < HEAD_SIZE, pair, zero), jnp.where(lane < HEAD_SIZE, zero, pair)], axis=0
    )


def join_heads(both, count):
    row = lax.broadcasted_iota(jnp.int32, (both.shape[0], count), 0)
    return jnp.where(row < HEAD_SIZE, both[:, :count], both[:, count:]).T


def set_bias(flags_ref, bias):
    blocks, size = flags_ref.shape[0], flags_ref.shape[3]
    asked = segment_of(flags_ref[0, 0])
    for j in range(blocks):
        keys = column(segment_of(flags_ref[j, 0]))
        bias[pl.ds(j * size, size), :] = jnp.where((keys == asked) & (keys > 0.0), 0.0, FLOOR_SCORE)


def attend_kernel(q_ref, k_ref, v_ref, flags_ref, mix_ref, full_ref, lse_ref, bias, held):
    count, blocks, size = q_ref.shape[1], k_ref.shape[0], k_ref.shape[2]

    @pl.when(pl.program_id(1) == 0)
    def _():
        set_bias(flags_ref, bias)

    live = segment_of(flags_ref[0, 0]) > 0.0
    live = jnp.concatenate([live, live], axis=1)
    for u in range(PAIRS):
        lanes = slice(u * LANES, (u + 1) * LANES)
        asked = split_heads(q_ref[0, :, lanes])
        top = None
        for j in range(blocks):
            rows = pl.ds(j * size, size)
            part = bias[rows, :]
            scores = dot(k_ref[j, 0, :, lanes], asked, 1, 1) + jnp.concatenate([part, part], axis=1)
            held[u % 2, rows, :] = scores
            high = jnp.max(scores, axis=0, keepdims=True)
            top = high if top is None else jnp.maximum(top, high)
        total, mixed = 0.0, 0.0
        for j in range(blocks):
            weights = jnp.exp(held[u % 2, pl.ds(j * size, size), :] - top)
            total = total + jnp.sum(weights, axis=0, keepdims=True)
            mixed = mixed + dot(v_ref[j, 0, :, lanes].T, weights.astype(BF16), 1, 0)
        result = join_heads(mixed * jnp.where(live, 1.0 / total, 0.0), count)
        mix_ref[0, :, lanes] = result.astype(BF16)
        full_ref[0, :, lanes] = result
        lse_ref[0, u] = jnp.where(live, top + jnp.log(total), 0.0)


def attend_back_kernel(
    q_ref, k_ref, v_ref, dm_ref, full_ref, lse_ref, flags_ref,
    dq_ref, dk_ref, dv_ref, qsum_ref, vsum_ref, bias,
):
    count, blocks, size = q_ref.shape[1], k_ref.shape[0], k_ref.shape[2]

    set_bias(flags_ref, bias)
    for u in range(q_ref.shape[2] // LANES):
        lanes = slice(u * LANES, (u + 1) * LANES)
        d_mixed = dm_ref[0, :, lanes]
        asked, pulled = split_heads(q_ref[0, :, lanes]), split_heads(d_mixed)
        product = (d_mixed.astype(F32) * full_ref[0, :, lanes]).T
        delta = jnp.concatenate(
            [
                jnp.sum(product[:HEAD_SIZE], axis=0, keepdims=True),
                jnp.sum(product[HEAD_SIZE:], axis=0, keepdims=True),
            ],
            axis=1,
        )
        lse = lse_ref[0, u]
        d_query, v_sum = 0.0, 0.0
        for j in range(blocks):
            keys = k_ref[j, 0, :, lanes]
            part = bias[pl.ds(j * size, size), :]
            scores = dot(keys, asked, 1, 1) + jnp.concatenate([part, part], axis=1)
            probs = jnp.exp(scores - lse)
            d_probs = dot(v_ref[j, 0, :, lanes], pulled, 1, 1)
            d_scores = (probs * (d_probs - delta)).astype(BF16)
            d_value = dot(probs.astype(BF16), pulled, 1, 0)
            dv_ref[j, 0, :, lanes] = d_value.astype(BF16)
            dk_ref[j, 0, :, lanes] = dot(d_scores, asked, 1, 0).astype(BF16)
            v_sum = v_sum + jnp.sum(d_value, axis=0, keepdims=True)
            d_query = d_query + dot(keys.T, d_scores, 1, 0)
        d_query = join_heads(d_query, count) * HEAD_SIZE**-0.5
        dq_ref[0, :, lanes] = d_query.astype(BF16)
        qsum_ref[0, u] = jnp.sum(d_query, axis=0, keepdims=True)
        vsum_ref[0, u] = v_sum


def attend(queries, key_values, flags):
    rows, count, width = queries.shape
    blocks, _, size, _ = key_values.shape
    pairs = width // LANES
    tile = pl.BlockSpec((1, count, PAIRS * LANES), lambda r, p: (r, 0, p))
    steps = pairs // PAIRS
    area = rows * count * blocks * size
    return pl.pallas_call(
        attend_kernel,
        grid=(rows, steps),
        in_specs=[
            tile,
            pl.BlockSpec((blocks, 1, size, PAIRS * LANES), lambda r, p: (0, r, 0, p)),
            pl.BlockSpec((blocks, 1, size, PAIRS * LANES), lambda r, p: (0, r, 0, steps + p)),
            pl.BlockSpec((blocks, 1, 1, size), lambda r, p: (0, r, 0, 0)),
        ],
        out_specs=[tile, tile, pl.BlockSpec((1, PAIRS, 1, 2 * count), lambda r, p: (r, p, 0, 0))],
        out_shape=[
            shaped(BF16, *queries.shape),
            placed(F32, *queries.shape),
            shaped(F32, rows, pairs, 1, 2 * count),
        ],
        scratch_shapes=[
            pltpu.VMEM((blocks * size, count), F32),
            pltpu.VMEM((2, blocks * size, 2 * count), F32),
        ],
        compiler_params=parameters(),
        cost_estimate=cost(16 * area * width, 8 * rows * blocks * size * width, area * 12),
        name="attend",
    )(far(queries), far(key_values), far(key_values), flags)


def attend_back(queries, key_values, d_mixed, mixed_full, lse, flags, after):
    rows, count, width = queries.shape
    blocks, _, size, _ = key_values.shape
    pairs = width // LANES
    tile = pl.BlockSpec((1, count, width), lambda r: (r, 0, 0))
    keys = pl.BlockSpec((blocks, 1, size, width), lambda r: (0, r, 0, 0))
    line = lambda w: pl.BlockSpec((1, pairs, 1, w), lambda r: (r, 0, 0, 0))
    area = rows * count * blocks * size
    grads = placed(BF16, blocks, rows, size, width)
    sums = shaped(F32, rows, pairs, 1, LANES)
    given = [queries, key_values, key_values, d_mixed, mixed_full, lse, flags]

    def kernel(*refs):
        attend_back_kernel(*refs[: len(given)], *refs[len(given) + len(after) :])

    return pl.pallas_call(
        kernel,
        grid=(rows,),
        in_specs=[
            tile, keys, pl.BlockSpec((blocks, 1, size, width), lambda r: (0, r, 0, 1)), tile, tile,
            line(2 * count), pl.BlockSpec((blocks, 1, 1, size), lambda r: (0, r, 0, 0)),
            *[ANYWHERE] * len(after),
        ],
        out_specs=[tile, keys, keys, line(LANES), line(LANES)],
        out_shape=[placed(BF16, *queries.shape), grads, grads, sums, sums],
        scratch_shapes=[pltpu.VMEM((blocks * size, count), F32)],
        compiler_params=parameters(40),
        cost_estimate=cost(32 * area * width, 16 * rows * blocks * size * width, area * 12),
        name="attend_back",
    )(*given, *after)


def project(near, sources, flags, left, left_other, right, right_other):
    own, width = sources[0].shape
    blocks, row_count, _, size = flags.shape
    total, steps = own * blocks, blocks
    halves, depth, part = left.shape
    half = width // 2

    def kernel(near_ref, *refs):
        first_ref, ahead_ref, lm_ref, lo_ref, rm_ref, ro_ref = refs[blocks : blocks + 6]
        rows_out, turned_ref, q_ref, kv_ref, w_out, vec_ref = refs[blocks + 6 : blocks + 12]
        rows, weights, normed, columns, sems, out_sems = refs[blocks + 12 :]
        step = pl.program_id(0)
        outward = [
            pltpu.make_async_copy(rows, rows_out, out_sems.at[0]),
            pltpu.make_async_copy(weights, w_out, out_sems.at[1]),
        ]

        def norm(at, slot, flags_ref):
            gain, shift = vec_ref[GAIN1 : GAIN1 + 1], vec_ref[SHIFT1 : SHIFT1 + 1]
            embed = vec_ref[EMBED : EMBED + 1]
            for r in range(row_count):
                masked = column(flags_ref[0, r]) >= MASKED
                here = rows[pl.ds(pl.multiple_of(at * own + r * size, size), size), :].astype(F32)
                hat, _ = norm_parts(jnp.where(masked, embed, here))
                normed[slot, r * size : (r + 1) * size, :] = (hat * gain + shift).astype(BF16)

        @pl.when(step == 0)
        def _():
            near_place = near_ref[0]
            later, first = [], []
            for which in range(2):
                mine = near_place if which == 0 else 1 - near_place
                low, high = (lm_ref, rm_ref) if which == 0 else (lo_ref, ro_ref)
                for x in range(halves):
                    at = pl.ds(pl.multiple_of(x * 2 * depth + mine * depth, depth), depth)
                    first.append((high.at[x, :, pl.ds(part, LANES)], columns.at[at, :]))
                    for side, source in enumerate((low, high)):
                        for kind in range(4):
                            later.append(
                                (
                                    source.at[x, :, pl.ds(kind * half, half)],
                                    weights.at[at, pl.ds(kind * width + side * half, half)],
                                )
                            )
            first.append((refs[0], rows.at[pl.ds(0, own), :]))
            later += [(refs[i], rows.at[pl.ds(i * own, own), :]) for i in range(1, blocks)]
            copies = [
                pltpu.make_async_copy(a, b, sems.at[i]) for i, (a, b) in enumerate([*first, *later])
            ]
            for copy in copies:
                copy.start()
            for copy in copies[: len(first)]:
                copy.wait()
            vec_ref[...] = columns[...].astype(F32).T[:KINDS]
            norm(0, 0, first_ref)
            for copy in copies[len(first) :]:
                copy.wait()
            for copy in outward:
                copy.start()

        slot = lax.rem(step, 2)
        here = normed[slot]
        kv_ref[:, :width] = dot(here, weights[:, width : 2 * width], 1, 0).astype(BF16)
        values = dot(here, weights[:, 2 * width : 3 * width], 1, 0)
        kv_ref[:, width:] = (values + vec_ref[VBIAS : VBIAS + 1]).astype(BF16)
        turned_ref[...] = here.T
        norm(jnp.minimum(step + 1, steps - 1), 1 - slot, ahead_ref)

        @pl.when(step == 0)
        def _():
            asked = dot(here, weights[:, :width], 1, 0) + vec_ref[QBIAS : QBIAS + 1]
            q_ref[...] = (asked * HEAD_SIZE**-0.5).astype(BF16)

        @pl.when(step == steps - 1)
        def _():
            for copy in outward:
                copy.wait()

    def ahead(t, _):
        return (jnp.minimum(t + 1, steps - 1), 0, 0, 0)

    return pl.pallas_call(
        kernel,
        grid_spec=pltpu.PrefetchScalarGridSpec(
            num_scalar_prefetch=1,
            grid=(steps,),
            in_specs=[
                *[ANYWHERE] * blocks,
                whole(1, row_count, 1, size),
                pl.BlockSpec((1, row_count, 1, size), ahead),
                *[ANYWHERE] * 4,
            ],
            out_specs=[
                ANYWHERE,
                pl.BlockSpec((width, own), lambda t, _: (0, t)),
                whole(own, width),
                pl.BlockSpec((own, 2 * width), lambda t, _: (t, 0)),
                ANYWHERE,
                whole(KINDS, width),
            ],
            scratch_shapes=[
                pltpu.VMEM((total, width), BF16),
                pltpu.VMEM((width, 4 * width), BF16),
                pltpu.VMEM((2, own, width), BF16),
                pltpu.VMEM((width, LANES), BF16),
                pltpu.SemaphoreType.DMA((18 * halves + blocks,)),
                pltpu.SemaphoreType.DMA((2,)),
            ],
        ),
        out_shape=[
            placed(BF16, total, width),
            placed(BF16, width, total),
            placed(BF16, own, width),
            placed(BF16, total, 2 * width),
            placed(BF16, width, 4 * width),
            shaped(F32, KINDS, width),
        ],
        compiler_params=parameters(40),
        cost_estimate=cost(5 * total * width * width, 8 * total * width + 16 * width * width, total),
        name="project",
    )(near, *sources, flags, flags, left, left_other, right, right_other)


def open_branch(mixed, rows_all, flags, vectors, weights):
    tokens, width = mixed.shape
    _, row_count, _, size = flags.shape

    def kernel(mixed_ref, rows_ref, flags_ref, vec_ref, w_ref, normed_ref, middle_ref):
        masked = column(flags_ref[0, 0]) >= MASKED
        embed, bias = vec_ref[EMBED : EMBED + 1], vec_ref[OBIAS : OBIAS + 1]
        gain, shift = vec_ref[GAIN2 : GAIN2 + 1], vec_ref[SHIFT2 : SHIFT2 + 1]
        added = dot(mixed_ref[...], w_ref[...], 1, 0)
        for c in range(0, size, CHUNK):
            cut = slice(c, c + CHUNK)
            values = jnp.where(masked[cut], embed, rows_ref[cut].astype(F32))
            middle = values + added[cut] + bias
            middle_ref[cut] = middle
            hat, _ = norm_parts(middle)
            normed_ref[cut] = (hat * gain + shift).astype(BF16)

    tile = pl.BlockSpec((size, width), lambda t: (t, 0))
    return pl.pallas_call(
        kernel,
        grid=(row_count,),
        in_specs=[
            tile, tile, pl.BlockSpec((1, 1, 1, size), lambda t: (0, t, 0, 0)), whole(KINDS, width),
            pl.BlockSpec((width, width), lambda t: (0, 3)),
        ],
        out_specs=[tile, tile],
        out_shape=[placed(BF16, tokens, width), placed(F32, tokens, width)],
        compiler_params=parameters(),
        cost_estimate=cost(2 * tokens * width * width, 10 * tokens * width),
        name="open_branch",
    )(mixed, rows_all, flags, vectors, weights)


def branch(places, normed, normed_other, pulled, pulled_other, vectors, rest):
    tokens, width = normed.shape
    groups = rest.shape[1] // 2
    cores, length = rest.shape[0], rest.shape[2]
    depth = length // 2
    both = 2 * tokens
    size = both

    def kernel(
        places_ref, n_ref, no_ref, c_ref, co_ref, vec_ref, down_ref, up_ref,
        total_ref, dn_ref, away_ref, sdown_ref, kdown_ref, gup_ref, gbias_ref,
        normed_all, turned, pulled_all, totals, d_normed, activated, d_hidden, up, down, staged, sems,
    ):
        step = pl.program_id(0)

        @pl.when(step == 0)
        def _():
            normed_all[:tokens] = n_ref[...]
            normed_all[tokens:] = no_ref[...]
            turned[:, :tokens] = n_ref[...].T
            turned[:, tokens:] = no_ref[...].T
            pulled_all[:tokens] = c_ref[...]
            pulled_all[tokens:] = co_ref[...]

        at = 0
        for x in range(2):
            for core in range(cores):
                up[at : at + depth] = up_ref[core, 0, x * depth : (x + 1) * depth]
                down[at : at + depth] = down_ref[core, 0, x * depth : (x + 1) * depth]
                at += depth
        bias = vec_ref[pl.ds(UBIAS + groups * places_ref[0] + step, 1), :]
        bias_grad = 0.0
        for c in range(0, both, size):
            cut = slice(c, c + size)
            hidden = dot(normed_all[cut], up[...], 1, 0) + bias
            d_active = dot(pulled_all[cut], down[...], 1, 1)
            phi = 0.5 * (1.0 + lax.erf(hidden * HALF_ROOT))
            slope = phi + hidden * (0.3989422804014327 * jnp.exp(-0.5 * hidden * hidden))
            activated[cut] = (hidden * phi).astype(BF16)
            grad = (d_active * slope).astype(BF16)
            d_hidden[cut] = grad
            bias_grad += jnp.sum(grad.astype(F32), axis=0, keepdims=True)
        gbias_ref[0] = bias_grad
        for c in range(0, both, size):
            cut = slice(c, c + size)
            more = dot(activated[cut], down[...], 1, 0)
            more_back = dot(d_hidden[cut], up[...], 1, 1)

            @pl.when(step == 0)
            def _(cut=cut, more=more, more_back=more_back):
                totals[cut] = more
                d_normed[cut] = more_back

            @pl.when(step > 0)
            def _(cut=cut, more=more, more_back=more_back):
                totals[cut] += more
                d_normed[cut] += more_back

        last = step == pl.num_programs(0) - 1
        outward = [
            pltpu.make_async_copy(totals.at[pl.ds(0, tokens)], total_ref, sems.at[0]),
            pltpu.make_async_copy(d_normed.at[pl.ds(0, tokens)], dn_ref, sems.at[1]),
            pltpu.make_async_copy(staged, away_ref, sems.at[2]),
        ]

        @pl.when(last)
        def _():
            staged[0] = totals[tokens:].astype(BF16)
            staged[1] = d_normed[tokens:].astype(BF16)
            for copy in outward:
                copy.start()

        gup_ref[0] = dot(turned[...], d_hidden[...], 1, 0).astype(BF16)
        grads = dot(activated[...], pulled_all[...], 0, 0).astype(BF16)
        (sent,), (kept,) = parted(grads, places_ref[1], length)
        for core in range(cores):
            sdown_ref[0, core] = sent[core * depth : (core + 1) * depth]
            kdown_ref[0, core] = kept[core * depth : (core + 1) * depth]

        @pl.when(last)
        def _():
            for copy in outward:
                copy.wait()

    weight = lambda f: pl.BlockSpec((cores, 1, length, width), lambda k, _: (0, f(k), 0, 0))
    piece = pl.BlockSpec((1, cores, depth, width), lambda k, _: (k, 0, 0, 0))
    square = pl.BlockSpec((1, width, width), lambda k, _: (k, 0, 0))
    patch = whole(tokens, width)
    return pl.pallas_call(
        kernel,
        grid_spec=pltpu.PrefetchScalarGridSpec(
            num_scalar_prefetch=1,
            grid=(groups,),
            in_specs=[
                patch, patch, patch, patch, whole(KINDS, width), weight(lambda k: k),
                weight(lambda k: groups + k),
            ],
            out_specs=[
                ANYWHERE, ANYWHERE, ANYWHERE, piece, piece, square,
                pl.BlockSpec((1, 1, width), lambda k, _: (k, 0, 0)),
            ],
            scratch_shapes=[
                pltpu.VMEM((both, width), BF16),
                pltpu.VMEM((width, both), BF16),
                pltpu.VMEM((both, width), BF16),
                pltpu.VMEM((both, width), F32),
                pltpu.VMEM((both, width), F32),
                pltpu.VMEM((both, width), BF16),
                pltpu.VMEM((both, width), BF16),
                pltpu.VMEM((width, width), BF16),
                pltpu.VMEM((width, width), BF16),
                pltpu.VMEM((2, tokens, width), BF16),
                pltpu.SemaphoreType.DMA((3,)),
            ],
        ),
        out_shape=[
            placed(F32, tokens, width),
            placed(F32, tokens, width),
            placed(BF16, 2, tokens, width),
            placed(BF16, groups, cores, depth, width),
            placed(BF16, groups, cores, depth, width),
            placed(BF16, groups, width, width),
            shaped(F32, groups, 1, width),
        ],
        compiler_params=parameters(52),
        cost_estimate=cost(
            12 * groups * both * width * width, 20 * width * width, 2 * both * width * groups
        ),
        name="branch",
    )(places, far(normed), normed_other, pulled, pulled_other, vectors, rest, rest)


def between(near, d_normed, d_normed_other, middle, pulled, vectors, mixed, weights, halves):
    tokens, width = mixed.shape
    depth = width // (2 * halves)
    size = tokens

    def kernel(
        near_ref, dn_ref, more_ref, middle_ref, cot_ref, vec_ref, mixed_ref, w_ref,
        dmiddle_ref, dmixed_ref, sent_ref, kept_ref, sums_ref, d_attn,
    ):
        gain = vec_ref[GAIN2 : GAIN2 + 1]
        sums = 0.0
        for c in range(0, size, CHUNK):
            cut = slice(c, c + CHUNK)
            d_out = dn_ref[cut] + more_ref[0, cut].astype(F32)
            cot = cot_ref[cut].astype(F32)
            hat, rate = norm_parts(middle_ref[cut])
            d_middle = cot + norm_back(d_out * gain, hat, rate)
            dmiddle_ref[cut] = d_middle
            low = d_middle.astype(BF16)
            d_attn[cut] = low
            parts = [low.astype(F32), d_out * hat, d_out, cot]
            sums += jnp.concatenate([jnp.sum(s, axis=0, keepdims=True) for s in parts], axis=0)
        sums = jnp.concatenate([sums, jnp.zeros_like(sums)], axis=0)
        dmixed_ref[...] = dot(d_attn[...], w_ref[...], 1, 1).astype(BF16)
        more = dot(mixed_ref[...], d_attn[...], 0, 0)

        sums_ref[...] = sums
        value = more.astype(BF16)
        for x, (sent, kept) in enumerate(zip(*parted(value, near_ref[0], depth), strict=True)):
            sent_ref[x] = sent
            kept_ref[x] = kept

    tile = pl.BlockSpec((size, width), lambda t, _: (t, 0))
    piece = whole(halves, depth, width)
    return pl.pallas_call(
        kernel,
        grid_spec=pltpu.PrefetchScalarGridSpec(
            num_scalar_prefetch=1,
            grid=(1,),
            in_specs=[
                tile, pl.BlockSpec((1, size, width), lambda t, _: (1, t, 0)), tile, tile,
                whole(KINDS, width), tile, pl.BlockSpec((width, width), lambda t, _: (0, 3)),
            ],
            out_specs=[tile, tile, piece, piece, whole(8, width)],
            scratch_shapes=[pltpu.VMEM((size, width), BF16)],
        ),
        out_shape=[
            placed(F32, tokens, width),
            shaped(BF16, tokens, width),
            placed(BF16, halves, depth, width),
            placed(BF16, halves, depth, width),
            shaped(F32, 8, width),
        ],
        compiler_params=parameters(),
        cost_estimate=cost(4 * tokens * width * width, 16 * tokens * width),
        name="between",
    )(near, d_normed, d_normed_other, middle, pulled, vectors, mixed, far(weights))


def weight_grads(near, turned, d_key, d_value, d_query, halves, after):
    width, total = turned.shape
    own = d_query.shape[0]
    depth = width // (2 * halves)

    def kernel(near_ref, turned_ref, dk_ref, dv_ref, dq_ref, *refs):
        sa_ref, ka_ref, sb_ref, kb_ref = refs[len(after) :]
        step = pl.program_id(0)

        def put(value, sent_ref, kept_ref, at):
            pieces = zip(*parted(value.astype(BF16), near_ref[0], depth), strict=True)
            for x, (sent, kept) in enumerate(pieces):
                sent_ref[x, :, at : at + width] = sent
                kept_ref[x, :, at : at + width] = kept

        @pl.when(step == 0)
        def _():
            put(dot(turned_ref[:, :own], dq_ref[...], 1, 0), sa_ref, ka_ref, 0)

        @pl.when(step == 1)
        def _():
            put(dot(turned_ref[...], dk_ref[...], 1, 0), sa_ref, ka_ref, width)

        @pl.when(step == 2)
        def _():
            put(dot(turned_ref[...], dv_ref[...], 1, 0), sb_ref, kb_ref, 0)

    pair, single = whole(halves, depth, 2 * width), whole(halves, depth, width)
    return pl.pallas_call(
        kernel,
        grid_spec=pltpu.PrefetchScalarGridSpec(
            num_scalar_prefetch=1,
            grid=(3,),
            in_specs=[
                whole(width, total), whole(total, width), whole(total, width), whole(own, width),
                *[ANYWHERE] * len(after),
            ],
            out_specs=[pair, pair, single, single],
        ),
        out_shape=[
            placed(BF16, halves, depth, 2 * width),
            placed(BF16, halves, depth, 2 * width),
            placed(BF16, halves, depth, width),
            placed(BF16, halves, depth, width),
        ],
        compiler_params=parameters(36),
        cost_estimate=cost(5 * total * width * width, 8 * total * width + 12 * width * width),
        name="weight_grads",
    )(near, turned, d_key, d_value, d_query, *after)


def first_norm(
    near, d_key, d_value, d_query, rows_all, flags, vectors, weights, d_middle, sums, gbias, qsum, vsum, halves, after,
):
    total, width = rows_all.shape
    blocks, row_count, _, size = flags.shape
    own = d_query.shape[0]
    depth = width // (2 * halves)
    groups = gbias.shape[0]

    def kernel(near_ref, *refs):
        (
            dk_ref, dv_ref, dq_ref, rows_ref, flags_ref, vec_ref, w_ref, dmiddle_ref, sums_ref,
            gbias_ref, qsum_ref, vsum_ref,
        ) = refs[:12]
        far_ref, near_share_ref, own_ref, sent_ref, kept_ref, totals = refs[12 + len(after) :]
        step = pl.program_id(0)

        def put_share(step, cut, value):
            @pl.when(step < blocks // 2)
            def _():
                far_ref[0, cut] = value

            @pl.when(step >= blocks // 2)
            def _():
                near_share_ref[0, cut] = value

        def one(mine):
            d_all = dot(dk_ref[...], w_ref[:, width : 2 * width], 1, 1)
            d_all += dot(dv_ref[...], w_ref[:, 2 * width :], 1, 1)
            if mine:
                d_all += dot(dq_ref[...], w_ref[:, :width], 1, 1)
            gain, embed = vec_ref[GAIN1 : GAIN1 + 1], vec_ref[EMBED : EMBED + 1]
            more = 0.0
            for r in range(row_count):
                cut = slice(r * size, (r + 1) * size)
                masked = column(flags_ref[0, r]) >= MASKED
                d_normed = d_all[cut]
                hat, rate = norm_parts(jnp.where(masked, embed, rows_ref[cut].astype(F32)))
                d_embedded = norm_back(d_normed * gain, hat, rate)
                if mine:
                    d_embedded = d_embedded + dmiddle_ref[cut]
                    own_ref[cut] = d_embedded
                else:
                    put_share(step, cut, d_embedded.astype(BF16))
                parts = [jnp.where(masked, d_embedded, 0.0), d_normed * hat, d_normed]
                more += jnp.concatenate([jnp.sum(s, axis=0, keepdims=True) for s in parts], axis=0)
            return more

        @pl.when(step == 0)
        def _():
            totals[:3] = one(True)

        @pl.when(step > 0)
        def _():
            totals[:3] += one(False)

        @pl.when(step == blocks - 1)
        def _():
            def line(ref):
                rows, pairs = ref.shape[0], ref.shape[1]
                return sum(
                    jnp.concatenate([ref[r, p] for p in range(pairs)], axis=1) for r in range(rows)
                )

            bias = jnp.concatenate([gbias_ref[k] for k in range(groups)], axis=0)
            none = jnp.zeros_like(bias)
            low = near_ref[0] == 0
            kinds = [
                totals[:3], line(qsum_ref), line(vsum_ref), sums_ref[:4],
                jnp.where(low, bias, none), jnp.where(low, none, bias),
            ]
            kinds.append(jnp.zeros((LANES - UBIAS - 2 * groups, width), F32))
            small = jnp.concatenate(kinds, axis=0).T.astype(BF16)
            for x, (sent, kept) in enumerate(zip(*parted(small, near_ref[0], depth), strict=True)):
                sent_ref[x] = sent
                kept_ref[x] = kept

    tile = pl.BlockSpec((own, width), lambda t, _: (t, 0))
    piece = whole(halves, depth, LANES)
    return pl.pallas_call(
        kernel,
        grid_spec=pltpu.PrefetchScalarGridSpec(
            num_scalar_prefetch=1,
            grid=(blocks,),
            in_specs=[
                tile, tile, whole(own, width), tile,
                pl.BlockSpec((1, row_count, 1, size), lambda t, _: (t, 0, 0, 0)),
                whole(KINDS, width), whole(width, 3 * width), whole(own, width),
                whole(*sums.shape), whole(*gbias.shape), whole(*qsum.shape), whole(*vsum.shape),
                *[ANYWHERE] * len(after),
            ],
            out_specs=[
                pl.BlockSpec((1, own, width), lambda t, _: (jnp.clip(t - 1, 0, blocks // 2 - 2), 0, 0)),
                pl.BlockSpec((1, own, width), lambda t, _: (jnp.maximum(t - blocks // 2, 0), 0, 0)),
                whole(own, width), piece, piece,
            ],
            scratch_shapes=[pltpu.VMEM((8, width), F32)],
        ),
        out_shape=[
            placed(BF16, blocks // 2 - 1, own, width),
            placed(BF16, blocks // 2, own, width),
            placed(F32, own, width),
            shaped(BF16, halves, depth, LANES),
            shaped(BF16, halves, depth, LANES),
        ],
        compiler_params=parameters(36),
        cost_estimate=cost(5 * total * width * width, 8 * total * width + 12 * width * width, total),
        name="first_norm",
    )(near, far(d_key), far(d_value), d_query, rows_all, flags, vectors, weights, d_middle, sums, gbias, qsum, vsum, *after)


def after(value, *others):
    return lax.optimization_barrier((value, *others))[0]


class Links:
    def __init__(self, seq, rows):
        self.sizes = {"seq": seq, "rows": rows}
        order = []
        for axis in EVERY:
            mask = self.sizes[axis] // 2
            while mask:
                order.append((axis, mask))
                mask //= 2
        self.order = order
        place = {axis: lax.axis_index(axis) for axis in EVERY}
        self.value = {(a, m): ((place[a] // m) % 2).astype(jnp.int32) for a, m in order}
        self.near = ("seq", 1)
        self.first = ("seq", 2)
        self.second = ("rows", 1)
        self.others = [b for b in order if b[0] == "rows" and b[1] > 1]

    def swap(self, array, bit):
        axis, mask = bit
        return lax.ppermute(array, axis, [(i, i ^ mask) for i in range(self.sizes[axis])])

    def pick(self, array, bit, other=False, axis=0):
        at = 1 - self.value[bit] if other else self.value[bit]
        return lax.dynamic_index_in_dim(array, at, axis, keepdims=False)

    def gather(self, shard, bits, wanted):
        held, have = shard, []
        for i, bit in enumerate(bits):
            if i in wanted:
                held = after(held, *wanted[i])
            have = sorted([*have, bit], key=self.order.index)
            parts = held.reshape(2 ** have.index(bit), -1, held.shape[-1])
            other = self.swap(held, bit).reshape(parts.shape)
            upper = self.value[bit] == 1
            low = jnp.where(upper, other, parts)
            high = jnp.where(upper, parts, other)
            held = jnp.stack([low, high], axis=1).reshape(-1, held.shape[-1])
        return held

    def half(self, held, have, bit, other):
        before = 1
        for key in have[: have.index(bit)]:
            before *= key if isinstance(key, int) else 2
        parts = held.reshape(before, 2, -1, held.shape[-1])
        return self.pick(parts, bit, other, 1).reshape(-1, held.shape[-1])

    def add(self, kept, came, have, bit):
        def part(other):
            first, second = (self.half(a, have, bit, other) for a in (kept, came))
            return (first.astype(F32) + second.astype(F32)).astype(BF16)

        return part(True), part(False), [b for b in have if b != bit]


def body(
    patches, segments, masked, mask_embedding, norm1_gain, norm1_bias, qkv_weight, query_bias,
    value_bias, out_weight, out_bias, norm2_gain, norm2_bias, up_weight, up_bias, down_weight,
    down_bias, cotangent, *, seq, rows,
):
    links = Links(seq, rows)
    row_count, patch_count, width = patches.shape
    tokens = row_count * patch_count
    n = qkv_weight.shape[0]
    devices = seq * rows
    groups = up_weight.shape[1] // width
    mine = groups // 2
    half = width // 2
    halves = seq // 2
    depth = rows * n
    near, first, second, others = links.near, links.first, links.second, links.others
    near_place = links.value[near].reshape(1)

    packed = jnp.stack(
        [
            down_weight.reshape(2, mine, n, width),
            up_weight.reshape(n, devices, groups, n).transpose(2, 0, 1, 3).reshape(2, mine, n, width),
        ],
        axis=1,
    ).reshape(2, 2 * mine, n, width)
    packed_kept, packed_sent = links.pick(packed, near), links.pick(packed, near, True)
    packed_came = links.swap(packed_sent, near)
    low = links.value[near] == 0
    packed = jnp.stack([jnp.where(low, packed_kept, packed_came), jnp.where(low, packed_came, packed_kept)], axis=0)

    flags = (segments + MASKED * masked).astype(BF16).reshape(1, row_count, patch_count)
    sources = [after(patches.reshape(tokens, width), packed_came)]
    for bit in (first, near):
        flags = jnp.concatenate([flags, links.swap(flags, bit)], axis=0)
        sources += [links.swap(source, bit) for source in sources]
    early_ones, late_ones = [sources[1], flags], sources[2:]
    flags = flags.astype(F32).reshape(seq, row_count, 1, patch_count)
    small = [
        mask_embedding, norm1_gain, norm1_bias, query_bias, value_bias, out_bias, norm2_gain,
        norm2_bias, down_bias,
    ]
    columns = jnp.concatenate([jnp.stack(small), up_bias.reshape(groups, n)], axis=0).T
    columns = jnp.pad(columns, ((0, 0), (0, LANES - columns.shape[1])))
    fourths = [qkv_weight[:, i * half : (i + 1) * half] for i in range(6)]
    fourths += [out_weight[:, :half], out_weight[:, half:]]
    left = after(jnp.concatenate(fourths[::2], axis=1), packed)
    right = after(jnp.concatenate([*fourths[1::2], columns], axis=1), packed)
    left = links.gather(left, [*others, second, first], {2: early_ones, 3: late_ones}).reshape(halves, depth, -1)
    right = links.gather(right, [*others, first, second], {}).reshape(halves, depth, -1)
    left_other, right_other = links.swap(left, near), links.swap(right, near)

    same_core = [
        [(x * 2 + core) * rows + r for x in range(halves) for r in range(rows)] for core in range(2)
    ]
    rest = lax.all_gather(packed, EVERY, axis=2, tiled=True, axis_index_groups=same_core)

    rows_all, turned, queries, key_values, weights, vectors = project(
        near_place, sources, flags, left, left_other, right, right_other
    )
    queries = queries.reshape(row_count, patch_count, width)
    key_values = key_values.reshape(seq, row_count, patch_count, 2 * width)
    mixed, mixed_full, lse = attend(queries, key_values, flags)
    mixed = mixed.reshape(tokens, width)
    d_branch = cotangent.reshape(tokens, width)
    d_branch_other = links.swap(d_branch, near)
    normed_two, middle = open_branch(mixed, rows_all, flags, vectors, weights)
    places = jnp.stack([links.value[near], links.value[first]])
    added, d_normed, away, down_sent, down_kept, grad_up, grad_up_bias = branch(
        places, normed_two, links.swap(normed_two, near), d_branch, d_branch_other, vectors, rest
    )

    row_bits = [*others, second]
    have = [first, *row_bits]
    flat = lambda held: held.reshape(-1, held.shape[-1])
    down_sent, down_kept = flat(down_sent), flat(down_kept)
    up_order = [mine, first, near, *row_bits]
    grad_up = flat(grad_up)
    up_sent = links.half(grad_up, up_order, second, True)
    up_kept = links.half(grad_up, up_order, second, False)
    up_order = [mine, first, near, *others]
    away = links.swap(away, near)
    down_came, up_came = links.swap(down_sent, first), links.swap(up_sent, second)
    d_middle, d_mixed, out_sent, out_kept, sums = between(
        near_place, d_normed, away, middle, d_branch, vectors, mixed, weights, halves
    )
    out_came = links.swap(out_sent, near)
    d_mixed = d_mixed.reshape(row_count, patch_count, width)

    given = (queries, key_values, d_mixed, mixed_full, lse, flags)
    d_query, d_key, d_value, query_sums, value_sums = attend_back(*given, [down_sent, up_sent])

    down_sent, down_kept, down_order = links.add(
        after(down_kept, d_query), down_came, [mine, near, *row_bits], second
    )
    down_came = links.swap(down_sent, second)
    up_sent, up_kept, up_order = links.add(after(up_kept, down_sent), up_came, up_order, first)
    up_came = links.swap(up_sent, first)
    d_query = d_query.reshape(tokens, width)
    d_key = d_key.reshape(-1, width)
    d_value = d_value.reshape(-1, width)
    pair_sent, pair_kept, value_sent, value_kept = weight_grads(
        near_place, turned, d_key, d_value, d_query, halves, [down_sent, up_sent]
    )
    output = after(middle, pair_sent) + added + away[0].astype(F32) + vectors[DBIAS]
    output = output.astype(BF16)
    early_kept = jnp.concatenate([after(down_kept, output), up_kept], axis=0)
    early_came = jnp.concatenate([after(down_came, output), up_came], axis=0)
    early_order = [2 * mine, near, *others]
    early_sent, early_kept, early_order = links.add(early_kept, early_came, early_order, others[-1])
    early = [early_kept, links.swap(early_sent, others[-1]), early_order]
    pair_came = links.swap(flat(after(pair_sent, early_sent)), near)
    value_came = links.swap(flat(after(value_sent, early_sent)), near)
    pair_sent, pair_kept, pair_order = links.add(flat(pair_kept), pair_came, have, second)
    pair_came = links.swap(pair_sent, second)
    last_kept = jnp.concatenate([flat(value_kept), flat(out_kept)], axis=1)
    last_came = jnp.concatenate([value_came, flat(out_came)], axis=1)
    last_sent, last_kept, last_order = links.add(after(last_kept, pair_sent), last_came, have, first)
    last_came = links.swap(last_sent, first)
    far_share, near_share, own, small_sent, small_kept = first_norm(
        near_place, d_key, d_value, d_query, rows_all, flags, vectors, weights, d_middle, sums,
        grad_up_bias, query_sums, value_sums, halves, [early_sent, pair_sent, last_sent],
    )

    pair = [pair_kept, pair_came, pair_order]
    last = [last_kept, last_came, last_order]

    def go(item, bit, gone):
        gone, item[0], item[2] = links.add(after(item[0], gone), item[1], item[2], bit)
        item[1] = links.swap(gone, bit)
        return gone

    rest_bits = others[-2::-1]
    gone = own
    for bit in rest_bits:
        gone = go(early, bit, gone)
    pair_sent, pair[0], pair[2] = links.add(after(pair[0], gone), pair[1], pair[2], first)
    gone = pair_sent
    gone = go(last, second, gone)
    near_share = links.swap(after(near_share, gone), near)
    small = [flat(small_kept), links.swap(flat(after(small_sent, gone)), near), have]
    gone = go(small, first, gone)
    pair[1] = links.swap(after(pair_sent, gone), first)
    gone = (after(far_share, gone).astype(F32) + near_share[1:].astype(F32)).astype(BF16)
    far_share = links.swap(gone, first)
    gone = go(small, second, gone)
    last[0] = jnp.concatenate([after(pair[0], gone), last[0], small[0]], axis=1)
    last[1] = jnp.concatenate([pair[1], last[1], small[1]], axis=1)
    gone = go(last, others[-1], gone)
    low = links.value[near] == 0
    early_sum = after(early[0], gone).astype(F32) + early[1].astype(F32)
    early_sum = early_sum.reshape(2 * mine, 2, n, width)
    far_sum = links.pick(early_sum, near, True, 1).astype(BF16)
    far_sum = links.swap(far_sum, near).astype(F32)
    early_sum = links.pick(early_sum, near, False, 1)
    for bit in rest_bits:
        gone = go(last, bit, gone)
    early_sum = after(early_sum, gone)
    joined = jnp.stack(
        [jnp.where(low, early_sum, far_sum), jnp.where(low, far_sum, early_sum)], axis=0
    )
    down_sum = joined[:, :mine].reshape(-1, width)
    up_sum = joined[:, mine:].reshape(groups, n, devices, n)
    up_sum = up_sum.transpose(1, 2, 0, 3).reshape(n, -1)
    input_grad = after(own, up_sum) + near_share[0].astype(F32) + far_share[0].astype(F32)
    is_masked = masked.reshape(tokens, 1) == 1
    input_grad = jnp.where(is_masked, 0.0, input_grad)
    last = after(last[0], input_grad).astype(F32) + last[1].astype(F32)
    project_sum, out_sum = last[:, : 3 * width], last[:, 3 * width : 4 * width]
    tail = last[:, 4 * width :].T
    shape = (row_count, patch_count, width)
    return (
        output.reshape(shape), input_grad.reshape(shape), tail[EMBED], tail[GAIN1], tail[SHIFT1],
        project_sum, tail[QBIAS], tail[VBIAS], out_sum, tail[OBIAS], tail[GAIN2], tail[SHIFT2],
        up_sum, tail[UBIAS : UBIAS + groups].reshape(-1), down_sum, tail[DBIAS],
    )


def solution(mesh):
    one, two = P(EVERY), P(EVERY, None)
    rows, flags = P("rows", "seq", None), P("rows", "seq")
    seq, row_groups = mesh.shape["seq"], mesh.shape["rows"]

    def run(*arguments):
        return body(*arguments, seq=seq, rows=row_groups)

    return jax.shard_map(
        run,
        mesh=mesh,
        in_specs=(
            rows, flags, flags, one, one, one, two, one, one, two, one, one, one, two, one, two,
            one, rows,
        ),
        out_specs=(
            rows, rows, one, one, one, two, one, one, two, one, one, one, two, one, two, one,
        ),
        check_vma=False,
    )
```
